128 devices in a mesh: group: 4 (over z_hi, core), tile: 32 (over x, y, z_lo).
Axes of the slice: x: 4, y: 4, z: 4 (z_hi: 2, z_lo: 2; z = z_hi * 2 + z_lo), core: 2. Of those that a mesh axis runs over, the one named last changes fastest.
Arguments:
- state: float32 [4, 32, 8, 384], P('group', 'tile'), may hold values from -6 to 6
- cotangent: float32 [4, 32, 8, 384], P('group', 'tile'), may hold values from -6 to 6
- neighbours: int32 [4, 32, 9, 384], P('group', 'tile'), may hold values from 0 to 649, as said below
- sea_cells: int32 [3, 32, 128], P(None, 'tile'), may hold values from 0 to 383, as said below
- atm_lift: bfloat16 [64, 10], replicated, may hold values from -2 to 2
- atm_conv: bfloat16 [2, 9, 64, 64], replicated, may hold values from -0.25 to 0.25
- atm_head: bfloat16 [12, 64], replicated, may hold values from -0.75 to 0.75
- ocn_lift: bfloat16 [64, 12], replicated, may hold values from -1.75 to 1.75
- ocn_conv: bfloat16 [2, 9, 64, 64], replicated, may hold values from -0.25 to 0.25
- ocn_head: bfloat16 [8, 64], replicated, may hold values from -0.75 to 0.75
Outputs:
- next_state: float32 [4, 32, 8, 384], P('group', 'tile')
- g_atm_lift: float32 [64, 10], replicated
- g_atm_conv: float32 [2, 9, 64, 64], replicated
- g_atm_head: float32 [12, 64], replicated
- g_ocn_lift: float32 [64, 12], replicated
- g_ocn_conv: float32 [2, 9, 64, 64], replicated
- g_ocn_head: float32 [8, 64], replicated
The draws below stay inside these ranges and needn't reach their ends.
Inputs may be any that keep to these rules, and one draw needn't show every extreme that they name: For a cycle g < 3, neighbours[g, t, :, c] indexes the block's grid extended by one cell on each side (row-major, 130 columns). Entries 0 to 4 are cell c itself and its north, south, west and east cells. Entries 5 and 6 are the north-west and north-east cells or the north cell; entries 7 and 8 are the south-west and south-east cells or the south cell. neighbours[3, t, :, c] indexes ocean cells of sector t: entry 0 is c itself, every entry within 128 positions of it. sea_cells[g, t] lists 128 distinct cells of block (g, t) in increasing order; ocean cell g*128+j of sector t lies under cell sea_cells[g, t, j].
All inputs are finite; a program needn't handle non-finite values.
Results may differ from the reference program's by a relative error of at most 0.022.
Values may be sent and summed in bfloat16 or wider, within the bound.
No kernel may reach another device: no remote copies, remote signals or barrier semaphores. Data moves between devices by JAX's collectives and lax.ppermute only.
A program may use at most 128 MiB of HBM per device.

```python
import math
import jax
import jax.numpy as jnp
from jax import lax

WIDTH = 64
FIELDS = 8
FLUX = 4
K = 9
STEPS = 8
LAT = 3
LON = 128
SEA_POINTS_UNDER = 128
MERIDIAN_WEDGES = 32
SLOTS = 4
CELLS_ALL = 49152


def draw_sea_cells(key, part):
    key = jax.random.fold_in(key, 11)
    block_total = (SLOTS - 1) * MERIDIAN_WEDGES
    keys = jax.random.split(key, block_total)
    orders = jax.vmap(lambda one_key: jax.random.permutation(one_key, LAT * LON))(keys)
    chosen = jnp.sort(orders[:, :SEA_POINTS_UNDER].astype(jnp.int32), axis=1)
    return chosen.reshape(SLOTS - 1, MERIDIAN_WEDGES, SEA_POINTS_UNDER)


def draw_neighbours(key, part):
    key = jax.random.fold_in(key, 23)
    atm_key = jax.random.fold_in(key, 1)
    ocean_key = jax.random.fold_in(key, 2)
    cell_total = LAT * LON
    span = LON + 2
    positions = jnp.arange(cell_total, dtype=jnp.int32)
    centre_row = positions // LON + 1
    centre_col = positions % LON + 1
    first_cell = positions == 0
    last_cell = positions == cell_total - 1
    shifts = jax.random.randint(atm_key, (SLOTS - 1, MERIDIAN_WEDGES, 4, cell_total), 0, 2, dtype=jnp.int32)
    shift_nw = jnp.where(first_cell, 0, shifts[:, :, 0])
    shift_ne = shifts[:, :, 1]
    shift_sw = shifts[:, :, 2]
    shift_se = jnp.where(last_cell, 0, shifts[:, :, 3])
    zeros_like = jnp.zeros((SLOTS - 1, MERIDIAN_WEDGES, cell_total), jnp.int32)
    entries = [zeros_like + centre_row * span + centre_col, zeros_like + (centre_row - 1) * span + centre_col, zeros_like + (centre_row + 1) * span + centre_col, zeros_like + centre_row * span + centre_col - 1, zeros_like + centre_row * span + centre_col + 1, (centre_row - 1) * span + centre_col - 1 + shift_nw, (centre_row - 1) * span + centre_col + 1 - shift_ne, (centre_row + 1) * span + centre_col - 1 + shift_sw, (centre_row + 1) * span + centre_col + 1 - shift_se]
    atm_table = jnp.stack(entries, axis=2)
    offsets = jax.random.randint(ocean_key, (MERIDIAN_WEDGES, 8, cell_total), -LON, LON + 1, dtype=jnp.int32)
    ocean_rest = jnp.clip(positions[None, None, :] + offsets, 0, cell_total - 1)
    ocean_self = jnp.broadcast_to(positions[None, None, :], (MERIDIAN_WEDGES, 1, cell_total))
    ocean_table = jnp.concatenate([ocean_self, ocean_rest], axis=1)
    return jnp.concatenate([atm_table, ocean_table[None]], axis=0).astype(jnp.int32)


def shard_levels(own_key, shape, shards, least, largest):
    loudness = 1.0
    for axis_at, blocks in shards:
        heights = jax.random.uniform(jax.random.fold_in(jax.random.fold_in(own_key, 6), axis_at), (blocks,), jnp.float32, least / len(shards), largest / len(shards))
        loudness = loudness * jnp.repeat(jnp.exp(heights), shape[axis_at] // blocks).reshape((-1,) + (1,) * (len(shape) - 1 - axis_at))
    return loudness


def noise(stream_key, shape, scale, reach, cuts=(), held_as=jnp.bfloat16):
    result = jax.random.normal(stream_key, shape, jnp.float32) * scale
    if len(cuts) > 0:
        result = shard_levels(stream_key, shape, cuts, -0.22, 0.18) * result
    return jnp.clip(result, min=-reach, max=reach).astype(held_as)


def setup_inputs(seed: int = 0) -> dict:
    seeds = jax.random.split(jax.random.key(seed), 11)
    return {
        "state": noise(seeds[0], (SLOTS, MERIDIAN_WEDGES, FIELDS, LAT * LON), 1.0, 6.0, ((0, 4), (1, 32)), jnp.float32),
        "cotangent": noise(seeds[1], (SLOTS, MERIDIAN_WEDGES, FIELDS, LAT * LON), 1.0, 6.0, ((0, 4), (1, 32)), jnp.float32),
        "neighbours": draw_neighbours(jax.random.fold_in(seeds[10], 71), 0),
        "sea_cells": draw_sea_cells(jax.random.fold_in(seeds[10], 71), 0),
        "atm_lift": noise(seeds[4], (WIDTH, FIELDS + 2), (FIELDS + 2) ** -0.5, 2.0),
        "atm_conv": noise(seeds[5], (2, K, WIDTH, WIDTH), (K * WIDTH) ** -0.5, 0.25),
        "atm_head": noise(seeds[6], (FIELDS + FLUX, WIDTH), WIDTH ** -0.5, 0.75),
        "ocn_lift": noise(seeds[7], (WIDTH, FIELDS + FLUX), (FIELDS + FLUX) ** -0.5, 1.75),
        "ocn_conv": noise(seeds[8], (2, K, WIDTH, WIDTH), (K * WIDTH) ** -0.5, 0.25),
        "ocn_head": noise(seeds[9], (FIELDS, WIDTH), WIDTH ** -0.5, 0.75),
    }


HIGHEST = lax.Precision.HIGHEST

def silu_slope(pre_value):
    gate_value = jax.nn.sigmoid(pre_value)
    return gate_value * (1.0 + pre_value * (1.0 - gate_value))

def flat_weight(weight):
    return jnp.transpose(weight, (1, 2, 0)).reshape(weight.shape[1], weight.shape[2] * weight.shape[0])

def conv_ahead(extended, neighbour, weight):
    picked = jnp.take(extended, neighbour, axis=1).reshape(-1, neighbour.shape[1])
    return jnp.dot(flat_weight(weight), picked, preferred_element_type=jnp.float32)

def conv_back(extended, neighbour, weight, slope_grad):
    picked = jnp.take(extended, neighbour, axis=1).reshape(-1, neighbour.shape[1])
    grad_flat = jnp.dot(slope_grad, picked.T, preferred_element_type=jnp.float32)
    spread = jnp.dot(flat_weight(weight).T, slope_grad, preferred_element_type=jnp.float32)
    spread = spread.reshape(extended.shape[0], neighbour.shape[0], neighbour.shape[1])
    grad_ext = jnp.zeros(extended.shape, jnp.float32).at[:, neighbour].add(spread)
    grad_weight = grad_flat.reshape(weight.shape[1], weight.shape[2], weight.shape[0]).transpose(2, 0, 1)
    return (grad_ext, grad_weight)

def grid_index():
    rollout_tally = SLOTS - 1
    row_ids = jnp.arange(rollout_tally, dtype=jnp.int32)[:, None] * LAT + jnp.arange(LAT + 2, dtype=jnp.int32)[None, :]
    col_ids = jnp.arange(MERIDIAN_WEDGES, dtype=jnp.int32)[:, None] * LON + jnp.arange(LON + 2, dtype=jnp.int32)[None, :]
    return (row_ids[:, None, :, None], col_ids[None, :, None, :])

def extend_all(blocks):
    rollout_tally, sectors, channels = (blocks.shape[0], blocks.shape[1], blocks.shape[2])
    global_grid = blocks.reshape(rollout_tally, sectors, channels, LAT, LON).transpose(2, 0, 3, 1, 4)
    global_grid = global_grid.reshape(channels, rollout_tally * LAT, sectors * LON)
    global_grid = jnp.pad(global_grid, ((0, 0), (1, 1), (0, 0)))
    global_grid = jnp.concatenate([global_grid[:, :, -1:], global_grid, global_grid[:, :, :1]], axis=2)
    row_ids, col_ids = grid_index()
    gathered = global_grid[:, row_ids, col_ids]
    return gathered.transpose(1, 2, 0, 3, 4).reshape(rollout_tally, sectors, channels, (LAT + 2) * (LON + 2))

def fold_all(grad_blocks):
    rollout_tally, sectors, channels = (grad_blocks.shape[0], grad_blocks.shape[1], grad_blocks.shape[2])
    pieces = grad_blocks.reshape(rollout_tally, sectors, channels, LAT + 2, LON + 2).transpose(2, 0, 1, 3, 4)
    row_ids, col_ids = grid_index()
    global_grid = jnp.zeros((channels, rollout_tally * LAT + 2, sectors * LON + 2), jnp.float32)
    global_grid = global_grid.at[:, row_ids, col_ids].add(pieces)
    inner_part = global_grid[:, 1:-1, 1:-1]
    inner_part = inner_part.at[:, :, -1].add(global_grid[:, 1:-1, 0])
    inner_part = inner_part.at[:, :, 0].add(global_grid[:, 1:-1, -1])
    inner_part = inner_part.reshape(channels, rollout_tally, LAT, sectors, LON).transpose(1, 3, 0, 2, 4)
    return inner_part.reshape(rollout_tally, sectors, channels, LAT * LON)

def reference(state, cotangent, neighbours, sea_cells, atm_lift, atm_conv, atm_head, ocn_lift, ocn_conv, ocn_head):
    rollout_tally = SLOTS - 1
    number_of_cells = LAT * LON
    tile_tally = rollout_tally * MERIDIAN_WEDGES
    grad_scale = 1.0 / math.sqrt(CELLS_ALL)
    atm_table = neighbours[:rollout_tally].reshape(tile_tally, K, number_of_cells)
    ocean_table = neighbours[rollout_tally]
    seawater_point_locator = sea_cells.reshape(tile_tally, SEA_POINTS_UNDER)
    seawater_condition = state[rollout_tally]
    seawater_skin_warmth = seawater_condition[:, 0, :].reshape(MERIDIAN_WEDGES, rollout_tally, SEA_POINTS_UNDER).transpose(1, 0, 2).reshape(tile_tally, SEA_POINTS_UNDER)

    def located_points(positions, amounts):
        return jnp.zeros((number_of_cells,), jnp.float32).at[positions].set(amounts)

    def place_flux(positions, amounts):
        return jnp.zeros((FLUX, number_of_cells), jnp.float32).at[:, positions].set(amounts)
    skin_warmth_map = jax.vmap(located_points)(seawater_point_locator, seawater_skin_warmth)
    water_indicator = jax.vmap(located_points)(seawater_point_locator, jnp.ones((tile_tally, SEA_POINTS_UNDER), jnp.float32))

    def atm_forward(present_variables):
        learner_feature_vector = jnp.concatenate([present_variables, skin_warmth_map[:, None, :], water_indicator[:, None, :]], axis=1).astype(jnp.bfloat16)
        lifted = lax.map(lambda packed: jnp.dot(atm_lift, packed, preferred_element_type=jnp.float32).astype(jnp.bfloat16), learner_feature_vector)
        lifted_ext = extend_all(lifted.reshape(rollout_tally, MERIDIAN_WEDGES, WIDTH, number_of_cells)).reshape(tile_tally, WIDTH, -1)
        pre_one = lax.map(lambda packed: conv_ahead(packed[0], packed[1], atm_conv[0]), (lifted_ext, atm_table))
        hidden_one = jax.nn.silu(pre_one).astype(jnp.bfloat16)
        hidden_ext = extend_all(hidden_one.reshape(rollout_tally, MERIDIAN_WEDGES, WIDTH, number_of_cells)).reshape(tile_tally, WIDTH, -1)
        pre_two = lax.map(lambda packed: conv_ahead(packed[0], packed[1], atm_conv[1]), (hidden_ext, atm_table))
        hidden_two = jax.nn.silu(pre_two).astype(jnp.bfloat16)
        update = lax.map(lambda packed: jnp.dot(atm_head, packed, preferred_element_type=jnp.float32), hidden_two)
        return (learner_feature_vector, lifted_ext, pre_one, hidden_ext, pre_two, hidden_two, update)
    history_fields = []
    present_variables = state[:rollout_tally].reshape(tile_tally, FIELDS, number_of_cells)
    flux_total = jnp.zeros((tile_tally, FLUX, number_of_cells), jnp.float32)
    for step_index in range(STEPS):
        history_fields.append(present_variables)
        update = atm_forward(present_variables)[6]
        present_variables = present_variables + update[:, :FIELDS]
        flux_total = flux_total + update[:, FIELDS:]
    flux_sea = (jnp.take_along_axis(flux_total, seawater_point_locator[:, None, :], axis=2) / STEPS).astype(jnp.bfloat16)
    ocean_flux = flux_sea.reshape(rollout_tally, MERIDIAN_WEDGES, FLUX, SEA_POINTS_UNDER).transpose(1, 2, 0, 3).reshape(MERIDIAN_WEDGES, FLUX, number_of_cells)

    def ocean_pass(packed):
        fields_here, forcing, neighbour, cotangent_here = packed
        learner_feature_vector = jnp.concatenate([fields_here.astype(jnp.bfloat16), forcing], axis=0)
        lifted = jnp.dot(ocn_lift, learner_feature_vector, preferred_element_type=jnp.float32).astype(jnp.bfloat16)
        pre_one = conv_ahead(lifted, neighbour, ocn_conv[0])
        hidden_one = jax.nn.silu(pre_one).astype(jnp.bfloat16)
        pre_two = conv_ahead(hidden_one, neighbour, ocn_conv[1])
        hidden_two = jax.nn.silu(pre_two).astype(jnp.bfloat16)
        advanced = fields_here + jnp.dot(ocn_head, hidden_two, preferred_element_type=jnp.float32)
        head_grad = (cotangent_here * grad_scale).astype(jnp.bfloat16)
        head_weight = jnp.dot(head_grad, hidden_two.T, preferred_element_type=jnp.float32)
        grad_hidden_two = jnp.dot(ocn_head.T, head_grad, preferred_element_type=jnp.float32)
        slope_two = (grad_hidden_two * silu_slope(pre_two)).astype(jnp.bfloat16)
        grad_hidden_one, conv_grad_two = conv_back(hidden_one, neighbour, ocn_conv[1], slope_two)
        slope_one = (grad_hidden_one * silu_slope(pre_one)).astype(jnp.bfloat16)
        grad_lifted, conv_grad_one = conv_back(lifted, neighbour, ocn_conv[0], slope_one)
        lift_weight = jnp.dot(grad_lifted, learner_feature_vector.astype(jnp.float32).T, precision=HIGHEST)
        grad_inputs = jnp.dot(ocn_lift.astype(jnp.float32).T, grad_lifted, precision=HIGHEST)
        return (advanced, lift_weight, jnp.stack([conv_grad_one, conv_grad_two]), head_weight, grad_inputs[FIELDS:])
    ocean_next, ocn_lift_terms, ocn_conv_terms, ocn_head_terms, forcing_grad = lax.map(ocean_pass, (seawater_condition, ocean_flux, ocean_table, cotangent[rollout_tally]))
    flux_sea_grad = forcing_grad.reshape(MERIDIAN_WEDGES, FLUX, rollout_tally, SEA_POINTS_UNDER).transpose(2, 0, 1, 3).reshape(tile_tally, FLUX, SEA_POINTS_UNDER) / STEPS
    flux_grad = jax.vmap(place_flux)(seawater_point_locator, flux_sea_grad)
    state_grad = cotangent[:rollout_tally].reshape(tile_tally, FIELDS, number_of_cells) * grad_scale
    lift_total = jnp.zeros((WIDTH, FIELDS + 2), jnp.float32)
    conv_total = jnp.zeros((2, K, WIDTH, WIDTH), jnp.float32)
    head_total = jnp.zeros((FIELDS + FLUX, WIDTH), jnp.float32)
    for step_index in reversed(range(STEPS)):
        learner_feature_vector, lifted_ext, pre_one, hidden_ext, pre_two, hidden_two, update = atm_forward(history_fields[step_index])
        head_grad = jnp.concatenate([state_grad, flux_grad], axis=1).astype(jnp.bfloat16)

        def second_back(packed):
            head_here, hidden_here, pre_here, ext_here, neighbour = packed
            head_weight = jnp.dot(head_here, hidden_here.T, preferred_element_type=jnp.float32)
            grad_hidden = jnp.dot(atm_head.T, head_here, preferred_element_type=jnp.float32)
            slope_two = (grad_hidden * silu_slope(pre_here)).astype(jnp.bfloat16)
            grad_ext, conv_grad = conv_back(ext_here, neighbour, atm_conv[1], slope_two)
            return (head_weight, grad_ext, conv_grad)
        head_weight, grad_ext_two, conv_grad_two = lax.map(second_back, (head_grad, hidden_two, pre_two, hidden_ext, atm_table))
        grad_hidden_one = fold_all(grad_ext_two.reshape(rollout_tally, MERIDIAN_WEDGES, WIDTH, -1)).reshape(tile_tally, WIDTH, number_of_cells)

        def first_back(packed):
            grad_here, pre_here, ext_here, neighbour = packed
            slope_one = (grad_here * silu_slope(pre_here)).astype(jnp.bfloat16)
            return conv_back(ext_here, neighbour, atm_conv[0], slope_one)
        grad_ext_one, conv_grad_one = lax.map(first_back, (grad_hidden_one, pre_one, lifted_ext, atm_table))
        grad_lifted = fold_all(grad_ext_one.reshape(rollout_tally, MERIDIAN_WEDGES, WIDTH, -1)).reshape(tile_tally, WIDTH, number_of_cells)

        def lift_back(packed):
            grad_here, inputs_here = packed
            lift_weight = jnp.dot(grad_here, inputs_here.astype(jnp.float32).T, precision=HIGHEST)
            grad_inputs = jnp.dot(atm_lift.astype(jnp.float32).T, grad_here, precision=HIGHEST)
            return (lift_weight, grad_inputs[:FIELDS])
        lift_weight, grad_fields = lax.map(lift_back, (grad_lifted, learner_feature_vector))
        state_grad = state_grad + grad_fields
        lift_total = lift_total + lift_weight.sum(0)
        conv_total = conv_total + jnp.stack([conv_grad_one.sum(0), conv_grad_two.sum(0)])
        head_total = head_total + head_weight.sum(0)
    next_state = jnp.concatenate([present_variables.reshape(rollout_tally, MERIDIAN_WEDGES, FIELDS, number_of_cells), ocean_next[None]], axis=0)
    return (next_state, lift_total, conv_total, head_total, ocn_lift_terms.sum(0), ocn_conv_terms.sum(0), ocn_head_terms.sum(0))
```

```python
import functools
import math

import jax
import jax.numpy as jnp
from jax import lax
from jax.experimental import pallas as pl
from jax.experimental.pallas import tpu as pltpu
from jax.sharding import PartitionSpec as P

STEPS = 8
LON = 128
ROWS = 9
CELLS = 384
WIN = ROWS * LON
K = 9
CH = 64
HALO = 32
WIRE = 512
BOTH = ("group", "tile")
BF = jnp.bfloat16
F32 = jnp.float32
INTERPRET = False
VMEM_LIMIT = 48 * 1024 * 1024

NN = (((1,), (0,)), ((), ()))
NT = (((1,), (1,)), ((), ()))


def dot(a, b, dims=NN):
    return lax.dot_general(a, b, dims, preferred_element_type=F32)


def call(body, outs, scratch=(), grid=(), in_specs=None, out_specs=None):
    vmem = pl.BlockSpec(memory_space=pltpu.VMEM)
    extra = {}
    if grid:
        extra = {"grid": grid, "in_specs": in_specs, "out_specs": out_specs}
    elif in_specs is not None:
        extra = {"in_specs": in_specs, "out_specs": [vmem] * len(outs)}
    return pl.pallas_call(
        body,
        out_shape=[jax.ShapeDtypeStruct(shape, dtype) for shape, dtype in outs],
        scratch_shapes=list(scratch),
        interpret=INTERPRET,
        compiler_params=pltpu.CompilerParams(vmem_limit_bytes=VMEM_LIMIT),
        **extra,
    )


def smem():
    return pl.BlockSpec(memory_space=pltpu.SMEM)


def vmem():
    return pl.BlockSpec(memory_space=pltpu.VMEM)


def lane_ids(shape):
    return lax.broadcasted_iota(jnp.int32, shape, len(shape) - 1)


def sigmoid(value):
    return 0.5 * jnp.tanh(0.5 * value) + 0.5


def seg(row):
    return slice(row * LON, (row + 1) * LON)


def pack_strip(read, half, shape):
    start = jnp.where(half == 0, 0, LON - HALO)
    quarter = lane_ids(shape) // HALO
    packed = []
    for block in range(3):
        total = jnp.zeros(shape, F32)
        for place in range(4):
            row = 4 * block + place
            if row < ROWS:
                moved = pltpu.roll(read(row), lax.rem(HALO * place - start + 2 * LON, LON), 1)
                total = jnp.where(quarter == place, moved, total)
        packed.append(total)
    return packed


def to_window(own, strip, row, half):
    place = row % 4
    lanes = lane_ids(own.shape)
    target = jnp.where(half == 0, LON - HALO, 0)
    moved = pltpu.roll(strip, lax.rem(target - HALO * place + 2 * LON, LON), 1)
    outside = (lanes >= target) & (lanes < target + HALO)
    merged = jnp.where(outside, moved, own)
    return pltpu.roll(merged, jnp.where(half == 0, HALO, LON - HALO), 1)


def pack_kernel(ids, state, cotangent, table, out):
    ocean = ids[0] == 3
    out[0:8, :] = state[...]
    out[8:16, :] = cotangent[...]
    entries = table[...]
    north = (entries[5:7] == entries[1:2]).astype(F32)
    south = (entries[7:9] == entries[2:3]).astype(F32)
    flags = jnp.concatenate(
        [jnp.zeros((2, CELLS), F32), north, south, jnp.zeros((3, CELLS), F32)], axis=0
    )
    chosen = jnp.where(ocean, entries.astype(F32), flags)
    out[16:32, :] = jnp.concatenate([chosen, jnp.zeros((7, CELLS), F32)], axis=0)


def one_hot_sea(sea_row):
    cells = lax.broadcasted_iota(jnp.int32, (CELLS, LON), 0)
    return jnp.where(cells == sea_row, 1.0, 0.0).astype(BF)


def sector_kernel(ids, gathered, sea, features, strip):
    half = ids[0] % 2
    for cycle in range(3):
        cols = slice(cycle * CELLS, (cycle + 1) * CELLS)
        features[0:16, cols] = gathered[cycle, 0:16, :]
        warm = gathered[3, 0:8, cycle * LON : (cycle + 1) * LON]
        row_ids = lax.broadcasted_iota(jnp.int32, (8, LON), 0)
        sources = jnp.where(row_ids == 0, warm[0:1], jnp.where(row_ids == 1, 1.0, 0.0))
        sources = jnp.concatenate([sources, jnp.zeros((8, LON), F32)], axis=0).astype(BF)
        placed = dot(sources, one_hot_sea(sea[cycle]), NT)[0:8]
        wide_ids = lax.broadcasted_iota(jnp.int32, (8, CELLS), 0)
        features[16:24, cols] = jnp.where(wide_ids < 2, placed, gathered[cycle, 16:24, :])
    packed = pack_strip(lambda row: features[:, seg(row)], half, (24, LON))
    for block in range(3):
        strip[:, seg(block)] = packed[block]


def build_columns(out, rows, flags):
    mid = [piece.astype(BF) for piece in rows]
    west = [pltpu.roll(piece, 1, 1).astype(BF) for piece in rows]
    east = [pltpu.roll(piece, LON - 1, 1).astype(BF) for piece in rows]
    zero = jnp.zeros((CH, LON), BF)
    for row in range(ROWS):
        up = row - 1
        down = row + 1
        north = mid[up] if up >= 0 else zero
        south = mid[down] if down < ROWS else zero
        taps = [mid[row], north, south, west[row], east[row]]
        corners = (
            (west[up], east[up]) if up >= 0 else (zero, zero),
            (west[down], east[down]) if down < ROWS else (zero, zero),
        )
        for corner in range(4):
            base = north if corner < 2 else south
            side = corners[corner // 2][corner % 2]
            flag = flags[corner : corner + 1, seg(row)] > 0.5
            taps.append(jnp.where(flag, base, side))
        for k in range(K):
            out[k * CH : (k + 1) * CH, seg(row)] = taps[k]


def spread_back(spread, flags):
    results = []
    for row in range(ROWS):
        def part(k, at):
            return spread[k * CH : (k + 1) * CH, seg(at)]

        mid = part(0, row)
        west = part(3, row)
        east = part(4, row)
        for at, straight, left, right in ((row + 1, 1, 5, 6), (row - 1, 2, 7, 8)):
            if 0 <= at < ROWS:
                corner = left - 5
                flag_left = flags[corner : corner + 1, seg(at)] > 0.5
                flag_right = flags[corner + 1 : corner + 2, seg(at)] > 0.5
                term_left = part(left, at)
                term_right = part(right, at)
                mid = mid + part(straight, at)
                mid = mid + jnp.where(flag_left, term_left, 0.0)
                mid = mid + jnp.where(flag_right, term_right, 0.0)
                west = west + jnp.where(flag_left, 0.0, term_left)
                east = east + jnp.where(flag_right, 0.0, term_right)
        results.append(mid + pltpu.roll(west, LON - 1, 1) + pltpu.roll(east, 1, 1))
    return results


def forward_kernel(
    ids, features, strip, lift, flat, head,
    inputs_out, source_out, gate_one, gate_two, last_out, window_out, final_out,
    window, total, columns,
):
    step = pl.program_id(0)
    half = ids[0] % 2
    first = ids[0] // 2 == 0

    @pl.when(step == 0)
    def _():
        for row in range(ROWS):
            block = row // 4
            window[:, seg(row)] = to_window(features[:, seg(row)], strip[:, seg(block)], row, half)
        total[0:8, :] = window[0:8, :]
        total[8:16, :] = jnp.zeros((8, WIN), F32)
        window_out[...] = window[8:24, :]

    flags = window[18:22, :]
    row_ids = lax.broadcasted_iota(jnp.int32, (8, WIN), 0)
    surface = window[16:24, :]
    surface = jnp.where(row_ids < 2, surface, 0.0)
    inputs = jnp.concatenate([total[0:8, :], surface], axis=0).astype(BF)
    inputs_out[0] = inputs
    lifted = dot(lift[...], inputs)
    build_columns(columns, [lifted[:, seg(row)] for row in range(ROWS)], flags)
    pre = dot(flat[0], columns[...])
    gate = sigmoid(pre)
    hidden = pre * gate
    gate_one[0] = (gate + hidden - hidden * gate).astype(BF)
    source_out[0] = jnp.where(first, lifted, hidden).astype(BF)
    build_columns(columns, [hidden[:, seg(row)] for row in range(ROWS)], flags)
    pre = dot(flat[1], columns[...])
    gate = sigmoid(pre)
    hidden = pre * gate
    gate_two[0] = (gate + hidden - hidden * gate).astype(BF)
    hidden = hidden.astype(BF)
    last_out[0] = hidden
    total[...] = total[...] + dot(head[...], hidden)

    @pl.when(step == STEPS - 1)
    def _():
        for row in range(ROWS):
            shift = jnp.where(half == 0, LON - HALO, HALO)
            final_out[:, seg(row)] = pltpu.roll(total[:, seg(row)], shift, 1)


def ocean_kernel(
    scale, ids, gathered, own, other, sea, lift, flat, head, lift_back, flat_back, head_back,
    next_state, flux_grad, strip, wire,
    hot, columns, scatter,
):
    group = ids[0]
    half = group % 2
    first = group // 2 == 0
    lanes = lane_ids((16, WIN))
    mine = ((lanes % LON) // (LON // 2)) == half
    merged = jnp.where(mine, own[...], other[...])
    flux = (merged[8:16, :] * (1.0 / STEPS)).astype(BF)
    flux = jnp.concatenate([flux, flux], axis=0)
    hot_sea = [one_hot_sea(sea[cycle]) for cycle in range(3)]
    forcing = [
        dot(flux[:, cycle * CELLS : (cycle + 1) * CELLS], hot_sea[cycle])[0:8] for cycle in range(3)
    ]
    forcing = jnp.concatenate(forcing, axis=1)
    fields = gathered[3, 0:8, :]
    inputs = jnp.concatenate([fields, forcing], axis=0).astype(BF)
    cell_ids = lax.broadcasted_iota(jnp.int32, (CELLS, CELLS), 0)
    for k in range(K):
        table = gathered[3, 16 + k : 17 + k, :].astype(jnp.int32)
        hot[k] = jnp.where(cell_ids == table, 1.0, 0.0).astype(BF)

    def gather(at, value):
        for k in range(K):
            columns[at, k * CH : (k + 1) * CH, :] = dot(value, hot[k]).astype(BF)

    def spread(index, slope):
        scatter[...] = dot(flat_back[index], slope).astype(BF)
        result = jnp.zeros((CH, CELLS), F32)
        for k in range(K):
            result = result + dot(scatter[k * CH : (k + 1) * CH, :], hot[k], NT)
        return result

    lifted = dot(lift[...], inputs).astype(BF)
    gather(0, lifted)
    pre = dot(flat[0], columns[0])
    gate = sigmoid(pre)
    hidden = pre * gate
    slope_of_one = gate + hidden - hidden * gate
    gather(1, hidden.astype(BF))
    pre = dot(flat[1], columns[1])
    gate = sigmoid(pre)
    hidden = pre * gate
    slope_of_two = gate + hidden - hidden * gate
    hidden = hidden.astype(BF)
    ocean_next = fields + dot(head[...], hidden)[0:8]
    block = jnp.where(group == 0, merged[0:8, 0:CELLS], ocean_next)
    block = jnp.where(group == 1, merged[0:8, CELLS : 2 * CELLS], block)
    next_state[...] = jnp.where(group == 2, merged[0:8, 2 * CELLS : 3 * CELLS], block)

    head_grad = gathered[3, 8:16, :] * scale
    head_grad = jnp.concatenate([head_grad, jnp.zeros((8, CELLS), F32)], axis=0).astype(BF)
    head_weight = dot(head_grad, hidden, NT)
    slope_two = (dot(head_back[...], head_grad) * slope_of_two).astype(BF)
    slope_one = (spread(1, slope_two) * slope_of_one).astype(BF)
    grad_lifted = spread(0, slope_one).astype(BF)
    lift_weight = dot(inputs, grad_lifted, NT)
    forcing_grad = dot(lift_back[...], grad_lifted)[8:16]
    forcing_grad = (forcing_grad * (1.0 / STEPS)).astype(BF)
    forcing_grad = jnp.concatenate([forcing_grad, forcing_grad], axis=0)
    for cycle in range(3):
        part = forcing_grad[:, cycle * LON : (cycle + 1) * LON]
        flux_grad[:, cycle * CELLS : (cycle + 1) * CELLS] = dot(part, hot_sea[cycle], NT)[0:8]
    packed = pack_strip(lambda row: flux_grad[:, seg(row)], half, (8, LON))
    for place in range(3):
        strip[:, seg(place)] = packed[place]

    slope = jnp.where(first, slope_one.astype(F32), slope_two.astype(F32)).astype(BF)
    chosen = jnp.where(first, 0, 1)
    weight = jnp.transpose(dot(columns[chosen], slope, NT))
    weight = jnp.where(half == 0, weight[0:32], weight[32:64])
    for j in range(4):
        wire[32 * j : 32 * j + 32, :] = weight[:, seg(j)]
    rest = weight[:, 512:576]
    wire[128:144, :] = jnp.concatenate([rest[0:16], rest[16:32]], axis=1)
    wire[144:160, :] = jnp.concatenate([lift_weight, head_weight], axis=1)


def backward_kernel(
    scale, ids, window, flux_own, flux_strip, ocean_wire, flat_back, head_back, lift_back,
    inputs, source, gate_one, gate_two, last,
    wire,
    state_grad, flux_grad, weight_total, small_total, columns, spread,
):
    step = pl.program_id(0)
    half = ids[0] % 2
    first = ids[0] // 2 == 0

    @pl.when(step == 0)
    def _():
        state_grad[...] = window[0:8, :] * scale
        for row in range(ROWS):
            place = row // 4
            flux_grad[:, seg(row)] = to_window(
                flux_own[:, seg(row)], flux_strip[:, seg(place)], row, half
            )
        weight_total[...] = jnp.zeros_like(weight_total)
        small_total[...] = jnp.zeros_like(small_total)

    flags = window[10:14, :]

    def owned(shape):
        lanes = lane_ids(shape) % LON
        return (lanes >= HALO) & (lanes < LON - HALO)

    def mask(value):
        return jnp.where(owned(value.shape), value, 0.0)

    head_grad = jnp.concatenate([state_grad[...], flux_grad[...]], axis=0)
    hidden = last[0]
    grad_two = dot(head_back[...], head_grad.astype(BF))
    slope_two = grad_two * gate_two[0].astype(F32)
    spread[...] = dot(flat_back[1], slope_two.astype(BF))
    grad_one = jnp.concatenate(spread_back(spread, flags), axis=1)
    slope_one = grad_one * gate_one[0].astype(F32)
    spread[...] = dot(flat_back[0], slope_one.astype(BF))
    grad_lifted = jnp.concatenate(spread_back(spread, flags), axis=1)
    lift_weight = dot(inputs[0], mask(grad_lifted).astype(BF), NT)
    head_weight = dot(mask(head_grad).astype(BF), hidden, NT)
    small_total[...] += jnp.concatenate([lift_weight, head_weight], axis=1)
    state_grad[...] += dot(lift_back[...], grad_lifted.astype(BF))[0:8]
    slope = mask(jnp.where(first, slope_one, slope_two)).astype(BF)
    values = source[0].astype(F32)
    build_columns(columns, [values[:, seg(row)] for row in range(ROWS)], flags)
    weight_total[...] += dot(columns[...], slope, NT)

    @pl.when(step == STEPS - 1)
    def _():
        weight = jnp.transpose(weight_total[...])
        for j in range(4):
            wire[64 * j : 64 * j + 64, :] = weight[:, seg(j)]
        rest = weight[:, 512:576]
        wire[256:288, :] = jnp.concatenate([rest[0:32], rest[32:64]], axis=1)
        wire[288:304, :] = small_total[...]
        wire[304:464, :] = ocean_wire[...]
        wire[464:512, :] = jnp.zeros((48, LON), F32)


def sum_kernel(sectors, rows, parts, out):
    sums = []
    for group in range(4):
        total = parts[group * sectors]
        for sector in range(1, sectors):
            total = total + parts[group * sectors + sector]
        sums.append(total)
    sums = jnp.concatenate(sums, axis=0).astype(BF)
    for place in range(4 * sectors):
        out[place] = sums


def final_kernel(
    rows, parts, g_lift, g_conv, g_head, o_lift, o_conv, o_head, sums
):
    places = WIRE // rows
    for place in range(places):
        piece = parts[place].astype(F32)
        for group in range(4):
            sums[group, place * rows : (place + 1) * rows, :] = piece[group * rows : (group + 1) * rows]
    for index in range(2):
        low, high = 2 * index, 2 * index + 1
        for j in range(4):
            pair = sums[low, 64 * j : 64 * j + 64, :] + sums[high, 64 * j : 64 * j + 64, :]
            g_conv[index, 2 * j] = pair[:, 0:64]
            g_conv[index, 2 * j + 1] = pair[:, 64:128]
            upper = sums[low, 304 + 32 * j : 336 + 32 * j, :]
            lower = sums[high, 304 + 32 * j : 336 + 32 * j, :]
            o_conv[index, 2 * j, 0:32] = upper[:, 0:64]
            o_conv[index, 2 * j, 32:64] = lower[:, 0:64]
            o_conv[index, 2 * j + 1, 0:32] = upper[:, 64:128]
            o_conv[index, 2 * j + 1, 32:64] = lower[:, 64:128]
        pair = sums[low, 256:288, :] + sums[high, 256:288, :]
        g_conv[index, 8, 0:32] = pair[:, 0:64]
        g_conv[index, 8, 32:64] = pair[:, 64:128]
        for side, at in ((low, 0), (high, 32)):
            piece = sums[side, 432:448, :]
            o_conv[index, 8, at : at + 16] = piece[:, 0:64]
            o_conv[index, 8, at + 16 : at + 32] = piece[:, 64:128]
    small = sums[0, 288:304, :] + sums[1, 288:304, :]
    g_lift[...] = jnp.transpose(small[:, 0:64])[:, 0:10]
    g_head[...] = small[0:12, 64:128]
    small = sums[0, 448:464, :]
    o_lift[...] = jnp.transpose(small[:, 0:64])[:, 0:12]
    o_head[...] = small[0:8, 64:128]


def padded(array, rows, columns):
    return jnp.pad(array, ((0, rows - array.shape[0]), (0, columns - array.shape[1])))


def shards(
    state,
    cotangent,
    neighbours,
    sea_cells,
    atm_lift,
    atm_conv,
    atm_head,
    ocn_lift,
    ocn_conv,
    ocn_head,
):
    sectors = lax.axis_size("tile")
    devices = 4 * sectors
    rows = WIRE // devices
    scale = 1.0 / math.sqrt(devices * CELLS)
    group = lax.axis_index("group")
    ids = group.astype(jnp.int32).reshape(1)

    partner = []
    beside = []
    for g in range(4):
        for t in range(sectors):
            partner.append((g * sectors + t, (g ^ 1) * sectors + t))
            other = (t + 1) % sectors if g % 2 else (t - 1) % sectors
            beside.append((g * sectors + t, (g ^ 1) * sectors + other))

    lift = padded(atm_lift, CH, 16)
    lift_back = padded(atm_lift.T, 16, CH)
    head = padded(atm_head, 16, CH)
    head_back = padded(atm_head.T, CH, 16)
    flat = jnp.transpose(atm_conv, (0, 2, 1, 3)).reshape(2, CH, K * CH)
    flat_back = jnp.transpose(atm_conv, (0, 1, 3, 2)).reshape(2, K * CH, CH)
    ocean_lift = padded(ocn_lift, CH, 16)
    ocean_lift_back = padded(ocn_lift.T, 16, CH)
    ocean_head = padded(ocn_head, 16, CH)
    ocean_head_back = padded(ocn_head.T, CH, 16)
    ocean_flat = jnp.transpose(ocn_conv, (0, 2, 1, 3)).reshape(2, CH, K * CH)
    ocean_flat_back = jnp.transpose(ocn_conv, (0, 1, 3, 2)).reshape(2, K * CH, CH)

    (packed,) = call(
        pack_kernel, [((32, CELLS), F32)], in_specs=[smem(), vmem(), vmem(), vmem()]
    )(ids, state[0, 0], cotangent[0, 0], neighbours[0, 0])
    gathered = lax.all_gather(packed, "group")
    features, strip = call(
        sector_kernel,
        [((24, WIN), F32), ((24, CELLS), F32)],
        in_specs=[smem(), vmem(), vmem()],
    )(ids, gathered, sea_cells)
    strip = lax.ppermute(strip, BOTH, beside)

    def whole(shape):
        return pl.BlockSpec(shape, lambda s: (0,) * len(shape))

    def at_step(shape):
        return pl.BlockSpec((1,) + shape, lambda s: (s, 0, 0))

    def at_step_back(shape):
        return pl.BlockSpec((1,) + shape, lambda s: (STEPS - 1 - s, 0, 0))

    wide = (CH, WIN)
    history = [(16, WIN), wide, wide, wide, wide]
    inputs, source, gate_one, gate_two, last, window, final = call(
        forward_kernel,
        [((STEPS,) + shape, BF) for shape in history] + [((16, WIN), F32), ((16, WIN), F32)],
        scratch=[
            pltpu.VMEM((24, WIN), F32),
            pltpu.VMEM((16, WIN), F32),
            pltpu.VMEM((K * CH, WIN), BF),
        ],
        grid=(STEPS,),
        in_specs=[
            smem(),
            whole((24, WIN)),
            whole((24, CELLS)),
            whole((CH, 16)),
            whole((2, CH, K * CH)),
            whole((16, CH)),
        ],
        out_specs=[at_step(shape) for shape in history] + [whole((16, WIN)), whole((16, WIN))],
    )(ids, features, strip, lift, flat, head)

    other_final = lax.ppermute(final, BOTH, partner)
    next_state, flux_grad, flux_strip, ocean_wire = call(
        functools.partial(ocean_kernel, scale),
        [((8, CELLS), F32), ((8, WIN), F32), ((8, CELLS), F32), ((160, LON), F32)],
        scratch=[
            pltpu.VMEM((K, CELLS, CELLS), BF),
            pltpu.VMEM((2, K * CH, CELLS), BF),
            pltpu.VMEM((K * CH, CELLS), BF),
        ],
        in_specs=[smem()] + [vmem()] * 10,
    )(
        ids, gathered, final, other_final, sea_cells, ocean_lift, ocean_flat, ocean_head,
        ocean_lift_back, ocean_flat_back, ocean_head_back,
    )
    flux_strip = lax.ppermute(flux_strip, BOTH, beside)

    (wire,) = call(
        functools.partial(backward_kernel, scale),
        [((WIRE, LON), F32)],
        scratch=[
            pltpu.VMEM((8, WIN), F32),
            pltpu.VMEM((8, WIN), F32),
            pltpu.VMEM((K * CH, CH), F32),
            pltpu.VMEM((16, LON), F32),
            pltpu.VMEM((K * CH, WIN), BF),
            pltpu.VMEM((K * CH, WIN), F32),
        ],
        grid=(STEPS,),
        in_specs=[
            smem(),
            whole((16, WIN)),
            whole((8, WIN)),
            whole((8, CELLS)),
            whole((160, LON)),
            whole((2, K * CH, CH)),
            whole((CH, 16)),
            whole((16, CH)),
        ]
        + [at_step_back(shape) for shape in history],
        out_specs=[whole((WIRE, LON))],
    )(
        ids, window, flux_grad, flux_strip, ocean_wire, flat_back, head_back, lift_back,
        inputs, source, gate_one, gate_two, last,
    )

    parts = lax.all_to_all(wire.reshape(devices, rows, LON), BOTH, 0, 0, tiled=True)
    (sums,) = call(
        functools.partial(sum_kernel, sectors, rows), [((devices, 4 * rows, LON), BF)]
    )(parts)
    sums = lax.all_to_all(sums, BOTH, 0, 0, tiled=True)
    totals = call(
        functools.partial(final_kernel, rows),
        [
            ((CH, 10), F32),
            ((2, K, CH, CH), F32),
            ((12, CH), F32),
            ((CH, 12), F32),
            ((2, K, CH, CH), F32),
            ((8, CH), F32),
        ],
        scratch=[pltpu.VMEM((4, WIRE, LON), F32)],
    )(sums)
    return (next_state[None, None], *totals)


def solution(mesh):
    return jax.shard_map(
        shards,
        mesh=mesh,
        in_specs=(
            P("group", "tile", None, None),
            P("group", "tile", None, None),
            P("group", "tile", None, None),
            P(None, "tile", None),
            P(),
            P(),
            P(),
            P(),
            P(),
            P(),
        ),
        out_specs=(P("group", "tile", None, None), P(), P(), P(), P(), P(), P()),
        check_vma=False,
    )
```

```python
import functools
import math

import jax
import jax.numpy as jnp
from jax import lax
from jax.experimental import pallas as pl
from jax.experimental.pallas import tpu as pltpu
from jax.sharding import PartitionSpec as P

STEPS = 8
LON = 128
ROWS = 9
CELLS = 384
WIN = ROWS * LON
K = 9
CH = 64
HALO = 32
WIRE = 512
BOTH = ("group", "tile")
BF = jnp.bfloat16
F32 = jnp.float32
INTERPRET = False
VMEM_LIMIT = 16 * 1024 * 1024
WHOLE_VMEM = 62 * 1024 * 1024
BACK = (0, 1, 2, 3, 4, 5, 6, 7, 8, 5, 6, 7, 8)

NN = (((1,), (0,)), ((), ()))
NT = (((1,), (1,)), ((), ()))


def dot(a, b, dims=NN):
    return lax.dot_general(a, b, dims, preferred_element_type=F32)


def call(body, outs, scratch=(), grid=(), in_specs=None, out_specs=None, limit=VMEM_LIMIT):
    vmem = pl.BlockSpec(memory_space=pltpu.VMEM)
    extra = {}
    if grid:
        extra = {"grid": grid, "in_specs": in_specs, "out_specs": out_specs}
    elif in_specs is not None:
        extra = {"in_specs": in_specs, "out_specs": [vmem] * len(outs)}
    return pl.pallas_call(
        body,
        out_shape=[jax.ShapeDtypeStruct(shape, dtype) for shape, dtype in outs],
        scratch_shapes=list(scratch),
        interpret=INTERPRET,
        compiler_params=pltpu.CompilerParams(vmem_limit_bytes=limit),
        **extra,
    )


def smem():
    return pl.BlockSpec(memory_space=pltpu.SMEM)


def hbm():
    return pl.BlockSpec(memory_space=pltpu.HBM)


def vmem():
    return pl.BlockSpec(memory_space=pltpu.VMEM)


def lane_ids(shape):
    return lax.broadcasted_iota(jnp.int32, shape, len(shape) - 1)


def sigmoid(value):
    return 0.5 * jnp.tanh(0.5 * value) + 0.5


def seg(row):
    return slice(row * LON, (row + 1) * LON)


def pack_strip(read, half, shape):
    start = jnp.where(half == 0, 0, LON - HALO)
    quarter = lane_ids(shape) // HALO
    packed = []
    for block in range(3):
        total = jnp.zeros(shape, F32)
        for place in range(4):
            row = 4 * block + place
            if row < ROWS:
                moved = pltpu.roll(read(row), lax.rem(HALO * place - start + 2 * LON, LON), 1)
                total = jnp.where(quarter == place, moved, total)
        packed.append(total)
    return packed


def to_window(own, strip, row, half):
    place = row % 4
    lanes = lane_ids(own.shape)
    target = jnp.where(half == 0, LON - HALO, 0)
    moved = pltpu.roll(strip, lax.rem(target - HALO * place + 2 * LON, LON), 1)
    outside = (lanes >= target) & (lanes < target + HALO)
    merged = jnp.where(outside, moved, own)
    return pltpu.roll(merged, jnp.where(half == 0, HALO, LON - HALO), 1)


def pack_kernel(state, cotangent, table, sea, out, held, held_sea, done):
    copies = [
        pltpu.make_async_copy(state, out.at[0:8], done.at[0]),
        pltpu.make_async_copy(cotangent, out.at[8:16], done.at[1]),
        pltpu.make_async_copy(table, held, done.at[2]),
        pltpu.make_async_copy(sea, held_sea, done.at[3]),
    ]
    for copy in copies:
        copy.start()
    for copy in copies:
        copy.wait()
    rows = [held[k] for k in range(K)]
    rows.append(jnp.concatenate([held_sea[cycle] for cycle in range(3)], axis=1))
    rows.append(jnp.zeros((6, CELLS), jnp.int32))
    out[16:32, :] = jnp.concatenate(rows, axis=0).astype(F32)


def turned(value):
    return jnp.transpose(value.astype(F32)).astype(BF)


def to_sixteen(value):
    zeros = jnp.zeros((16 - value.shape[0], value.shape[1]), F32)
    return jnp.concatenate([value.astype(F32), zeros], axis=0).astype(BF)


def weights_kernel(
    far_atm_lift, far_atm_conv, far_atm_head, far_ocn_lift, far_ocn_conv, far_ocn_head,
    lift, lift_back, head, head_back, flat, back,
    ocean_lift, ocean_lift_back, ocean_head, ocean_head_back, ocean_flat, ocean_back,
    atm_lift, atm_conv, atm_head, ocn_lift, ocn_conv, ocn_head, done,
):
    far = (far_atm_lift, far_atm_conv, far_atm_head, far_ocn_lift, far_ocn_conv, far_ocn_head)
    near = (atm_lift, atm_conv, atm_head, ocn_lift, ocn_conv, ocn_head)
    copies = [pltpu.make_async_copy(a, b, done.at[i]) for i, (a, b) in enumerate(zip(far, near))]
    for copy in copies:
        copy.start()
    for copy in copies:
        copy.wait()
    for raw, ahead, behind in ((atm_lift, lift, lift_back), (ocn_lift, ocean_lift, ocean_lift_back)):
        full = to_sixteen(raw[...])
        behind[...] = full
        ahead[...] = turned(full)
    for raw, ahead, behind in ((atm_head, head, head_back), (ocn_head, ocean_head, ocean_head_back)):
        full = to_sixteen(raw[...])
        ahead[...] = full
        behind[...] = turned(full)
    for index in range(2):
        blocks = [atm_conv[index, k] for k in range(K)]
        flat[index] = jnp.concatenate(blocks, axis=1)
        blocks = [turned(block) for block in blocks]
        back[index] = jnp.concatenate([blocks[k] for k in BACK], axis=1)
        blocks = [ocn_conv[index, k] for k in range(K)]
        ocean_flat[index] = jnp.concatenate(blocks, axis=1)
        for k in range(K):
            ocean_back[index, k * CH : (k + 1) * CH, :] = turned(blocks[k])


def one_hot_sea(row):
    cells = lax.broadcasted_iota(jnp.int32, (CELLS, LON), 0)
    return jnp.where(cells == row, 1.0, 0.0).astype(BF)


def sea_row(gathered, cycle):
    return gathered[3, 25:26, cycle * LON : (cycle + 1) * LON].astype(jnp.int32)


def sector_kernel(ids, gathered, features, strip):
    half = ids[0] % 2
    for cycle in range(3):
        cols = slice(cycle * CELLS, (cycle + 1) * CELLS)
        features[0:16, cols] = gathered[cycle, 0:16, :]
        warm = gathered[3, 0:8, cycle * LON : (cycle + 1) * LON]
        row_ids = lax.broadcasted_iota(jnp.int32, (8, LON), 0)
        sources = jnp.where(row_ids == 0, warm[0:1], jnp.where(row_ids == 1, 1.0, 0.0))
        sources = jnp.concatenate([sources, jnp.zeros((8, LON), F32)], axis=0).astype(BF)
        placed = dot(sources, one_hot_sea(sea_row(gathered, cycle)), NT)[0:8]
        features[16:24, cols] = placed
        table = gathered[cycle, 16:32, :]
        features[18:20, cols] = jnp.where(table[5:7] == table[1:2], 1.0, 0.0)
        features[20:22, cols] = jnp.where(table[7:9] == table[2:3], 1.0, 0.0)
    packed = pack_strip(lambda row: features[:, seg(row)], half, (24, LON))
    for block in range(3):
        strip[:, seg(block)] = packed[block]


def build_columns(out, rows, flags):
    mid = [piece.astype(BF) for piece in rows]
    west = [pltpu.roll(piece, 1, 1).astype(BF) for piece in rows]
    east = [pltpu.roll(piece, LON - 1, 1).astype(BF) for piece in rows]
    zero = jnp.zeros((CH, LON), BF)
    for row in range(ROWS):
        up = row - 1
        down = row + 1
        north = mid[up] if up >= 0 else zero
        south = mid[down] if down < ROWS else zero
        taps = [mid[row], north, south, west[row], east[row]]
        corners = (
            (west[up], east[up]) if up >= 0 else (zero, zero),
            (west[down], east[down]) if down < ROWS else (zero, zero),
        )
        for corner in range(4):
            base = north if corner < 2 else south
            side = corners[corner // 2][corner % 2]
            flag = flags[corner : corner + 1, seg(row)] > 0.5
            taps.append(jnp.where(flag, base, side))
        for k in range(K):
            out[k * CH : (k + 1) * CH, seg(row)] = taps[k]


def build_back(out, at, rows, flags):
    mid = [piece.astype(BF) for piece in rows]
    from_east = [pltpu.roll(piece, LON - 1, 1).astype(BF) for piece in rows]
    from_west = [pltpu.roll(piece, 1, 1).astype(BF) for piece in rows]
    zero = jnp.zeros((CH, LON), BF)

    def flag(index, row):
        return flags[index : index + 1, seg(row)] > 0.5

    for row in range(ROWS):
        below = row + 1 if row + 1 < ROWS else None
        above = row - 1 if row > 0 else None
        blocks = [mid[row], zero, zero, from_east[row], from_west[row]] + [zero] * 8
        for source, straight, first in ((below, 1, 0), (above, 2, 2)):
            if source is not None:
                blocks[straight] = mid[source]
                blocks[5 + first] = jnp.where(flag(4 + first, source), zero, from_east[source])
                blocks[6 + first] = jnp.where(flag(5 + first, source), zero, from_west[source])
                blocks[9 + first] = jnp.where(flag(first, source), mid[source], zero)
                blocks[10 + first] = jnp.where(flag(first + 1, source), mid[source], zero)
        for j in range(13):
            out[at, j * CH : (j + 1) * CH, seg(row)] = blocks[j]


def split_rows(value):
    return [value[:, seg(row)] for row in range(ROWS)]


def keep_owned(value):
    lanes = lane_ids(value.shape) % LON
    return jnp.where((lanes >= HALO) & (lanes < LON - HALO), value, 0.0)


def forward_kernel(
    ids, features, strip, lift, flat, head,
    inputs_out, source_out, gate_one, gate_two, last_out, window_out, final_out,
    window, total, columns,
):
    step = pl.program_id(0)
    half = ids[0] % 2
    first = ids[0] // 2 == 0

    @pl.when(step == 0)
    def _():
        for row in range(ROWS):
            block = row // 4
            window[:, seg(row)] = to_window(features[:, seg(row)], strip[:, seg(block)], row, half)
        total[0:8, :] = window[0:8, :]
        total[8:16, :] = jnp.zeros((8, WIN), F32)
        window_out[...] = window[8:24, :]

    flags = window[18:22, :]
    row_ids = lax.broadcasted_iota(jnp.int32, (8, WIN), 0)
    surface = window[16:24, :]
    surface = jnp.where(row_ids < 2, surface, 0.0)
    inputs = jnp.concatenate([total[0:8, :], surface], axis=0).astype(BF)
    inputs_out[0] = keep_owned(jnp.concatenate([total[0:8, :], surface], axis=0)).astype(BF)
    lifted = dot(lift[...], inputs)
    build_columns(columns, [lifted[:, seg(row)] for row in range(ROWS)], flags)
    pre = dot(flat[0], columns[...])
    gate = sigmoid(pre)
    hidden = pre * gate
    gate_one[0] = (gate + hidden - hidden * gate).astype(BF)
    source_out[0] = keep_owned(jnp.where(first, lifted, hidden)).astype(BF)
    build_columns(columns, [hidden[:, seg(row)] for row in range(ROWS)], flags)
    pre = dot(flat[1], columns[...])
    gate = sigmoid(pre)
    hidden = pre * gate
    gate_two[0] = (gate + hidden - hidden * gate).astype(BF)
    last_out[0] = keep_owned(hidden).astype(BF)
    hidden = hidden.astype(BF)
    total[...] = total[...] + dot(head[...], hidden)

    @pl.when(step == STEPS - 1)
    def _():
        for row in range(ROWS):
            shift = jnp.where(half == 0, LON - HALO, HALO)
            final_out[:, seg(row)] = pltpu.roll(total[:, seg(row)], shift, 1)


def ocean_kernel(
    scale, ids, gathered, own, other, lift, flat, head, lift_back, flat_back, head_back,
    next_state, flux_grad, strip, wire,
    hot, columns, scatter,
):
    group = ids[0]
    half = group % 2
    first = group // 2 == 0
    lanes = lane_ids((16, WIN))
    mine = ((lanes % LON) // (LON // 2)) == half
    merged = jnp.where(mine, own[...], other[...])
    flux = (merged[8:16, :] * (1.0 / STEPS)).astype(BF)
    flux = jnp.concatenate([flux, flux], axis=0)
    hot_sea = [one_hot_sea(sea_row(gathered, cycle)) for cycle in range(3)]
    forcing = [
        dot(flux[:, cycle * CELLS : (cycle + 1) * CELLS], hot_sea[cycle])[0:8] for cycle in range(3)
    ]
    forcing = jnp.concatenate(forcing, axis=1)
    fields = gathered[3, 0:8, :]
    inputs = jnp.concatenate([fields, forcing], axis=0).astype(BF)
    cell_ids = lax.broadcasted_iota(jnp.int32, (CELLS, CELLS), 0)
    for k in range(K):
        table = gathered[3, 16 + k : 17 + k, :].astype(jnp.int32)
        hot[k] = jnp.where(cell_ids == table, 1.0, 0.0).astype(BF)

    def gather(at, value):
        for k in range(K):
            columns[at, k * CH : (k + 1) * CH, :] = dot(value, hot[k]).astype(BF)

    def spread(index, slope):
        scatter[...] = dot(flat_back[index], slope).astype(BF)
        result = jnp.zeros((CH, CELLS), F32)
        for k in range(K):
            result = result + dot(scatter[k * CH : (k + 1) * CH, :], hot[k], NT)
        return result

    lifted = dot(lift[...], inputs).astype(BF)
    gather(0, lifted)
    pre = dot(flat[0], columns[0])
    gate = sigmoid(pre)
    hidden = pre * gate
    slope_of_one = gate + hidden - hidden * gate
    gather(1, hidden.astype(BF))
    pre = dot(flat[1], columns[1])
    gate = sigmoid(pre)
    hidden = pre * gate
    slope_of_two = gate + hidden - hidden * gate
    hidden = hidden.astype(BF)
    ocean_next = fields + dot(head[...], hidden)[0:8]
    block = jnp.where(group == 0, merged[0:8, 0:CELLS], ocean_next)
    block = jnp.where(group == 1, merged[0:8, CELLS : 2 * CELLS], block)
    next_state[...] = jnp.where(group == 2, merged[0:8, 2 * CELLS : 3 * CELLS], block)

    head_grad = gathered[3, 8:16, :] * scale
    head_grad = jnp.concatenate([head_grad, jnp.zeros((8, CELLS), F32)], axis=0).astype(BF)
    head_weight = dot(head_grad, hidden, NT)
    slope_two = (dot(head_back[...], head_grad) * slope_of_two).astype(BF)
    slope_one = (spread(1, slope_two) * slope_of_one).astype(BF)
    grad_lifted = spread(0, slope_one).astype(BF)
    lift_weight = dot(inputs, grad_lifted, NT)
    forcing_grad = dot(lift_back[...], grad_lifted)[8:16]
    forcing_grad = (forcing_grad * (1.0 / STEPS)).astype(BF)
    forcing_grad = jnp.concatenate([forcing_grad, forcing_grad], axis=0)
    for cycle in range(3):
        part = forcing_grad[:, cycle * LON : (cycle + 1) * LON]
        flux_grad[:, cycle * CELLS : (cycle + 1) * CELLS] = dot(part, hot_sea[cycle], NT)[0:8]
    packed = pack_strip(lambda row: flux_grad[:, seg(row)], half, (8, LON))
    for place in range(3):
        strip[:, seg(place)] = packed[place]

    slope = jnp.where(first, slope_one.astype(F32), slope_two.astype(F32)).astype(BF)
    chosen = jnp.where(first, 0, 1)
    weight = jnp.transpose(dot(columns[chosen], slope, NT))
    weight = jnp.where(half == 0, weight[0:32], weight[32:64])
    for j in range(4):
        wire[32 * j : 32 * j + 32, :] = weight[:, seg(j)]
    rest = weight[:, 512:576]
    wire[128:144, :] = jnp.concatenate([rest[0:16], rest[16:32]], axis=1)
    wire[144:160, :] = jnp.concatenate([lift_weight, head_weight], axis=1)


def backward_kernel(
    scale, ids, window, flux_own, flux_strip, ocean_wire, back, head_back, lift_back,
    inputs, source, gate_one, gate_two, last,
    wire,
    head_grad, flags, weight_total, small_total, taps,
):
    step = pl.program_id(0)
    half = ids[0] % 2
    chosen = 1 - jnp.where(ids[0] // 2 == 0, 1, 0)

    @pl.when(step == 0)
    def _():
        head_grad[0:8, :] = window[0:8, :] * scale
        for row in range(ROWS):
            place = row // 4
            head_grad[8:16, seg(row)] = to_window(
                flux_own[:, seg(row)], flux_strip[:, seg(place)], row, half
            )
            plain = window[10:14, seg(row)]
            east = pltpu.roll(window[8:16, seg(row)], LON - 1, 1)
            west = pltpu.roll(window[8:16, seg(row)], 1, 1)
            flags[0:4, seg(row)] = plain
            flags[4:5, seg(row)] = east[2:3]
            flags[5:6, seg(row)] = west[3:4]
            flags[6:7, seg(row)] = east[4:5]
            flags[7:8, seg(row)] = west[5:6]
        weight_total[...] = jnp.zeros_like(weight_total)
        small_total[...] = jnp.zeros_like(small_total)

    grad = head_grad[...].astype(BF)
    slope_two = dot(head_back[...], grad) * gate_two[0].astype(F32)
    build_back(taps, 1, split_rows(slope_two), flags)
    slope_one = dot(back[1], taps[1]) * gate_one[0].astype(F32)
    build_back(taps, 0, split_rows(slope_one), flags)
    grad_lifted = dot(back[0], taps[0]).astype(BF)
    head_grad[0:8, :] += dot(lift_back[...], grad_lifted)[0:8]
    lift_weight = dot(inputs[0], grad_lifted, NT)
    head_weight = dot(grad, last[0], NT)
    small_total[...] += jnp.concatenate([lift_weight, head_weight], axis=1)
    weight_total[...] += dot(taps[chosen], source[0], NT)

    @pl.when(step == STEPS - 1)
    def _():
        blocks = []
        for k in range(K):
            block = weight_total[k * CH : (k + 1) * CH, :]
            if k >= 5:
                block = block + weight_total[(k + 4) * CH : (k + 5) * CH, :]
            blocks.append(block)
        for j in range(4):
            wire[64 * j : 64 * j + 64, :] = jnp.concatenate(blocks[2 * j : 2 * j + 2], axis=1)
        wire[256:288, :] = jnp.concatenate([blocks[8][0:32], blocks[8][32:64]], axis=1)
        wire[288:304, :] = small_total[...]
        wire[304:464, :] = ocean_wire[...]
        wire[464:512, :] = jnp.zeros((48, LON), F32)


def sum_kernel(sectors, rows, parts, out):
    sums = []
    for group in range(4):
        total = parts[group * sectors]
        for sector in range(1, sectors):
            total = total + parts[group * sectors + sector]
        sums.append(total)
    sums = jnp.concatenate(sums, axis=0).astype(BF)
    for place in range(4 * sectors):
        out[place] = sums


def final_kernel(
    rows, parts, g_lift, g_conv, g_head, o_lift, o_conv, o_head, sums
):
    places = WIRE // rows
    for place in range(places):
        piece = parts[place].astype(F32)
        for group in range(4):
            sums[group, place * rows : (place + 1) * rows, :] = piece[group * rows : (group + 1) * rows]
    for index in range(2):
        low, high = 2 * index, 2 * index + 1
        for j in range(4):
            pair = sums[low, 64 * j : 64 * j + 64, :] + sums[high, 64 * j : 64 * j + 64, :]
            g_conv[index, 2 * j] = pair[:, 0:64]
            g_conv[index, 2 * j + 1] = pair[:, 64:128]
            upper = sums[low, 304 + 32 * j : 336 + 32 * j, :]
            lower = sums[high, 304 + 32 * j : 336 + 32 * j, :]
            o_conv[index, 2 * j, 0:32] = upper[:, 0:64]
            o_conv[index, 2 * j, 32:64] = lower[:, 0:64]
            o_conv[index, 2 * j + 1, 0:32] = upper[:, 64:128]
            o_conv[index, 2 * j + 1, 32:64] = lower[:, 64:128]
        pair = sums[low, 256:288, :] + sums[high, 256:288, :]
        g_conv[index, 8, 0:32] = pair[:, 0:64]
        g_conv[index, 8, 32:64] = pair[:, 64:128]
        for side, at in ((low, 0), (high, 32)):
            piece = sums[side, 432:448, :]
            o_conv[index, 8, at : at + 16] = piece[:, 0:64]
            o_conv[index, 8, at + 16 : at + 32] = piece[:, 64:128]
    small = sums[0, 288:304, :] + sums[1, 288:304, :]
    g_lift[...] = small[0:10, 0:64]
    g_head[...] = small[0:12, 64:128]
    small = sums[0, 448:464, :]
    o_lift[...] = small[0:12, 0:64]
    o_head[...] = small[0:8, 64:128]


def shards(
    state,
    cotangent,
    neighbours,
    sea_cells,
    atm_lift,
    atm_conv,
    atm_head,
    ocn_lift,
    ocn_conv,
    ocn_head,
):
    sectors = lax.axis_size("tile")
    devices = 4 * sectors
    rows = WIRE // devices
    scale = 1.0 / math.sqrt(devices * CELLS)
    group = lax.axis_index("group")
    ids = group.astype(jnp.int32).reshape(1)

    partner = []
    beside = []
    for g in range(4):
        for t in range(sectors):
            partner.append((g * sectors + t, (g ^ 1) * sectors + t))
            other = (t + 1) % sectors if g % 2 else (t - 1) % sectors
            beside.append((g * sectors + t, (g ^ 1) * sectors + other))

    (packed,) = call(
        pack_kernel,
        [((32, CELLS), F32)],
        scratch=[
            pltpu.VMEM((K, 1, CELLS), jnp.int32),
            pltpu.VMEM((3, 1, LON), jnp.int32),
            pltpu.SemaphoreType.DMA((4,)),
        ],
        in_specs=[hbm()] * 4,
        limit=WHOLE_VMEM,
    )(state[0, 0], cotangent[0, 0], neighbours.reshape(K, 1, CELLS), sea_cells)
    weights = call(
        weights_kernel,
        [
            ((CH, 16), BF),
            ((16, CH), BF),
            ((16, CH), BF),
            ((CH, 16), BF),
            ((2, CH, K * CH), BF),
            ((2, CH, 13 * CH), BF),
            ((CH, 16), BF),
            ((16, CH), BF),
            ((16, CH), BF),
            ((CH, 16), BF),
            ((2, CH, K * CH), BF),
            ((2, K * CH, CH), BF),
        ],
        scratch=[
            pltpu.VMEM(array.shape, BF)
            for array in (atm_lift.T, atm_conv, atm_head, ocn_lift.T, ocn_conv, ocn_head)
        ]
        + [pltpu.SemaphoreType.DMA((6,))],
        in_specs=[hbm()] * 6,
    )(atm_lift.T, atm_conv, atm_head, ocn_lift.T, ocn_conv, ocn_head)
    lift, lift_back, head, head_back, flat, back = weights[:6]
    ocean_lift, ocean_lift_back, ocean_head, ocean_head_back, ocean_flat, ocean_back = weights[6:]

    gathered = lax.all_gather(packed, "group")
    features, strip = call(
        sector_kernel,
        [((24, WIN), F32), ((24, CELLS), F32)],
        in_specs=[smem(), vmem()],
    )(ids, gathered)
    strip = lax.ppermute(strip, BOTH, beside)

    def whole(shape):
        return pl.BlockSpec(shape, lambda s: (0,) * len(shape))

    def at_step(shape):
        return pl.BlockSpec((1,) + shape, lambda s: (s, 0, 0))

    def at_step_back(shape):
        return pl.BlockSpec((1,) + shape, lambda s: (STEPS - 1 - s, 0, 0))

    wide = (CH, WIN)
    history = [(16, WIN), wide, wide, wide, wide]
    inputs, source, gate_one, gate_two, last, window, final = call(
        forward_kernel,
        [((STEPS,) + shape, BF) for shape in history] + [((16, WIN), F32), ((16, WIN), F32)],
        scratch=[
            pltpu.VMEM((24, WIN), F32),
            pltpu.VMEM((16, WIN), F32),
            pltpu.VMEM((K * CH, WIN), BF),
        ],
        grid=(STEPS,),
        in_specs=[
            smem(),
            whole((24, WIN)),
            whole((24, CELLS)),
            whole((CH, 16)),
            whole((2, CH, K * CH)),
            whole((16, CH)),
        ],
        out_specs=[at_step(shape) for shape in history] + [whole((16, WIN)), whole((16, WIN))],
    )(ids, features, strip, lift, flat, head)

    other_final = lax.ppermute(final, BOTH, partner)
    next_state, flux_grad, flux_strip, ocean_wire = call(
        functools.partial(ocean_kernel, scale),
        [((8, CELLS), F32), ((8, WIN), F32), ((8, CELLS), F32), ((160, LON), F32)],
        scratch=[
            pltpu.VMEM((K, CELLS, CELLS), BF),
            pltpu.VMEM((2, K * CH, CELLS), BF),
            pltpu.VMEM((K * CH, CELLS), BF),
        ],
        in_specs=[smem()] + [vmem()] * 9,
    )(
        ids, gathered, final, other_final, ocean_lift, ocean_flat, ocean_head,
        ocean_lift_back, ocean_back, ocean_head_back,
    )
    flux_strip = lax.ppermute(flux_strip, BOTH, beside)

    (wire,) = call(
        functools.partial(backward_kernel, scale),
        [((WIRE, LON), F32)],
        scratch=[
            pltpu.VMEM((16, WIN), F32),
            pltpu.VMEM((8, WIN), F32),
            pltpu.VMEM((13 * CH, CH), F32),
            pltpu.VMEM((16, LON), F32),
            pltpu.VMEM((2, 13 * CH, WIN), BF),
        ],
        grid=(STEPS,),
        in_specs=[
            smem(),
            whole((16, WIN)),
            whole((8, WIN)),
            whole((8, CELLS)),
            whole((160, LON)),
            whole((2, CH, 13 * CH)),
            whole((CH, 16)),
            whole((16, CH)),
        ]
        + [at_step_back(shape) for shape in history],
        out_specs=[whole((WIRE, LON))],
    )(
        ids, window, flux_grad, flux_strip, ocean_wire, back, head_back, lift_back,
        inputs, source, gate_one, gate_two, last,
    )

    parts = lax.all_to_all(wire.reshape(devices, rows, LON), BOTH, 0, 0, tiled=True)
    (sums,) = call(
        functools.partial(sum_kernel, sectors, rows), [((devices, 4 * rows, LON), BF)]
    )(parts)
    sums = lax.all_to_all(sums, BOTH, 0, 0, tiled=True)
    totals = call(
        functools.partial(final_kernel, rows),
        [
            ((10, CH), F32),
            ((2, K, CH, CH), F32),
            ((12, CH), F32),
            ((12, CH), F32),
            ((2, K, CH, CH), F32),
            ((8, CH), F32),
        ],
        scratch=[pltpu.VMEM((4, WIRE, LON), F32)],
    )(sums)
    g_lift, g_conv, g_head, o_lift, o_conv, o_head = totals
    return (next_state[None, None], g_lift.T, g_conv, g_head, o_lift.T, o_conv, o_head)


def solution(mesh):
    return jax.shard_map(
        shards,
        mesh=mesh,
        in_specs=(
            P("group", "tile", None, None),
            P("group", "tile", None, None),
            P("group", "tile", None, None),
            P(None, "tile", None),
            P(),
            P(),
            P(),
            P(),
            P(),
            P(),
        ),
        out_specs=(P("group", "tile", None, None), P(), P(), P(), P(), P(), P()),
        check_vma=False,
    )
```

```python
import functools
import math

import jax
import jax.numpy as jnp
from jax import lax
from jax.experimental import pallas as pl
from jax.experimental.pallas import tpu as pltpu
from jax.sharding import PartitionSpec as P

STEPS = 8
LON = 128
ROWS = 9
CELLS = 384
WIN = ROWS * LON
K = 9
CH = 64
HALO = 32
WIRE = 512
BOTH = ("group", "tile")
BF = jnp.bfloat16
F32 = jnp.float32
INTERPRET = False
VMEM_LIMIT = 16 * 1024 * 1024
WHOLE_VMEM = 62 * 1024 * 1024
BACK = (0, 1, 2, 5, 6, 7, 8, 3, 4, 5, 6, 7, 8)

NN = (((1,), (0,)), ((), ()))
NT = (((1,), (1,)), ((), ()))


def dot(a, b, dims=NN):
    return lax.dot_general(a, b, dims, preferred_element_type=F32)


def call(body, outs, scratch=(), grid=(), in_specs=None, out_specs=None, limit=VMEM_LIMIT):
    vmem = pl.BlockSpec(memory_space=pltpu.VMEM)
    extra = {}
    if grid:
        extra = {"grid": grid, "in_specs": in_specs, "out_specs": out_specs}
    elif in_specs is not None:
        extra = {"in_specs": in_specs, "out_specs": [vmem] * len(outs)}
    return pl.pallas_call(
        body,
        out_shape=[jax.ShapeDtypeStruct(shape, dtype) for shape, dtype in outs],
        scratch_shapes=list(scratch),
        interpret=INTERPRET,
        compiler_params=pltpu.CompilerParams(vmem_limit_bytes=limit),
        **extra,
    )


def smem():
    return pl.BlockSpec(memory_space=pltpu.SMEM)


def hbm():
    return pl.BlockSpec(memory_space=pltpu.HBM)


def vmem():
    return pl.BlockSpec(memory_space=pltpu.VMEM)


def lane_ids(shape):
    return lax.broadcasted_iota(jnp.int32, shape, len(shape) - 1)


def sigmoid(value):
    return 0.5 * jnp.tanh(0.5 * value) + 0.5


def seg(row):
    return slice(row * LON, (row + 1) * LON)


def pack_strip(read, half, shape):
    start = jnp.where(half == 0, 0, LON - HALO)
    quarter = lane_ids(shape) // HALO
    packed = []
    for block in range(3):
        total = jnp.zeros(shape, F32)
        for place in range(4):
            row = 4 * block + place
            if row < ROWS:
                moved = pltpu.roll(read(row), lax.rem(HALO * place - start + 2 * LON, LON), 1)
                total = jnp.where(quarter == place, moved, total)
        packed.append(total)
    return packed


def to_window(own, strip, row, half):
    place = row % 4
    lanes = lane_ids(own.shape)
    target = jnp.where(half == 0, LON - HALO, 0)
    moved = pltpu.roll(strip, lax.rem(target - HALO * place + 2 * LON, LON), 1)
    outside = (lanes >= target) & (lanes < target + HALO)
    merged = jnp.where(outside, moved, own)
    return pltpu.roll(merged, jnp.where(half == 0, HALO, LON - HALO), 1)


def pack_kernel(
    ids, state, cotangent, table, sea, atm_lift, atm_head, ocn_lift, ocn_head,
    out, held, held_sea, near_one, near_two, near_three, near_four, done,
):
    near = (near_one, near_two, near_three, near_four)
    pairs = [(state, out.at[0:8]), (cotangent, out.at[8:16]), (table, held), (sea, held_sea)]
    pairs += list(zip((atm_lift, atm_head, ocn_lift, ocn_head), near))
    copies = [pltpu.make_async_copy(a, b, done.at[i]) for i, (a, b) in enumerate(pairs)]
    for copy in copies:
        copy.start()
    for copy in copies:
        copy.wait()
    small = [to_sixteen(ref[...]) for ref in near]
    small = jnp.concatenate(small + [jnp.zeros((16, LON), F32)], axis=1)
    share = small[0:4]
    for place in range(1, 4):
        share = jnp.where(ids[0] == place, small[4 * place : 4 * place + 4], share)
    rows = [held[k].astype(F32) for k in range(K)]
    rows.append(jnp.concatenate([held_sea[cycle] for cycle in range(3)], axis=1).astype(F32))
    rows += [share, jnp.zeros((2, CELLS), F32)]
    out[16:32, :] = jnp.concatenate(rows, axis=0)


def turned(value):
    return jnp.transpose(value.astype(F32)).astype(BF)


def to_sixteen(value):
    zeros = jnp.zeros((16 - value.shape[0], value.shape[1]), F32)
    return jnp.concatenate([value.astype(F32), zeros], axis=0)


def weights_kernel(
    gathered, atm_conv, ocn_conv,
    lift, lift_back, head, head_back, flat, back,
    ocean_lift, ocean_lift_back, ocean_head, ocean_head_back, ocean_flat, ocean_back,
):
    small = jnp.concatenate([gathered[group, 26:30, :] for group in range(4)], axis=0)
    lift_back[...] = small[:, 0:64].astype(BF)
    lift[...] = turned(small[:, 0:64])
    head[...] = small[:, 64:128].astype(BF)
    head_back[...] = turned(small[:, 64:128])
    ocean_lift_back[...] = small[:, 128:192].astype(BF)
    ocean_lift[...] = turned(small[:, 128:192])
    ocean_head[...] = small[:, 192:256].astype(BF)
    ocean_head_back[...] = turned(small[:, 192:256])
    for index in range(2):
        blocks = [atm_conv[index, k] for k in range(K)]
        flat[index] = jnp.concatenate(blocks, axis=1)
        blocks = [turned(block) for block in blocks]
        back[index] = jnp.concatenate([blocks[k] for k in BACK], axis=1)
        blocks = [ocn_conv[index, k] for k in range(K)]
        ocean_flat[index] = jnp.concatenate(blocks, axis=1)
        for k in range(K):
            ocean_back[index, k * CH : (k + 1) * CH, :] = turned(blocks[k])


def hot_kernel(gathered, hot, hot_back):
    table = gathered[3, 16:32, :]
    columns = jnp.transpose(table).astype(jnp.int32)
    table = table.astype(jnp.int32)
    cell_rows = lax.broadcasted_iota(jnp.int32, (CELLS, CELLS), 0)
    cell_lanes = lane_ids((CELLS, CELLS))
    for k in range(K):
        hot[k] = jnp.where(cell_rows == table[k : k + 1], 1.0, 0.0).astype(BF)
        target = columns[:, k : k + 1]
        hot_back[k * CELLS : (k + 1) * CELLS, :] = jnp.where(cell_lanes == target, 1.0, 0.0).astype(BF)


def one_hot_sea(row):
    cells = lax.broadcasted_iota(jnp.int32, (CELLS, LON), 0)
    return jnp.where(cells == row, 1.0, 0.0).astype(BF)


def sea_row(gathered, cycle):
    return gathered[3, 25:26, cycle * LON : (cycle + 1) * LON].astype(jnp.int32)


def sector_kernel(ids, gathered, features, strip):
    half = ids[0] % 2
    for cycle in range(3):
        cols = slice(cycle * CELLS, (cycle + 1) * CELLS)
        features[0:16, cols] = gathered[cycle, 0:16, :]
        warm = gathered[3, 0:8, cycle * LON : (cycle + 1) * LON]
        row_ids = lax.broadcasted_iota(jnp.int32, (8, LON), 0)
        sources = jnp.where(row_ids == 0, warm[0:1], jnp.where(row_ids == 1, 1.0, 0.0))
        sources = jnp.concatenate([sources, jnp.zeros((8, LON), F32)], axis=0).astype(BF)
        placed = dot(sources, one_hot_sea(sea_row(gathered, cycle)), NT)[0:8]
        features[16:24, cols] = placed
        table = gathered[cycle, 16:32, :]
        features[18:20, cols] = jnp.where(table[5:7] == table[1:2], 1.0, 0.0)
        features[20:22, cols] = jnp.where(table[7:9] == table[2:3], 1.0, 0.0)
    packed = pack_strip(lambda row: features[:, seg(row)], half, (24, LON))
    for block in range(3):
        strip[:, seg(block)] = packed[block]


def pick(mask, chosen, other):
    shape = (CH // 16, 16, LON)
    result = jnp.where(mask[None], chosen.reshape(shape), other.reshape(shape))
    return result.reshape(CH, LON)


def shifted(piece):
    mid = piece.astype(BF)
    return mid, pltpu.roll(mid, 1, 1), pltpu.roll(mid, LON - 1, 1)


def build_columns(out, rows, flags):
    for row in range(ROWS):
        mid, west, east = shifted(rows[row])
        places = [(0, row, mid), (3, row, west), (4, row, east)]
        for cell, straight, first in ((row + 1, 1, 5), (row - 1, 2, 7)):
            if 0 <= cell < ROWS:
                places.append((straight, cell, mid))
                for side, k in ((west, first), (east, first + 1)):
                    flag = flags[k - 5, :, seg(cell)] > 0.5
                    places.append((k, cell, pick(flag, mid, side)))
        for k, cell, value in places:
            out[k * CH : (k + 1) * CH, seg(cell)] = value


def build_back(out, at, rows, flags):
    mid = [piece.astype(BF) for piece in rows]
    from_east = [pltpu.roll(piece, LON - 1, 1).astype(BF) for piece in rows]
    from_west = [pltpu.roll(piece, 1, 1).astype(BF) for piece in rows]
    zero = jnp.zeros((CH, LON), BF)

    def flag(index, row):
        return flags[index : index + 1, seg(row)] > 0.5

    for row in range(ROWS):
        blocks = {0: mid[row], 7: from_east[row], 8: from_west[row]}
        for source, straight, first in ((row + 1, 1, 0), (row - 1, 2, 2)):
            if 0 <= source < ROWS:
                blocks[straight] = mid[source]
                blocks[3 + first] = jnp.where(flag(first, source), mid[source], zero)
                blocks[4 + first] = jnp.where(flag(first + 1, source), mid[source], zero)
                blocks[9 + first] = jnp.where(flag(4 + first, source), zero, from_east[source])
                blocks[10 + first] = jnp.where(flag(5 + first, source), zero, from_west[source])
        for j, value in blocks.items():
            out[at, j * CH : (j + 1) * CH, seg(row)] = value


def split_rows(value):
    return [value[:, seg(row)] for row in range(ROWS)]


def keep_owned(value):
    lanes = lane_ids(value.shape) % LON
    return jnp.where((lanes >= HALO) & (lanes < LON - HALO), value, jnp.zeros_like(value))


def forward_kernel(
    ids, features, strip, lift, flat, head,
    inputs_out, source_out, gate_one, gate_two, last_out, window_out, final_out,
    window, total, columns, flags,
):
    step = pl.program_id(0)
    half = ids[0] % 2
    first = ids[0] // 2 == 0

    @pl.when(step == 0)
    def _():
        for row in range(ROWS):
            block = row // 4
            window[:, seg(row)] = to_window(features[:, seg(row)], strip[:, seg(block)], row, half)
        total[0:8, :] = window[0:8, :]
        total[8:16, :] = jnp.zeros((8, WIN), F32)
        window_out[...] = window[8:24, :]
        for j in range(4):
            flags[j] = jnp.broadcast_to(window[18 + j : 19 + j, :], (16, WIN)).astype(BF)
        columns[...] = jnp.zeros_like(columns)

    row_ids = lax.broadcasted_iota(jnp.int32, (8, WIN), 0)
    surface = window[16:24, :]
    surface = jnp.where(row_ids < 2, surface, 0.0)
    inputs = jnp.concatenate([total[0:8, :], surface], axis=0).astype(BF)
    inputs_out[0] = keep_owned(jnp.concatenate([total[0:8, :], surface], axis=0)).astype(BF)
    lifted = dot(lift[...], inputs)
    build_columns(columns, [lifted[:, seg(row)] for row in range(ROWS)], flags)
    pre = dot(flat[0], columns[...])
    gate = sigmoid(pre)
    hidden = pre * gate
    gate_one[0] = (gate + hidden - hidden * gate).astype(BF)
    source_out[0] = jnp.where(first, lifted, hidden).astype(BF)
    build_columns(columns, [hidden[:, seg(row)] for row in range(ROWS)], flags)
    pre = dot(flat[1], columns[...])
    gate = sigmoid(pre)
    hidden = pre * gate
    gate_two[0] = (gate + hidden - hidden * gate).astype(BF)
    last_out[0] = keep_owned(hidden).astype(BF)
    hidden = hidden.astype(BF)
    total[...] = total[...] + dot(head[...], hidden)

    @pl.when(step == STEPS - 1)
    def _():
        for row in range(ROWS):
            shift = jnp.where(half == 0, LON - HALO, HALO)
            final_out[:, seg(row)] = pltpu.roll(total[:, seg(row)], shift, 1)


def ocean_kernel(
    scale, ids, gathered, own, other, hot, hot_back,
    lift, flat, head, lift_back, flat_back, head_back,
    next_state, flux_grad, strip, columns, slopes, sixteen, wide,
    scatter,
):
    group = ids[0]
    half = group % 2
    lanes = lane_ids((16, WIN))
    mine = ((lanes % LON) // (LON // 2)) == half
    merged = jnp.where(mine, own[...], other[...])
    flux = (merged[8:16, :] * (1.0 / STEPS)).astype(BF)
    flux = jnp.concatenate([flux, flux], axis=0)
    hot_sea = [one_hot_sea(sea_row(gathered, cycle)) for cycle in range(3)]
    forcing = [
        dot(flux[:, cycle * CELLS : (cycle + 1) * CELLS], hot_sea[cycle])[0:8] for cycle in range(3)
    ]
    forcing = jnp.concatenate(forcing, axis=1)
    fields = gathered[3, 0:8, :]
    inputs = jnp.concatenate([fields, forcing], axis=0).astype(BF)

    def gather(at, value):
        for k in range(K):
            columns[at, k * CH : (k + 1) * CH, :] = dot(value, hot[k]).astype(BF)

    def spread(index, slope):
        parts = dot(flat_back[index], slope).astype(BF)
        for k in range(K):
            scatter[:, k * CELLS : (k + 1) * CELLS] = parts[k * CH : (k + 1) * CH]
        return dot(scatter[...], hot_back[...])

    lifted = dot(lift[...], inputs).astype(BF)
    gather(0, lifted)
    pre = dot(flat[0], columns[0])
    gate = sigmoid(pre)
    hidden = pre * gate
    slope_of_one = gate + hidden - hidden * gate
    gather(1, hidden.astype(BF))
    pre = dot(flat[1], columns[1])
    gate = sigmoid(pre)
    hidden = pre * gate
    slope_of_two = gate + hidden - hidden * gate
    hidden = hidden.astype(BF)
    ocean_next = fields + dot(head[...], hidden)[0:8]
    block = jnp.where(group == 0, merged[0:8, 0:CELLS], ocean_next)
    block = jnp.where(group == 1, merged[0:8, CELLS : 2 * CELLS], block)
    next_state[...] = jnp.where(group == 2, merged[0:8, 2 * CELLS : 3 * CELLS], block)

    head_grad = gathered[3, 8:16, :] * scale
    head_grad = jnp.concatenate([head_grad, jnp.zeros((8, CELLS), F32)], axis=0).astype(BF)
    slope_two = (dot(head_back[...], head_grad) * slope_of_two).astype(BF)
    slope_one = (spread(1, slope_two) * slope_of_one).astype(BF)
    grad_lifted = spread(0, slope_one).astype(BF)
    forcing_grad = dot(lift_back[...], grad_lifted)[8:16]
    forcing_grad = (forcing_grad * (1.0 / STEPS)).astype(BF)
    forcing_grad = jnp.concatenate([forcing_grad, forcing_grad], axis=0)
    for cycle in range(3):
        part = forcing_grad[:, cycle * LON : (cycle + 1) * LON]
        flux_grad[:, cycle * CELLS : (cycle + 1) * CELLS] = dot(part, hot_sea[cycle], NT)[0:8]
    packed = pack_strip(lambda row: flux_grad[:, seg(row)], half, (8, LON))
    for place in range(3):
        strip[:, seg(place)] = packed[place]
    slopes[0] = slope_one
    slopes[1] = slope_two
    sixteen[0] = inputs
    sixteen[1] = head_grad
    wide[0] = grad_lifted
    wide[1] = hidden


def ocean_weight_kernel(ids, columns, slopes, sixteen, wide, wire):
    half = ids[0] % 2
    chosen = ids[0] // 2
    weight = jnp.transpose(dot(columns[chosen], slopes[chosen], NT))
    weight = jnp.where(half == 0, weight[0:32], weight[32:64])
    for j in range(4):
        wire[32 * j : 32 * j + 32, :] = weight[:, seg(j)].astype(BF)
    rest = weight[:, 512:576]
    wire[128:144, :] = jnp.concatenate([rest[0:16], rest[16:32]], axis=1).astype(BF)
    small = [dot(sixteen[index], wide[index], NT) for index in range(2)]
    wire[144:160, :] = jnp.concatenate(small, axis=1).astype(BF)


def backward_kernel(
    scale, ids, window, flux_own, flux_strip, ocean_wire, back, head_back, lift_back,
    inputs, source, gate_one, gate_two, last,
    wire,
    head_grad, flags, weight_total, small_total, taps, sources,
):
    step = pl.program_id(0)
    half = ids[0] % 2
    chosen = 1 - jnp.where(ids[0] // 2 == 0, 1, 0)

    @pl.when(step == 0)
    def _():
        head_grad[0:8, :] = window[0:8, :] * scale
        for row in range(ROWS):
            place = row // 4
            head_grad[8:16, seg(row)] = to_window(
                flux_own[:, seg(row)], flux_strip[:, seg(place)], row, half
            )
            plain = window[8:16, seg(row)]
            east = pltpu.roll(plain, LON - 1, 1)
            west = pltpu.roll(plain, 1, 1)
            for j in range(4):
                flags[j : j + 1, seg(row)] = plain[2 + j : 3 + j]
                flags[4 + j : 5 + j, seg(row)] = (east, west)[j % 2][2 + j : 3 + j]
        taps[...] = jnp.zeros_like(taps)
        weight_total[...] = jnp.zeros_like(weight_total)
        small_total[...] = jnp.zeros_like(small_total)

    for row in range(ROWS):
        mid = source[0, :, seg(row)]
        for place, value in enumerate((pltpu.roll(mid, 1, 1), mid, pltpu.roll(mid, LON - 1, 1))):
            sources[place * CH : (place + 1) * CH, seg(row)] = keep_owned(value)
    grad = head_grad[...].astype(BF)
    slope_two = dot(head_back[...], grad) * gate_two[0].astype(F32)
    build_back(taps, 1, split_rows(slope_two), flags)
    slope_one = dot(back[1], taps[1]) * gate_one[0].astype(F32)
    build_back(taps, 0, split_rows(slope_one), flags)
    grad_lifted = dot(back[0], taps[0]).astype(BF)
    head_grad[0:8, :] += dot(lift_back[...], grad_lifted)[0:8]
    lift_weight = dot(inputs[0], grad_lifted, NT)
    head_weight = dot(grad, last[0], NT)
    small_total[...] += jnp.concatenate([lift_weight, head_weight], axis=1)
    weight_total[...] += dot(taps[chosen, 0 : 7 * CH, :], sources[...], NT)

    @pl.when(step == STEPS - 1)
    def _():
        def product(slope, side):
            rows = weight_total[slope * CH : (slope + 1) * CH, :]
            return rows[:, side * CH : (side + 1) * CH]

        blocks = [product(0, 1), product(1, 1), product(2, 1), product(0, 0), product(0, 2)]
        for j in range(4):
            straight, side = 1 + j // 2, 2 * (j % 2)
            turned_part = product(straight, side) - product(3 + j, side)
            blocks.append(product(3 + j, 1) + turned_part)
        for j in range(4):
            pair = jnp.concatenate(blocks[2 * j : 2 * j + 2], axis=1)
            wire[64 * j : 64 * j + 64, :] = pair.astype(BF)
        pair = jnp.concatenate([blocks[8][0:32], blocks[8][32:64]], axis=1)
        wire[256:288, :] = pair.astype(BF)
        wire[288:304, :] = small_total[...].astype(BF)
        wire[304:464, :] = ocean_wire[...]
        wire[464:512, :] = jnp.zeros((48, LON), BF)


def sum_kernel(sectors, devices, parts, out):
    total = parts[0].astype(F32)
    for sector in range(1, sectors):
        total = total + parts[sector].astype(F32)
    total = total.astype(BF)
    for place in range(devices):
        out[place] = total


def final_kernel(
    sectors, rows, parts, g_lift, g_conv, g_head, o_lift, o_conv, o_head, sums
):
    for group in range(4):
        for sector in range(sectors):
            piece = parts[group * sectors + sector].astype(F32)
            sums[group, sector * rows : (sector + 1) * rows, :] = piece
    for index in range(2):
        low, high = 2 * index, 2 * index + 1
        for j in range(4):
            pair = sums[low, 64 * j : 64 * j + 64, :] + sums[high, 64 * j : 64 * j + 64, :]
            g_conv[index, 2 * j] = pair[:, 0:64]
            g_conv[index, 2 * j + 1] = pair[:, 64:128]
            upper = sums[low, 304 + 32 * j : 336 + 32 * j, :]
            lower = sums[high, 304 + 32 * j : 336 + 32 * j, :]
            o_conv[index, 2 * j, 0:32] = upper[:, 0:64]
            o_conv[index, 2 * j, 32:64] = lower[:, 0:64]
            o_conv[index, 2 * j + 1, 0:32] = upper[:, 64:128]
            o_conv[index, 2 * j + 1, 32:64] = lower[:, 64:128]
        pair = sums[low, 256:288, :] + sums[high, 256:288, :]
        g_conv[index, 8, 0:32] = pair[:, 0:64]
        g_conv[index, 8, 32:64] = pair[:, 64:128]
        for side, at in ((low, 0), (high, 32)):
            piece = sums[side, 432:448, :]
            o_conv[index, 8, at : at + 16] = piece[:, 0:64]
            o_conv[index, 8, at + 16 : at + 32] = piece[:, 64:128]
    small = sums[0, 288:304, :] + sums[1, 288:304, :]
    g_lift[...] = small[0:10, 0:64]
    g_head[...] = small[0:12, 64:128]
    small = sums[0, 448:464, :]
    o_lift[...] = small[0:12, 0:64]
    o_head[...] = small[0:8, 64:128]


def shards(
    state,
    cotangent,
    neighbours,
    sea_cells,
    atm_lift,
    atm_conv,
    atm_head,
    ocn_lift,
    ocn_conv,
    ocn_head,
):
    sectors = lax.axis_size("tile")
    devices = 4 * sectors
    rows = WIRE // sectors
    scale = 1.0 / math.sqrt(devices * CELLS)
    group = lax.axis_index("group")
    ids = group.astype(jnp.int32).reshape(1)

    partner = []
    beside = []
    for g in range(4):
        for t in range(sectors):
            partner.append((g * sectors + t, (g ^ 1) * sectors + t))
            other = (t + 1) % sectors if g % 2 else (t - 1) % sectors
            beside.append((g * sectors + t, (g ^ 1) * sectors + other))

    lifts = (atm_lift.T, atm_head, ocn_lift.T, ocn_head)
    (packed,) = call(
        pack_kernel,
        [((32, CELLS), F32)],
        scratch=[
            pltpu.VMEM((K, 1, CELLS), jnp.int32),
            pltpu.VMEM((3, 1, LON), jnp.int32),
        ]
        + [pltpu.VMEM(array.shape, BF) for array in lifts]
        + [pltpu.SemaphoreType.DMA((8,))],
        in_specs=[smem()] + [hbm()] * 8,
        limit=WHOLE_VMEM,
    )(ids, state[0, 0], cotangent[0, 0], neighbours.reshape(K, 1, CELLS), sea_cells, *lifts)
    gathered = lax.all_gather(packed, "group")
    features, strip = call(
        sector_kernel,
        [((24, WIN), F32), ((24, CELLS), F32)],
        in_specs=[smem(), vmem()],
    )(ids, gathered)
    strip = lax.ppermute(strip, BOTH, beside)

    weights = call(
        weights_kernel,
        [
            ((CH, 16), BF),
            ((16, CH), BF),
            ((16, CH), BF),
            ((CH, 16), BF),
            ((2, CH, K * CH), BF),
            ((2, CH, 13 * CH), BF),
            ((CH, 16), BF),
            ((16, CH), BF),
            ((16, CH), BF),
            ((CH, 16), BF),
            ((2, CH, K * CH), BF),
            ((2, K * CH, CH), BF),
        ],
    )(gathered, atm_conv, ocn_conv)
    lift, lift_back, head, head_back, flat, back = weights[:6]
    ocean_lift, ocean_lift_back, ocean_head, ocean_head_back, ocean_flat, ocean_back = weights[6:]

    hot, hot_back = call(hot_kernel, [((K, CELLS, CELLS), BF), ((K * CELLS, CELLS), BF)])(gathered)
    strip, hot, hot_back = lax.optimization_barrier((strip, hot, hot_back))

    def whole(shape):
        return pl.BlockSpec(shape, lambda s: (0,) * len(shape))

    def at_step(shape):
        return pl.BlockSpec((1,) + shape, lambda s: (s, 0, 0))

    def at_step_back(shape):
        return pl.BlockSpec((1,) + shape, lambda s: (STEPS - 1 - s, 0, 0))

    wide = (CH, WIN)
    history = [(16, WIN), wide, wide, wide, wide]
    inputs, source, gate_one, gate_two, last, window, final = call(
        forward_kernel,
        [((STEPS,) + shape, BF) for shape in history] + [((16, WIN), F32), ((16, WIN), F32)],
        scratch=[
            pltpu.VMEM((24, WIN), F32),
            pltpu.VMEM((16, WIN), F32),
            pltpu.VMEM((K * CH, WIN), BF),
            pltpu.VMEM((4, 16, WIN), BF),
        ],
        grid=(STEPS,),
        in_specs=[
            smem(),
            whole((24, WIN)),
            whole((24, CELLS)),
            whole((CH, 16)),
            whole((2, CH, K * CH)),
            whole((16, CH)),
        ],
        out_specs=[at_step(shape) for shape in history] + [whole((16, WIN)), whole((16, WIN))],
    )(ids, features, strip, lift, flat, head)

    other_final = lax.ppermute(final, BOTH, partner)
    next_state, flux_grad, flux_strip, *ocean_parts = call(
        functools.partial(ocean_kernel, scale),
        [
            ((8, CELLS), F32),
            ((8, WIN), F32),
            ((8, CELLS), F32),
            ((2, K * CH, CELLS), BF),
            ((2, CH, CELLS), BF),
            ((2, 16, CELLS), BF),
            ((2, CH, CELLS), BF),
        ],
        scratch=[pltpu.VMEM((CH, K * CELLS), BF)],
        in_specs=[smem()] + [vmem()] * 11,
    )(
        ids, gathered, final, other_final, hot, hot_back, ocean_lift, ocean_flat, ocean_head,
        ocean_lift_back, ocean_back, ocean_head_back,
    )
    flux_strip = lax.ppermute(flux_strip, BOTH, beside)
    (ocean_wire,) = call(
        ocean_weight_kernel, [((160, LON), BF)], in_specs=[smem()] + [vmem()] * 4
    )(ids, *ocean_parts)

    (wire,) = call(
        functools.partial(backward_kernel, scale),
        [((WIRE, LON), BF)],
        scratch=[
            pltpu.VMEM((16, WIN), F32),
            pltpu.VMEM((8, WIN), F32),
            pltpu.VMEM((7 * CH, 3 * CH), F32),
            pltpu.VMEM((16, LON), F32),
            pltpu.VMEM((2, 13 * CH, WIN), BF),
            pltpu.VMEM((3 * CH, WIN), BF),
        ],
        grid=(STEPS,),
        in_specs=[
            smem(),
            whole((16, WIN)),
            whole((8, WIN)),
            whole((8, CELLS)),
            whole((160, LON)),
            whole((2, CH, 13 * CH)),
            whole((CH, 16)),
            whole((16, CH)),
        ]
        + [at_step_back(shape) for shape in history],
        out_specs=[whole((WIRE, LON))],
    )(
        ids, window, flux_grad, flux_strip, ocean_wire, back, head_back, lift_back,
        inputs, source, gate_one, gate_two, last,
    )

    parts = lax.all_to_all(wire.reshape(sectors, rows, LON), "tile", 0, 0, tiled=True)
    (sums,) = call(
        functools.partial(sum_kernel, sectors, devices), [((devices, rows, LON), BF)]
    )(parts)
    sums = lax.all_to_all(sums, BOTH, 0, 0, tiled=True)
    totals = call(
        functools.partial(final_kernel, sectors, rows),
        [
            ((10, CH), F32),
            ((2, K, CH, CH), F32),
            ((12, CH), F32),
            ((12, CH), F32),
            ((2, K, CH, CH), F32),
            ((8, CH), F32),
        ],
        scratch=[pltpu.VMEM((4, WIRE, LON), F32)],
    )(sums)
    g_lift, g_conv, g_head, o_lift, o_conv, o_head = totals
    return (next_state[None, None], g_lift.T, g_conv, g_head, o_lift.T, o_conv, o_head)


def solution(mesh):
    return jax.shard_map(
        shards,
        mesh=mesh,
        in_specs=(
            P("group", "tile", None, None),
            P("group", "tile", None, None),
            P("group", "tile", None, None),
            P(None, "tile", None),
            P(),
            P(),
            P(),
            P(),
            P(),
            P(),
        ),
        out_specs=(P("group", "tile", None, None), P(), P(), P(), P(), P(), P()),
        check_vma=False,
    )
```

```python
import functools
import math

import jax
import jax.numpy as jnp
from jax import lax
from jax.experimental import pallas as pl
from jax.experimental.pallas import tpu as pltpu
from jax.sharding import PartitionSpec as P

STEPS = 8
LON = 128
ROWS = 9
CELLS = 384
WIN = ROWS * LON
K = 9
CH = 64
HALO = 32
WIRE = 512
BOTH = ("group", "tile")
BF = jnp.bfloat16
F32 = jnp.float32
INTERPRET = False
VMEM_LIMIT = 24 * 1024 * 1024
WHOLE_VMEM = 62 * 1024 * 1024
BACK = (0, 1, 2, 5, 6, 7, 8, 3, 4, 5, 6, 7, 8)

NN = (((1,), (0,)), ((), ()))
NT = (((1,), (1,)), ((), ()))


def dot(a, b, dims=NN):
    return lax.dot_general(a, b, dims, preferred_element_type=F32)


def call(body, outs, scratch=(), in_specs=None, limit=VMEM_LIMIT):
    extra = {}
    if in_specs is not None:
        extra = {"in_specs": in_specs, "out_specs": [vmem()] * len(outs)}
    return pl.pallas_call(
        body,
        out_shape=[jax.ShapeDtypeStruct(shape, dtype) for shape, dtype in outs],
        scratch_shapes=list(scratch),
        interpret=INTERPRET,
        compiler_params=pltpu.CompilerParams(vmem_limit_bytes=limit),
        **extra,
    )


def smem():
    return pl.BlockSpec(memory_space=pltpu.SMEM)


def hbm():
    return pl.BlockSpec(memory_space=pltpu.HBM)


def vmem():
    return pl.BlockSpec(memory_space=pltpu.VMEM)


def lane_ids(shape):
    return lax.broadcasted_iota(jnp.int32, shape, len(shape) - 1)


def sigmoid(value):
    return 0.5 * jnp.tanh(0.5 * value) + 0.5


def seg(row):
    return slice(row * LON, (row + 1) * LON)


def pack_strip(read, half, shape):
    start = jnp.where(half == 0, 0, LON - HALO)
    quarter = lane_ids(shape) // HALO
    packed = []
    for block in range(3):
        total = jnp.zeros(shape, F32)
        for place in range(4):
            row = 4 * block + place
            if row < ROWS:
                moved = pltpu.roll(read(row), lax.rem(HALO * place - start + 2 * LON, LON), 1)
                total = jnp.where(quarter == place, moved, total)
        packed.append(total)
    return packed


def to_window(own, strip, row, half):
    place = row % 4
    lanes = lane_ids(own.shape)
    target = jnp.where(half == 0, LON - HALO, 0)
    moved = pltpu.roll(strip, lax.rem(target - HALO * place + 2 * LON, LON), 1)
    outside = (lanes >= target) & (lanes < target + HALO)
    merged = jnp.where(outside, moved, own)
    return pltpu.roll(merged, jnp.where(half == 0, HALO, LON - HALO), 1)


def pack_kernel(
    ids, state, cotangent, table, sea, atm_lift, atm_head, ocn_lift, ocn_head,
    out, held, held_sea, near_one, near_two, near_three, near_four, done,
):
    near = (near_one, near_two, near_three, near_four)
    pairs = [(state, out.at[0:8]), (cotangent, out.at[8:16]), (table, held), (sea, held_sea)]
    pairs += list(zip((atm_lift, atm_head, ocn_lift, ocn_head), near))
    copies = [pltpu.make_async_copy(a, b, done.at[i]) for i, (a, b) in enumerate(pairs)]
    for copy in copies:
        copy.start()
    for copy in copies:
        copy.wait()
    small = [to_sixteen(ref[...]) for ref in near]
    small = jnp.concatenate(small + [jnp.zeros((16, LON), F32)], axis=1)
    share = small[0:4]
    for place in range(1, 4):
        share = jnp.where(ids[0] == place, small[4 * place : 4 * place + 4], share)
    rows = [held[k].astype(F32) for k in range(K)]
    rows.append(jnp.concatenate([held_sea[cycle] for cycle in range(3)], axis=1).astype(F32))
    rows += [share, jnp.zeros((2, CELLS), F32)]
    out[16:32, :] = jnp.concatenate(rows, axis=0)


def turned(value):
    return jnp.transpose(value.astype(F32)).astype(BF)


def to_sixteen(value):
    zeros = jnp.zeros((16 - value.shape[0], value.shape[1]), F32)
    return jnp.concatenate([value.astype(F32), zeros], axis=0)


def weights_kernel(
    gathered, atm_conv, ocn_conv,
    lift, lift_back, head, head_back, flat, back,
    ocean_lift, ocean_lift_back, ocean_head, ocean_head_back, ocean_flat, ocean_back,
):
    small = jnp.concatenate([gathered[group, 26:30, :] for group in range(4)], axis=0)
    lift[...] = turned(small[:, 0:64])
    head_back[...] = turned(small[:, 64:128])
    row_ids = lax.broadcasted_iota(jnp.int32, (16, CH), 0)
    fields = jnp.where(row_ids < 8, small[:, 64:128], 0.0).astype(BF)
    mixed = dot(turned(small[:, 0:64]), fields)
    head[...] = jnp.concatenate([small[:, 64:128], mixed], axis=0).astype(BF)
    lift_back[...] = jnp.concatenate([small[:, 0:64], jnp.transpose(mixed)], axis=0).astype(BF)
    ocean_lift_back[...] = small[:, 128:192].astype(BF)
    ocean_lift[...] = turned(small[:, 128:192])
    ocean_head[...] = small[:, 192:256].astype(BF)
    ocean_head_back[...] = turned(small[:, 192:256])
    for index in range(2):
        blocks = [atm_conv[index, k] for k in range(K)]
        flat[index] = jnp.concatenate(blocks, axis=1)
        blocks = [turned(block) for block in blocks]
        back[index] = jnp.concatenate([blocks[k] for k in BACK], axis=1)
        blocks = [ocn_conv[index, k] for k in range(K)]
        ocean_flat[index] = jnp.concatenate(blocks, axis=1)
        for k in range(K):
            ocean_back[index, k * CH : (k + 1) * CH, :] = turned(blocks[k])


def hot_kernel(gathered, hot, hot_back):
    table = gathered[3, 16:32, :]
    columns = jnp.transpose(table).astype(jnp.int32)
    table = table.astype(jnp.int32)
    cell_rows = lax.broadcasted_iota(jnp.int32, (CELLS, CELLS), 0)
    cell_lanes = lane_ids((CELLS, CELLS))
    for k in range(K):
        hot[k] = jnp.where(cell_rows == table[k : k + 1], 1.0, 0.0).astype(BF)
        target = columns[:, k : k + 1]
        hot_back[k * CELLS : (k + 1) * CELLS, :] = jnp.where(cell_lanes == target, 1.0, 0.0).astype(BF)


def one_hot_sea(row):
    cells = lax.broadcasted_iota(jnp.int32, (CELLS, LON), 0)
    return jnp.where(cells == row, 1.0, 0.0).astype(BF)


def sea_row(gathered, cycle):
    return gathered[3, 25:26, cycle * LON : (cycle + 1) * LON].astype(jnp.int32)


def sector_kernel(ids, gathered, features, strip):
    half = ids[0] % 2
    for cycle in range(3):
        cols = slice(cycle * CELLS, (cycle + 1) * CELLS)
        features[0:16, cols] = gathered[cycle, 0:16, :]
        warm = gathered[3, 0:8, cycle * LON : (cycle + 1) * LON]
        row_ids = lax.broadcasted_iota(jnp.int32, (8, LON), 0)
        sources = jnp.where(row_ids == 0, warm[0:1], jnp.where(row_ids == 1, 1.0, 0.0))
        sources = jnp.concatenate([sources, jnp.zeros((8, LON), F32)], axis=0).astype(BF)
        placed = dot(sources, one_hot_sea(sea_row(gathered, cycle)), NT)[0:8]
        features[16:24, cols] = placed
        table = gathered[cycle, 16:32, :]
        features[18:20, cols] = jnp.where(table[5:7] == table[1:2], 1.0, 0.0)
        features[20:22, cols] = jnp.where(table[7:9] == table[2:3], 1.0, 0.0)
    packed = pack_strip(lambda row: features[:, seg(row)], half, (24, LON))
    for block in range(3):
        strip[:, seg(block)] = packed[block]


def pick(mask, chosen, other):
    shape = (CH // 16, 16, LON)
    result = jnp.where(mask[None], chosen.reshape(shape), other.reshape(shape))
    return result.reshape(CH, LON)


def shifted(piece):
    mid = piece.astype(BF)
    return mid, pltpu.roll(mid, 1, 1), pltpu.roll(mid, LON - 1, 1)


def build_columns(out, rows, flags):
    for row in range(ROWS):
        mid, west, east = shifted(rows[row])
        places = [(0, row, mid), (3, row, west), (4, row, east)]
        for cell, straight, first in ((row + 1, 1, 5), (row - 1, 2, 7)):
            if 0 <= cell < ROWS:
                places.append((straight, cell, mid))
                for side, k in ((west, first), (east, first + 1)):
                    flag = flags[k - 5, :, seg(cell)] > 0.5
                    places.append((k, cell, pick(flag, mid, side)))
        for k, cell, value in places:
            out[k * CH : (k + 1) * CH, seg(cell)] = value


def build_back(out, at, rows, flags):
    mid = [piece.astype(BF) for piece in rows]
    from_east = [pltpu.roll(piece, LON - 1, 1).astype(BF) for piece in rows]
    from_west = [pltpu.roll(piece, 1, 1).astype(BF) for piece in rows]
    zero = jnp.zeros((CH, LON), BF)

    def flag(index, row):
        return flags[index : index + 1, seg(row)] > 0.5

    for row in range(ROWS):
        blocks = {0: mid[row], 7: from_east[row], 8: from_west[row]}
        for source, straight, first in ((row + 1, 1, 0), (row - 1, 2, 2)):
            if 0 <= source < ROWS:
                blocks[straight] = mid[source]
                blocks[3 + first] = jnp.where(flag(first, source), mid[source], zero)
                blocks[4 + first] = jnp.where(flag(first + 1, source), mid[source], zero)
                blocks[9 + first] = jnp.where(flag(4 + first, source), zero, from_east[source])
                blocks[10 + first] = jnp.where(flag(5 + first, source), zero, from_west[source])
        for j, value in blocks.items():
            out[at, j * CH : (j + 1) * CH, seg(row)] = value


def split_rows(value):
    return [value[:, seg(row)] for row in range(ROWS)]


def keep_owned(value):
    lanes = lane_ids(value.shape) % LON
    return jnp.where((lanes >= HALO) & (lanes < LON - HALO), value, jnp.zeros_like(value))


def forward_kernel(
    ids, features, strip, lift, flat, head,
    inputs_out, source_out, gate_one, gate_two, last_out, window_out, final_out,
    window, total, columns, columns_two, flags, surface, lifted_total,
):
    half = ids[0] % 2
    first = ids[0] // 2 == 0

    for row in range(ROWS):
        block = row // 4
        window[:, seg(row)] = to_window(features[:, seg(row)], strip[:, seg(block)], row, half)
    total[0:8, :] = window[0:8, :]
    total[8:16, :] = jnp.zeros((8, WIN), F32)
    window_out[...] = window[8:24, :]
    for j in range(4):
        flags[j] = jnp.broadcast_to(window[18 + j : 19 + j, :], (16, WIN)).astype(BF)
    for held in (columns, columns_two):
        for row, blocks in ((0, (1, 5, 6)), (ROWS - 1, (2, 7, 8))):
            for k in blocks:
                held[k * CH : (k + 1) * CH, seg(row)] = jnp.zeros((CH, LON), BF)

    row_ids = lax.broadcasted_iota(jnp.int32, (8, WIN), 0)
    surface[...] = jnp.where(row_ids < 2, window[16:24, :], 0.0)
    inputs = jnp.concatenate([total[0:8, :], surface[...]], axis=0)
    lifted_total[...] = dot(lift[...], inputs.astype(BF))

    for at in range(STEPS):
        inputs = jnp.concatenate([total[0:8, :], surface[...]], axis=0)
        inputs_out[at] = keep_owned(inputs).astype(BF)
        lifted = lifted_total[...]
        build_columns(columns, [lifted[:, seg(row)] for row in range(ROWS)], flags)
        pre = dot(flat[0], columns[...])
        gate = sigmoid(pre)
        hidden = pre * gate
        gate_one[at] = (gate + hidden - hidden * gate).astype(BF)
        source_out[at] = jnp.where(first, lifted, hidden).astype(BF)
        build_columns(columns_two, [hidden[:, seg(row)] for row in range(ROWS)], flags)
        pre = dot(flat[1], columns_two[...])
        gate = sigmoid(pre)
        hidden = pre * gate
        gate_two[at] = (gate + hidden - hidden * gate).astype(BF)
        last_out[at] = keep_owned(hidden).astype(BF)
        hidden = hidden.astype(BF)
        change = dot(head[...], hidden)
        total[...] += change[0:16]
        lifted_total[...] += change[16:]

    for row in range(ROWS):
        shift = jnp.where(half == 0, LON - HALO, HALO)
        final_out[:, seg(row)] = pltpu.roll(total[:, seg(row)], shift, 1)


def ocean_kernel(
    scale, ids, gathered, own, other, hot, hot_back,
    lift, flat, head, lift_back, flat_back, head_back,
    next_state, flux_grad, strip, columns, slopes, sixteen, wide,
    scatter,
):
    group = ids[0]
    half = group % 2
    lanes = lane_ids((16, WIN))
    mine = ((lanes % LON) // (LON // 2)) == half
    merged = jnp.where(mine, own[...], other[...])
    flux = (merged[8:16, :] * (1.0 / STEPS)).astype(BF)
    flux = jnp.concatenate([flux, flux], axis=0)
    hot_sea = [one_hot_sea(sea_row(gathered, cycle)) for cycle in range(3)]
    forcing = [
        dot(flux[:, cycle * CELLS : (cycle + 1) * CELLS], hot_sea[cycle])[0:8] for cycle in range(3)
    ]
    forcing = jnp.concatenate(forcing, axis=1)
    fields = gathered[3, 0:8, :]
    inputs = jnp.concatenate([fields, forcing], axis=0).astype(BF)

    def gather(at, value):
        for k in range(K):
            columns[at, k * CH : (k + 1) * CH, :] = dot(value, hot[k]).astype(BF)

    def spread(index, slope):
        parts = dot(flat_back[index], slope).astype(BF)
        for k in range(K):
            scatter[:, k * CELLS : (k + 1) * CELLS] = parts[k * CH : (k + 1) * CH]
        return dot(scatter[...], hot_back[...])

    lifted = dot(lift[...], inputs).astype(BF)
    gather(0, lifted)
    pre = dot(flat[0], columns[0])
    gate = sigmoid(pre)
    hidden = pre * gate
    slope_of_one = gate + hidden - hidden * gate
    gather(1, hidden.astype(BF))
    pre = dot(flat[1], columns[1])
    gate = sigmoid(pre)
    hidden = pre * gate
    slope_of_two = gate + hidden - hidden * gate
    hidden = hidden.astype(BF)
    ocean_next = fields + dot(head[...], hidden)[0:8]
    block = jnp.where(group == 0, merged[0:8, 0:CELLS], ocean_next)
    block = jnp.where(group == 1, merged[0:8, CELLS : 2 * CELLS], block)
    next_state[...] = jnp.where(group == 2, merged[0:8, 2 * CELLS : 3 * CELLS], block)

    head_grad = gathered[3, 8:16, :] * scale
    head_grad = jnp.concatenate([head_grad, jnp.zeros((8, CELLS), F32)], axis=0).astype(BF)
    slope_two = (dot(head_back[...], head_grad) * slope_of_two).astype(BF)
    slope_one = (spread(1, slope_two) * slope_of_one).astype(BF)
    grad_lifted = spread(0, slope_one).astype(BF)
    forcing_grad = dot(lift_back[...], grad_lifted)[8:16]
    forcing_grad = (forcing_grad * (1.0 / STEPS)).astype(BF)
    forcing_grad = jnp.concatenate([forcing_grad, forcing_grad], axis=0)
    for cycle in range(3):
        part = forcing_grad[:, cycle * LON : (cycle + 1) * LON]
        flux_grad[:, cycle * CELLS : (cycle + 1) * CELLS] = dot(part, hot_sea[cycle], NT)[0:8]
    packed = pack_strip(lambda row: flux_grad[:, seg(row)], half, (8, LON))
    for place in range(3):
        strip[:, seg(place)] = packed[place]
    slopes[0] = slope_one
    slopes[1] = slope_two
    sixteen[0] = inputs
    sixteen[1] = head_grad
    wide[0] = grad_lifted
    wide[1] = hidden


def ocean_weight_kernel(ids, columns, slopes, sixteen, wide, wire):
    half = ids[0] % 2
    chosen = ids[0] // 2
    weight = jnp.transpose(dot(columns[chosen], slopes[chosen], NT))
    weight = jnp.where(half == 0, weight[0:32], weight[32:64])
    for j in range(4):
        wire[32 * j : 32 * j + 32, :] = weight[:, seg(j)].astype(BF)
    rest = weight[:, 512:576]
    wire[128:144, :] = jnp.concatenate([rest[0:16], rest[16:32]], axis=1).astype(BF)
    small = [dot(sixteen[index], wide[index], NT) for index in range(2)]
    wire[144:160, :] = jnp.concatenate(small, axis=1).astype(BF)


def backward_kernel(
    scale, ids, window, flux_own, flux_strip, ocean_wire, back, head_back, lift_back,
    inputs, source, gate_one, gate_two, last,
    wire,
    head_grad, flags, weight_total, small_total, taps_even, taps_odd, sources_even, sources_odd, grad_total,
):
    half = ids[0] % 2
    all_taps = (taps_even, taps_odd)
    all_sources = (sources_even, sources_odd)
    chosen = 1 - jnp.where(ids[0] // 2 == 0, 1, 0)

    head_grad[0:8, :] = window[0:8, :] * scale
    for row in range(ROWS):
        place = row // 4
        head_grad[8:16, seg(row)] = to_window(
            flux_own[:, seg(row)], flux_strip[:, seg(place)], row, half
        )
        plain = window[8:16, seg(row)]
        east = pltpu.roll(plain, LON - 1, 1)
        west = pltpu.roll(plain, 1, 1)
        for j in range(4):
            flags[j : j + 1, seg(row)] = plain[2 + j : 3 + j]
            flags[4 + j : 5 + j, seg(row)] = (east, west)[j % 2][2 + j : 3 + j]
    for taps in all_taps:
        for row, blocks in ((ROWS - 1, (1, 3, 4, 9, 10)), (0, (2, 5, 6, 11, 12))):
            for j in blocks:
                for at in range(2):
                    taps[at, j * CH : (j + 1) * CH, seg(row)] = jnp.zeros((CH, LON), BF)
    grad_total[...] = dot(head_back[...], head_grad[...].astype(BF))
    weight_total[...] = jnp.zeros_like(weight_total)
    small_total[...] = jnp.zeros_like(small_total)

    for at in reversed(range(STEPS)):
        taps = all_taps[at % 2]
        sources = all_sources[at % 2]
        for row in range(ROWS):
            mid = source[at, :, seg(row)]
            for place, value in enumerate((pltpu.roll(mid, 1, 1), mid, pltpu.roll(mid, LON - 1, 1))):
                sources[place * CH : (place + 1) * CH, seg(row)] = keep_owned(value)
        grad = head_grad[...].astype(BF)
        slope_two = grad_total[...] * gate_two[at].astype(F32)
        build_back(taps, 1, split_rows(slope_two), flags)
        slope_one = dot(back[1], taps[1]) * gate_one[at].astype(F32)
        build_back(taps, 0, split_rows(slope_one), flags)
        grad_lifted = dot(back[0], taps[0]).astype(BF)
        change = dot(lift_back[...], grad_lifted)
        grad_total[...] += change[16:]
        head_grad[0:8, :] += change[0:8]
        lift_weight = dot(inputs[at], grad_lifted, NT)
        head_weight = dot(grad, last[at], NT)
        small_total[...] += jnp.concatenate([lift_weight, head_weight], axis=1)
        weight_total[...] += dot(taps[chosen, 0 : 7 * CH, :], sources[...], NT)

    def product(slope, side):
        rows = weight_total[slope * CH : (slope + 1) * CH, :]
        return rows[:, side * CH : (side + 1) * CH]

    blocks = [product(0, 1), product(1, 1), product(2, 1), product(0, 0), product(0, 2)]
    for j in range(4):
        straight, side = 1 + j // 2, 2 * (j % 2)
        turned_part = product(straight, side) - product(3 + j, side)
        blocks.append(product(3 + j, 1) + turned_part)
    for j in range(4):
        pair = jnp.concatenate(blocks[2 * j : 2 * j + 2], axis=1)
        wire[64 * j : 64 * j + 64, :] = pair.astype(BF)
    pair = jnp.concatenate([blocks[8][0:32], blocks[8][32:64]], axis=1)
    wire[256:288, :] = pair.astype(BF)
    wire[288:304, :] = small_total[...].astype(BF)
    wire[304:464, :] = ocean_wire[...]
    wire[464:512, :] = jnp.zeros((48, LON), BF)


def sum_kernel(sectors, devices, parts, out):
    total = parts[0].astype(F32)
    for sector in range(1, sectors):
        total = total + parts[sector].astype(F32)
    total = total.astype(BF)
    for place in range(devices):
        out[place] = total


def final_kernel(
    sectors, rows, parts, g_lift, g_conv, g_head, o_lift, o_conv, o_head, sums
):
    for group in range(4):
        for sector in range(sectors):
            piece = parts[group * sectors + sector].astype(F32)
            sums[group, sector * rows : (sector + 1) * rows, :] = piece
    for index in range(2):
        low, high = 2 * index, 2 * index + 1
        for j in range(4):
            pair = sums[low, 64 * j : 64 * j + 64, :] + sums[high, 64 * j : 64 * j + 64, :]
            g_conv[index, 2 * j] = pair[:, 0:64]
            g_conv[index, 2 * j + 1] = pair[:, 64:128]
            upper = sums[low, 304 + 32 * j : 336 + 32 * j, :]
            lower = sums[high, 304 + 32 * j : 336 + 32 * j, :]
            o_conv[index, 2 * j, 0:32] = upper[:, 0:64]
            o_conv[index, 2 * j, 32:64] = lower[:, 0:64]
            o_conv[index, 2 * j + 1, 0:32] = upper[:, 64:128]
            o_conv[index, 2 * j + 1, 32:64] = lower[:, 64:128]
        pair = sums[low, 256:288, :] + sums[high, 256:288, :]
        g_conv[index, 8, 0:32] = pair[:, 0:64]
        g_conv[index, 8, 32:64] = pair[:, 64:128]
        for side, at in ((low, 0), (high, 32)):
            piece = sums[side, 432:448, :]
            o_conv[index, 8, at : at + 16] = piece[:, 0:64]
            o_conv[index, 8, at + 16 : at + 32] = piece[:, 64:128]
    small = sums[0, 288:304, :] + sums[1, 288:304, :]
    g_lift[...] = small[0:10, 0:64]
    g_head[...] = small[0:12, 64:128]
    small = sums[0, 448:464, :]
    o_lift[...] = small[0:12, 0:64]
    o_head[...] = small[0:8, 64:128]


def shards(
    state,
    cotangent,
    neighbours,
    sea_cells,
    atm_lift,
    atm_conv,
    atm_head,
    ocn_lift,
    ocn_conv,
    ocn_head,
):
    sectors = lax.axis_size("tile")
    devices = 4 * sectors
    rows = WIRE // sectors
    scale = 1.0 / math.sqrt(devices * CELLS)
    group = lax.axis_index("group")
    ids = group.astype(jnp.int32).reshape(1)

    partner = []
    beside = []
    for g in range(4):
        for t in range(sectors):
            partner.append((g * sectors + t, (g ^ 1) * sectors + t))
            other = (t + 1) % sectors if g % 2 else (t - 1) % sectors
            beside.append((g * sectors + t, (g ^ 1) * sectors + other))

    lifts = (atm_lift.T, atm_head, ocn_lift.T, ocn_head)
    (packed,) = call(
        pack_kernel,
        [((32, CELLS), F32)],
        scratch=[
            pltpu.VMEM((K, 1, CELLS), jnp.int32),
            pltpu.VMEM((3, 1, LON), jnp.int32),
        ]
        + [pltpu.VMEM(array.shape, BF) for array in lifts]
        + [pltpu.SemaphoreType.DMA((8,))],
        in_specs=[smem()] + [hbm()] * 8,
        limit=WHOLE_VMEM,
    )(ids, state[0, 0], cotangent[0, 0], neighbours.reshape(K, 1, CELLS), sea_cells, *lifts)
    gathered = lax.all_gather(packed, "group")
    features, strip = call(
        sector_kernel,
        [((24, WIN), F32), ((24, CELLS), F32)],
        in_specs=[smem(), vmem()],
    )(ids, gathered)
    strip = lax.ppermute(strip, BOTH, beside)

    weights = call(
        weights_kernel,
        [
            ((CH, 16), BF),
            ((16 + CH, CH), BF),
            ((16 + CH, CH), BF),
            ((CH, 16), BF),
            ((2, CH, K * CH), BF),
            ((2, CH, 13 * CH), BF),
            ((CH, 16), BF),
            ((16, CH), BF),
            ((16, CH), BF),
            ((CH, 16), BF),
            ((2, CH, K * CH), BF),
            ((2, K * CH, CH), BF),
        ],
    )(gathered, atm_conv, ocn_conv)
    lift, lift_back, head, head_back, flat, back = weights[:6]
    ocean_lift, ocean_lift_back, ocean_head, ocean_head_back, ocean_flat, ocean_back = weights[6:]

    hot, hot_back = call(hot_kernel, [((K, CELLS, CELLS), BF), ((K * CELLS, CELLS), BF)])(gathered)
    strip, hot, hot_back = lax.optimization_barrier((strip, hot, hot_back))

    wide = (CH, WIN)
    history = [(16, WIN), wide, wide, wide, wide]
    inputs, source, gate_one, gate_two, last, window, final = call(
        forward_kernel,
        [((STEPS,) + shape, BF) for shape in history] + [((16, WIN), F32), ((16, WIN), F32)],
        scratch=[
            pltpu.VMEM((24, WIN), F32),
            pltpu.VMEM((16, WIN), F32),
            pltpu.VMEM((K * CH, WIN), BF),
            pltpu.VMEM((K * CH, WIN), BF),
            pltpu.VMEM((4, 16, WIN), BF),
            pltpu.VMEM((8, WIN), F32),
            pltpu.VMEM((CH, WIN), F32),
        ],
        in_specs=[smem()] + [vmem()] * 5,
    )(ids, features, strip, lift, flat, head)

    other_final = lax.ppermute(final, BOTH, partner)
    next_state, flux_grad, flux_strip, *ocean_parts = call(
        functools.partial(ocean_kernel, scale),
        [
            ((8, CELLS), F32),
            ((8, WIN), F32),
            ((8, CELLS), F32),
            ((2, K * CH, CELLS), BF),
            ((2, CH, CELLS), BF),
            ((2, 16, CELLS), BF),
            ((2, CH, CELLS), BF),
        ],
        scratch=[pltpu.VMEM((CH, K * CELLS), BF)],
        in_specs=[smem()] + [vmem()] * 11,
    )(
        ids, gathered, final, other_final, hot, hot_back, ocean_lift, ocean_flat, ocean_head,
        ocean_lift_back, ocean_back, ocean_head_back,
    )
    flux_strip = lax.ppermute(flux_strip, BOTH, beside)
    (ocean_wire,) = call(
        ocean_weight_kernel, [((160, LON), BF)], in_specs=[smem()] + [vmem()] * 4
    )(ids, *ocean_parts)

    (wire,) = call(
        functools.partial(backward_kernel, scale),
        [((WIRE, LON), BF)],
        scratch=[
            pltpu.VMEM((16, WIN), F32),
            pltpu.VMEM((8, WIN), F32),
            pltpu.VMEM((7 * CH, 3 * CH), F32),
            pltpu.VMEM((16, LON), F32),
            pltpu.VMEM((2, 13 * CH, WIN), BF),
            pltpu.VMEM((2, 13 * CH, WIN), BF),
            pltpu.VMEM((3 * CH, WIN), BF),
            pltpu.VMEM((3 * CH, WIN), BF),
            pltpu.VMEM((CH, WIN), F32),
        ],
        in_specs=[smem()] + [vmem()] * 12,
    )(
        ids, window, flux_grad, flux_strip, ocean_wire, back, head_back, lift_back,
        inputs, source, gate_one, gate_two, last,
    )

    parts = lax.all_to_all(wire.reshape(sectors, rows, LON), "tile", 0, 0, tiled=True)
    (sums,) = call(
        functools.partial(sum_kernel, sectors, devices), [((devices, rows, LON), BF)]
    )(parts)
    sums = lax.all_to_all(sums, BOTH, 0, 0, tiled=True)
    totals = call(
        functools.partial(final_kernel, sectors, rows),
        [
            ((10, CH), F32),
            ((2, K, CH, CH), F32),
            ((12, CH), F32),
            ((12, CH), F32),
            ((2, K, CH, CH), F32),
            ((8, CH), F32),
        ],
        scratch=[pltpu.VMEM((4, WIRE, LON), F32)],
    )(sums)
    g_lift, g_conv, g_head, o_lift, o_conv, o_head = totals
    return (next_state[None, None], g_lift.T, g_conv, g_head, o_lift.T, o_conv, o_head)


def solution(mesh):
    return jax.shard_map(
        shards,
        mesh=mesh,
        in_specs=(
            P("group", "tile", None, None),
            P("group", "tile", None, None),
            P("group", "tile", None, None),
            P(None, "tile", None),
            P(),
            P(),
            P(),
            P(),
            P(),
            P(),
        ),
        out_specs=(P("group", "tile", None, None), P(), P(), P(), P(), P(), P()),
        check_vma=False,
    )
```

```python
import functools
import math

import jax
import jax.numpy as jnp
from jax import lax
from jax.experimental import pallas as pl
from jax.experimental.pallas import tpu as pltpu
from jax.sharding import Mesh
from jax.sharding import PartitionSpec as P

STEPS = 8
LON = 128
ROWS = 9
CELLS = 384
WIN = ROWS * LON
K = 9
CH = 64
HALO = 32
WIRE = 512
GROUP = ("high", "core")
BOTH = ("high", "core", "tile")
BF = jnp.bfloat16
F32 = jnp.float32
INTERPRET = False
VMEM_LIMIT = 24 * 1024 * 1024
WHOLE_VMEM = 62 * 1024 * 1024
BACK = (
    ((0, 1), (1, 1), (2, 1), (5, 1), (6, 1), (7, 1), (8, 1)),
    ((3, 1), (5, 1), (7, 1), (5, -1), None, (7, -1), None),
    ((4, 1), (6, 1), (8, 1), None, (6, -1), None, (8, -1)),
)

NN = (((1,), (0,)), ((), ()))
NT = (((1,), (1,)), ((), ()))


def dot(a, b, dims=NN):
    return lax.dot_general(a, b, dims, preferred_element_type=F32)


def call(body, outs, scratch=(), in_specs=None, limit=VMEM_LIMIT):
    extra = {}
    if in_specs is not None:
        extra = {"in_specs": in_specs, "out_specs": [vmem()] * len(outs)}
    return pl.pallas_call(
        body,
        out_shape=[jax.ShapeDtypeStruct(shape, dtype) for shape, dtype in outs],
        scratch_shapes=list(scratch),
        interpret=INTERPRET,
        compiler_params=pltpu.CompilerParams(vmem_limit_bytes=limit),
        **extra,
    )


def smem():
    return pl.BlockSpec(memory_space=pltpu.SMEM)


def hbm():
    return pl.BlockSpec(memory_space=pltpu.HBM)


def vmem():
    return pl.BlockSpec(memory_space=pltpu.VMEM)


def lane_ids(shape):
    return lax.broadcasted_iota(jnp.int32, shape, len(shape) - 1)


def sigmoid(value):
    return 0.5 * jnp.tanh(0.5 * value) + 0.5


def seg(row):
    return slice(row * LON, (row + 1) * LON)


def pack_strip(read, half, shape):
    start = jnp.where(half == 0, 0, LON - HALO)
    quarter = lane_ids(shape) // HALO
    packed = []
    for block in range(3):
        total = jnp.zeros(shape, F32)
        for place in range(4):
            row = 4 * block + place
            if row < ROWS:
                moved = pltpu.roll(read(row), lax.rem(HALO * place - start + 2 * LON, LON), 1)
                total = jnp.where(quarter == place, moved, total)
        packed.append(total)
    return packed


def to_window(own, strip, row, half):
    place = row % 4
    lanes = lane_ids(own.shape)
    target = jnp.where(half == 0, LON - HALO, 0)
    moved = pltpu.roll(strip, lax.rem(target - HALO * place + 2 * LON, LON), 1)
    outside = (lanes >= target) & (lanes < target + HALO)
    merged = jnp.where(outside, moved, own)
    return pltpu.roll(merged, jnp.where(half == 0, HALO, LON - HALO), 1)


def pack_kernel(
    ids, state, cotangent, table, sea, atm_lift, atm_head, ocn_lift, ocn_head,
    out, held, held_sea, near_one, near_two, near_three, near_four, done,
):
    near = (near_one, near_two, near_three, near_four)
    pairs = [(state, out.at[0:8]), (cotangent, out.at[8:16]), (table, held), (sea, held_sea)]
    pairs += list(zip((atm_lift, atm_head, ocn_lift, ocn_head), near))
    copies = [pltpu.make_async_copy(a, b, done.at[i]) for i, (a, b) in enumerate(pairs)]
    for copy in copies:
        copy.start()
    for copy in copies:
        copy.wait()
    small = [to_sixteen(ref[...]) for ref in near]
    small = jnp.concatenate(small + [jnp.zeros((16, LON), F32)], axis=1)
    share = small[0:4]
    for place in range(1, 4):
        share = jnp.where(ids[0] == place, small[4 * place : 4 * place + 4], share)
    rows = [held[k].astype(F32) for k in range(K)]
    rows.append(jnp.concatenate([held_sea[cycle] for cycle in range(3)], axis=1).astype(F32))
    rows += [share, jnp.zeros((2, CELLS), F32)]
    out[16:32, :] = jnp.concatenate(rows, axis=0)


def turned(value):
    return jnp.transpose(value.astype(F32)).astype(BF)


def to_sixteen(value):
    zeros = jnp.zeros((16 - value.shape[0], value.shape[1]), F32)
    return jnp.concatenate([value.astype(F32), zeros], axis=0)


def weights_kernel(
    gathered, atm_conv, ocn_conv,
    lift, lift_back, head, head_back, flat, back,
    ocean_lift, ocean_lift_back, ocean_head, ocean_head_back, ocean_flat, ocean_back,
):
    small = jnp.concatenate([gathered[group, 26:30, :] for group in range(4)], axis=0)
    lift[...] = turned(small[:, 0:64])
    head_back[...] = turned(small[:, 64:128])
    row_ids = lax.broadcasted_iota(jnp.int32, (16, CH), 0)
    fields = jnp.where(row_ids < 8, small[:, 64:128], 0.0).astype(BF)
    mixed = dot(turned(small[:, 0:64]), fields)
    head[...] = jnp.concatenate([small[:, 64:128], mixed], axis=0).astype(BF)
    lift_back[...] = jnp.concatenate([small[:, 0:64], jnp.transpose(mixed)], axis=0).astype(BF)
    ocean_lift_back[...] = small[:, 128:192].astype(BF)
    ocean_lift[...] = turned(small[:, 128:192])
    ocean_head[...] = small[:, 192:256].astype(BF)
    ocean_head_back[...] = turned(small[:, 192:256])
    for index in range(2):
        blocks = [atm_conv[index, k] for k in range(K)]
        flat[index] = jnp.concatenate(blocks, axis=1)
        blocks = [turned(block) for block in blocks]
        for side, terms in enumerate(BACK):
            parts = [
                jnp.zeros((CH, CH), BF) if term is None else blocks[term[0]] * term[1]
                for term in terms
            ]
            back[index, side * CH : (side + 1) * CH, :] = jnp.concatenate(parts, axis=1)
        blocks = [ocn_conv[index, k] for k in range(K)]
        ocean_flat[index] = jnp.concatenate(blocks, axis=1)
        for k in range(K):
            ocean_back[index, k * CH : (k + 1) * CH, :] = turned(blocks[k])


def hot_kernel(gathered, hot, hot_back):
    table = gathered[3, 16:32, :]
    columns = jnp.transpose(table).astype(jnp.int32)
    table = table.astype(jnp.int32)
    cell_rows = lax.broadcasted_iota(jnp.int32, (CELLS, CELLS), 0)
    cell_lanes = lane_ids((CELLS, CELLS))
    for k in range(K):
        place = slice(k * CELLS, (k + 1) * CELLS)
        hot[k] = jnp.where(cell_rows == table[k : k + 1], 1.0, 0.0).astype(BF)
        target = columns[:, k : k + 1]
        hot_back[place, :] = jnp.where(cell_lanes == target, 1.0, 0.0).astype(BF)


def one_hot_sea(row):
    cells = lax.broadcasted_iota(jnp.int32, (CELLS, LON), 0)
    return jnp.where(cells == row, 1.0, 0.0).astype(BF)


def sea_row(gathered, cycle):
    return gathered[3, 25:26, cycle * LON : (cycle + 1) * LON].astype(jnp.int32)


def sector_kernel(ids, gathered, features, strip):
    half = ids[0] % 2
    for cycle in range(3):
        cols = slice(cycle * CELLS, (cycle + 1) * CELLS)
        features[0:16, cols] = gathered[cycle, 0:16, :]
        warm = gathered[3, 0:8, cycle * LON : (cycle + 1) * LON]
        row_ids = lax.broadcasted_iota(jnp.int32, (8, LON), 0)
        sources = jnp.where(row_ids == 0, warm[0:1], jnp.where(row_ids == 1, 1.0, 0.0))
        sources = jnp.concatenate([sources, jnp.zeros((8, LON), F32)], axis=0).astype(BF)
        placed = dot(sources, one_hot_sea(sea_row(gathered, cycle)), NT)[0:8]
        features[16:24, cols] = placed
        table = gathered[cycle, 16:32, :]
        features[18:20, cols] = jnp.where(table[5:7] == table[1:2], 1.0, 0.0)
        features[20:22, cols] = jnp.where(table[7:9] == table[2:3], 1.0, 0.0)
    packed = pack_strip(lambda row: features[:, seg(row)], half, (24, LON))
    for block in range(3):
        strip[:, seg(block)] = packed[block]


def pick(mask, chosen, other):
    shape = (CH // 16, 16, LON)
    result = jnp.where(mask[None], chosen.reshape(shape), other.reshape(shape))
    return result.reshape(CH, LON)


def shifted(piece):
    mid = piece.astype(BF)
    return mid, pltpu.roll(mid, 1, 1), pltpu.roll(mid, LON - 1, 1)


def build_columns(out, rows, flags):
    for row in range(ROWS):
        mid, west, east = shifted(rows[row])
        places = [(0, row, mid), (3, row, west), (4, row, east)]
        for cell, straight, first in ((row + 1, 1, 5), (row - 1, 2, 7)):
            if 0 <= cell < ROWS:
                places.append((straight, cell, mid))
                for side, k in ((west, first), (east, first + 1)):
                    flag = flags[k - 5, :, seg(cell)] > 0.5
                    places.append((k, cell, pick(flag, mid, side)))
        for k, cell, value in places:
            out[k * CH : (k + 1) * CH, seg(cell)] = value


def build_back(out, at, rows, flags):
    mid = [piece.astype(BF) for piece in rows]
    zero = jnp.zeros((CH, LON), BF)
    for row in range(ROWS):
        blocks = {0: mid[row]}
        for source, straight, first in ((row + 1, 1, 0), (row - 1, 2, 2)):
            if 0 <= source < ROWS:
                blocks[straight] = mid[source]
                for j in (first, first + 1):
                    flag = flags[j : j + 1, seg(source)] > 0.5
                    blocks[3 + j] = jnp.where(flag, mid[source], zero)
        for j, value in blocks.items():
            out[at, j * CH : (j + 1) * CH, seg(row)] = value


def join_sides(value):
    rows = []
    for row in range(ROWS):
        here = value[0:CH, seg(row)]
        west = pltpu.roll(value[CH : 2 * CH, seg(row)], LON - 1, 1)
        east = pltpu.roll(value[2 * CH : 3 * CH, seg(row)], 1, 1)
        rows.append(here + west + east)
    return rows


def split_rows(value):
    return [value[:, seg(row)] for row in range(ROWS)]


def keep_owned(value):
    lanes = lane_ids(value.shape) % LON
    return jnp.where((lanes >= HALO) & (lanes < LON - HALO), value, jnp.zeros_like(value))


def forward_kernel(
    ids, features, strip, lift, flat, head,
    inputs_out, source_out, gate_one, gate_two, last_out, window_out, final_out,
    window, total, columns, columns_two, flags, surface, lifted_total,
):
    half = ids[0] % 2
    first = ids[0] // 2 == 0

    for row in range(ROWS):
        block = row // 4
        window[:, seg(row)] = to_window(features[:, seg(row)], strip[:, seg(block)], row, half)
    total[0:8, :] = window[0:8, :]
    total[8:16, :] = jnp.zeros((8, WIN), F32)
    window_out[...] = window[8:24, :]
    for j in range(4):
        flags[j] = jnp.broadcast_to(window[18 + j : 19 + j, :], (16, WIN)).astype(BF)
    for held in (columns, columns_two):
        for row, blocks in ((0, (1, 5, 6)), (ROWS - 1, (2, 7, 8))):
            for k in blocks:
                held[k * CH : (k + 1) * CH, seg(row)] = jnp.zeros((CH, LON), BF)

    row_ids = lax.broadcasted_iota(jnp.int32, (8, WIN), 0)
    surface[...] = jnp.where(row_ids < 2, window[16:24, :], 0.0)
    inputs = jnp.concatenate([total[0:8, :], surface[...]], axis=0)
    lifted_total[...] = dot(lift[...], inputs.astype(BF))

    for at in range(STEPS):
        inputs = jnp.concatenate([total[0:8, :], surface[...]], axis=0)
        inputs_out[at] = keep_owned(inputs).astype(BF)
        lifted = lifted_total[...]
        build_columns(columns, [lifted[:, seg(row)] for row in range(ROWS)], flags)
        pre = dot(flat[0], columns[...])
        gate = sigmoid(pre)
        hidden = pre * gate
        gate_one[at] = (gate + hidden - hidden * gate).astype(BF)
        source_out[at] = jnp.where(first, columns[0:CH, :], hidden.astype(BF))
        build_columns(columns_two, [hidden[:, seg(row)] for row in range(ROWS)], flags)
        pre = dot(flat[1], columns_two[...])
        gate = sigmoid(pre)
        hidden = pre * gate
        gate_two[at] = (gate + hidden - hidden * gate).astype(BF)
        hidden = hidden.astype(BF)
        last_out[at] = hidden
        change = dot(head[...], hidden)
        total[...] += change[0:16]
        lifted_total[...] += change[16:]

    for row in range(ROWS):
        shift = jnp.where(half == 0, LON - HALO, HALO)
        final_out[:, seg(row)] = pltpu.roll(total[:, seg(row)], shift, 1)


def ocean_kernel(
    scale, ids, gathered, own, other, hot, hot_back,
    lift, flat, head, lift_back, flat_back, head_back,
    next_state, flux_grad, strip, columns, slopes, sixteen, wide,
    scatter,
):
    group = ids[0]
    half = group % 2
    lanes = lane_ids((16, WIN))
    mine = ((lanes % LON) // (LON // 2)) == half
    merged = jnp.where(mine, own[...], other[...])
    flux = (merged[8:16, :] * (1.0 / STEPS)).astype(BF)
    flux = jnp.concatenate([flux, flux], axis=0)
    hot_sea = [one_hot_sea(sea_row(gathered, cycle)) for cycle in range(3)]
    forcing = [
        dot(flux[:, cycle * CELLS : (cycle + 1) * CELLS], hot_sea[cycle])[0:8] for cycle in range(3)
    ]
    forcing = jnp.concatenate(forcing, axis=1)
    fields = gathered[3, 0:8, :]
    inputs = jnp.concatenate([fields, forcing], axis=0).astype(BF)

    def gather(at, value):
        for k in range(K):
            columns[at, k * CH : (k + 1) * CH, :] = dot(value, hot[k]).astype(BF)

    def spread(index, slope):
        parts = dot(flat_back[index], slope).astype(BF)
        for k in range(K):
            scatter[:, k * CELLS : (k + 1) * CELLS] = parts[k * CH : (k + 1) * CH]
        return dot(scatter[...], hot_back[...])

    lifted = dot(lift[...], inputs).astype(BF)
    gather(0, lifted)
    pre = dot(flat[0], columns[0])
    gate = sigmoid(pre)
    hidden = pre * gate
    slope_of_one = gate + hidden - hidden * gate
    gather(1, hidden.astype(BF))
    pre = dot(flat[1], columns[1])
    gate = sigmoid(pre)
    hidden = pre * gate
    slope_of_two = gate + hidden - hidden * gate
    hidden = hidden.astype(BF)
    ocean_next = fields + dot(head[...], hidden)[0:8]
    block = jnp.where(group == 0, merged[0:8, 0:CELLS], ocean_next)
    block = jnp.where(group == 1, merged[0:8, CELLS : 2 * CELLS], block)
    next_state[...] = jnp.where(group == 2, merged[0:8, 2 * CELLS : 3 * CELLS], block)

    head_grad = gathered[3, 8:16, :] * scale
    head_grad = jnp.concatenate([head_grad, jnp.zeros((8, CELLS), F32)], axis=0).astype(BF)
    slope_two = (dot(head_back[...], head_grad) * slope_of_two).astype(BF)
    slope_one = (spread(1, slope_two) * slope_of_one).astype(BF)
    grad_lifted = spread(0, slope_one).astype(BF)
    forcing_grad = dot(lift_back[...], grad_lifted)[8:16]
    forcing_grad = (forcing_grad * (1.0 / STEPS)).astype(BF)
    forcing_grad = jnp.concatenate([forcing_grad, forcing_grad], axis=0)
    for cycle in range(3):
        part = forcing_grad[:, cycle * LON : (cycle + 1) * LON]
        flux_grad[:, cycle * CELLS : (cycle + 1) * CELLS] = dot(part, hot_sea[cycle], NT)[0:8]
    packed = pack_strip(lambda row: flux_grad[:, seg(row)], half, (8, LON))
    for place in range(3):
        strip[:, seg(place)] = packed[place]
    slopes[0] = slope_one
    slopes[1] = slope_two
    sixteen[0] = inputs
    sixteen[1] = head_grad
    wide[0] = grad_lifted
    wide[1] = hidden


def ocean_weight_kernel(ids, columns, slopes, sixteen, wide, wire):
    half = ids[0] % 2
    chosen = ids[0] // 2
    weight = jnp.transpose(dot(columns[chosen], slopes[chosen], NT))
    weight = jnp.where(half == 0, weight[0:32], weight[32:64])
    for j in range(4):
        wire[32 * j : 32 * j + 32, :] = weight[:, seg(j)].astype(BF)
    rest = weight[:, 512:576]
    wire[128:144, :] = jnp.concatenate([rest[0:16], rest[16:32]], axis=1).astype(BF)
    small = [dot(sixteen[index], wide[index], NT) for index in range(2)]
    wire[144:160, :] = jnp.concatenate(small, axis=1).astype(BF)


def backward_kernel(
    scale, ids, window, flux_own, flux_strip, ocean_wire, back, head_back, lift_back,
    inputs, source, gate_one, gate_two, last,
    wire,
    head_grad, flags, weight_total, small_total, taps_even, taps_odd, sources_even, sources_odd, grad_total,
):
    half = ids[0] % 2
    all_taps = (taps_even, taps_odd)
    all_sources = (sources_even, sources_odd)
    chosen = 1 - jnp.where(ids[0] // 2 == 0, 1, 0)

    head_grad[0:8, :] = window[0:8, :] * scale
    for row in range(ROWS):
        place = row // 4
        head_grad[8:16, seg(row)] = to_window(
            flux_own[:, seg(row)], flux_strip[:, seg(place)], row, half
        )
    flags[0:4, :] = window[10:14, :]
    for taps in all_taps:
        for row, blocks in ((ROWS - 1, (1, 3, 4)), (0, (2, 5, 6))):
            for j in blocks:
                for at in range(2):
                    taps[at, j * CH : (j + 1) * CH, seg(row)] = jnp.zeros((CH, LON), BF)
    grad_total[...] = dot(head_back[...], head_grad[...].astype(BF))
    weight_total[...] = jnp.zeros_like(weight_total)
    small_total[...] = jnp.zeros_like(small_total)

    for at in reversed(range(STEPS)):
        taps = all_taps[at % 2]
        sources = all_sources[at % 2]
        for row in range(ROWS):
            mid = source[at, :, seg(row)]
            for place, value in enumerate((pltpu.roll(mid, 1, 1), mid, pltpu.roll(mid, LON - 1, 1))):
                sources[place * CH : (place + 1) * CH, seg(row)] = keep_owned(value)
        grad = head_grad[...].astype(BF)
        slope_two = grad_total[...] * gate_two[at].astype(F32)
        build_back(taps, 1, split_rows(slope_two), flags)
        grad_one = join_sides(dot(back[1], taps[1]))
        slope_one = [
            grad_one[row] * gate_one[at, :, seg(row)].astype(F32) for row in range(ROWS)
        ]
        build_back(taps, 0, slope_one, flags)
        grad_lifted = jnp.concatenate(join_sides(dot(back[0], taps[0])), axis=1).astype(BF)
        change = dot(lift_back[...], grad_lifted)
        grad_total[...] += change[16:]
        head_grad[0:8, :] += change[0:8]
        lift_weight = dot(inputs[at], grad_lifted, NT)
        head_weight = dot(keep_owned(grad), last[at], NT)
        small_total[...] += jnp.concatenate([lift_weight, head_weight], axis=1)
        weight_total[...] += dot(taps[chosen], sources[...], NT)

    def product(slope, side):
        rows = weight_total[slope * CH : (slope + 1) * CH, :]
        return rows[:, side * CH : (side + 1) * CH]

    blocks = [product(0, 1), product(1, 1), product(2, 1), product(0, 0), product(0, 2)]
    for j in range(4):
        straight, side = 1 + j // 2, 2 * (j % 2)
        turned_part = product(straight, side) - product(3 + j, side)
        blocks.append(product(3 + j, 1) + turned_part)
    for j in range(4):
        pair = jnp.concatenate(blocks[2 * j : 2 * j + 2], axis=1)
        wire[64 * j : 64 * j + 64, :] = pair.astype(BF)
    pair = jnp.concatenate([blocks[8][0:32], blocks[8][32:64]], axis=1)
    wire[256:288, :] = pair.astype(BF)
    wire[288:304, :] = small_total[...].astype(BF)
    wire[304:464, :] = ocean_wire[...]
    wire[464:512, :] = jnp.zeros((48, LON), BF)


def sum_kernel(sectors, devices, parts, out):
    total = parts[0].astype(F32)
    for sector in range(1, sectors):
        total = total + parts[sector].astype(F32)
    total = total.astype(BF)
    for place in range(devices):
        out[place] = total


def final_kernel(sectors, rows, ids, own, other, g_lift, g_conv, g_head, o_lift, o_conv, o_head):
    def piece(group, start):
        place = (group // 2) * sectors + start // rows
        at = slice(start % rows, start % rows + 16)
        value = jnp.where(ids[0] % 2 == group % 2, own[place, at, :], other[place, at, :])
        return value.astype(F32)

    def spread(out, index, j, at, value):
        out[index, 2 * j, at : at + 16, :] = value[:, 0:64]
        out[index, 2 * j + 1, at : at + 16, :] = value[:, 64:128]

    for index in range(2):
        low, high = 2 * index, 2 * index + 1
        for j in range(4):
            for at in range(0, 64, 16):
                start = 64 * j + at
                spread(g_conv, index, j, at, piece(low, start) + piece(high, start))
            for at in range(0, 32, 16):
                start = 304 + 32 * j + at
                spread(o_conv, index, j, at, piece(low, start))
                spread(o_conv, index, j, at + 32, piece(high, start))
        for at in range(0, 32, 16):
            pair = piece(low, 256 + at) + piece(high, 256 + at)
            g_conv[index, 8, at : at + 16, :] = pair[:, 0:64]
            g_conv[index, 8, at + 32 : at + 48, :] = pair[:, 64:128]
        for side, at in ((low, 0), (high, 32)):
            value = piece(side, 432)
            o_conv[index, 8, at : at + 16, :] = value[:, 0:64]
            o_conv[index, 8, at + 16 : at + 32, :] = value[:, 64:128]
    small = piece(0, 288) + piece(1, 288)
    g_lift[...] = small[0:10, 0:64]
    g_head[...] = small[0:12, 64:128]
    small = piece(0, 448)
    o_lift[...] = small[0:12, 0:64]
    o_head[...] = small[0:8, 64:128]


def shards(
    state,
    cotangent,
    neighbours,
    sea_cells,
    atm_lift,
    atm_conv,
    atm_head,
    ocn_lift,
    ocn_conv,
    ocn_head,
):
    sectors = lax.axis_size("tile")
    devices = 4 * sectors
    rows = WIRE // sectors
    scale = 1.0 / math.sqrt(devices * CELLS)
    group = 2 * lax.axis_index("high") + lax.axis_index("core")
    ids = group.astype(jnp.int32).reshape(1)

    partner = []
    beside = []
    for g in range(4):
        for t in range(sectors):
            partner.append((g * sectors + t, (g ^ 1) * sectors + t))
            other = (t + 1) % sectors if g % 2 else (t - 1) % sectors
            beside.append((g * sectors + t, (g ^ 1) * sectors + other))

    lifts = (atm_lift.T, atm_head, ocn_lift.T, ocn_head)
    (packed,) = call(
        pack_kernel,
        [((32, CELLS), F32)],
        scratch=[
            pltpu.VMEM((K, 1, CELLS), jnp.int32),
            pltpu.VMEM((3, 1, LON), jnp.int32),
        ]
        + [pltpu.VMEM(array.shape, BF) for array in lifts]
        + [pltpu.SemaphoreType.DMA((8,))],
        in_specs=[smem()] + [hbm()] * 8,
        limit=WHOLE_VMEM,
    )(ids, state[0, 0], cotangent[0, 0], neighbours.reshape(K, 1, CELLS), sea_cells, *lifts)
    gathered = lax.all_gather(packed, GROUP)
    features, strip = call(
        sector_kernel,
        [((24, WIN), F32), ((24, CELLS), F32)],
        in_specs=[smem(), vmem()],
    )(ids, gathered)
    strip = lax.ppermute(strip, BOTH, beside)

    weights = call(
        weights_kernel,
        [
            ((CH, 16), BF),
            ((16 + CH, CH), BF),
            ((16 + CH, CH), BF),
            ((CH, 16), BF),
            ((2, CH, K * CH), BF),
            ((2, 3 * CH, 7 * CH), BF),
            ((CH, 16), BF),
            ((16, CH), BF),
            ((16, CH), BF),
            ((CH, 16), BF),
            ((2, CH, K * CH), BF),
            ((2, K * CH, CH), BF),
        ],
    )(gathered, atm_conv, ocn_conv)
    lift, lift_back, head, head_back, flat, back = weights[:6]
    ocean_lift, ocean_lift_back, ocean_head, ocean_head_back, ocean_flat, ocean_back = weights[6:]

    hot, hot_back = call(hot_kernel, [((K, CELLS, CELLS), BF), ((K * CELLS, CELLS), BF)])(gathered)
    strip, hot, hot_back = lax.optimization_barrier((strip, hot, hot_back))

    wide = (CH, WIN)
    history = [(16, WIN), wide, wide, wide, wide]
    inputs, source, gate_one, gate_two, last, window, final = call(
        forward_kernel,
        [((STEPS,) + shape, BF) for shape in history] + [((16, WIN), F32), ((16, WIN), F32)],
        scratch=[
            pltpu.VMEM((24, WIN), F32),
            pltpu.VMEM((16, WIN), F32),
            pltpu.VMEM((K * CH, WIN), BF),
            pltpu.VMEM((K * CH, WIN), BF),
            pltpu.VMEM((4, 16, WIN), BF),
            pltpu.VMEM((8, WIN), F32),
            pltpu.VMEM((CH, WIN), F32),
        ],
        in_specs=[smem()] + [vmem()] * 5,
    )(ids, features, strip, lift, flat, head)

    other_final = lax.ppermute(final, BOTH, partner)
    next_state, flux_grad, flux_strip, *ocean_parts = call(
        functools.partial(ocean_kernel, scale),
        [
            ((8, CELLS), F32),
            ((8, WIN), F32),
            ((8, CELLS), F32),
            ((2, K * CH, CELLS), BF),
            ((2, CH, CELLS), BF),
            ((2, 16, CELLS), BF),
            ((2, CH, CELLS), BF),
        ],
        scratch=[pltpu.VMEM((CH, K * CELLS), BF)],
        in_specs=[smem()] + [vmem()] * 11,
    )(
        ids, gathered, final, other_final, hot, hot_back, ocean_lift, ocean_flat, ocean_head,
        ocean_lift_back, ocean_back, ocean_head_back,
    )
    flux_strip = lax.ppermute(flux_strip, BOTH, beside)
    (ocean_wire,) = call(
        ocean_weight_kernel, [((160, LON), BF)], in_specs=[smem()] + [vmem()] * 4
    )(ids, *ocean_parts)

    (wire,) = call(
        functools.partial(backward_kernel, scale),
        [((WIRE, LON), BF)],
        scratch=[
            pltpu.VMEM((16, WIN), F32),
            pltpu.VMEM((8, WIN), F32),
            pltpu.VMEM((7 * CH, 3 * CH), F32),
            pltpu.VMEM((16, LON), F32),
            pltpu.VMEM((2, 7 * CH, WIN), BF),
            pltpu.VMEM((2, 7 * CH, WIN), BF),
            pltpu.VMEM((3 * CH, WIN), BF),
            pltpu.VMEM((3 * CH, WIN), BF),
            pltpu.VMEM((CH, WIN), F32),
        ],
        in_specs=[smem()] + [vmem()] * 12,
    )(
        ids, window, flux_grad, flux_strip, ocean_wire, back, head_back, lift_back,
        inputs, source, gate_one, gate_two, last,
    )

    parts = lax.all_to_all(wire.reshape(sectors, rows, LON), "tile", 0, 0, tiled=True)
    (sums,) = call(
        functools.partial(sum_kernel, sectors, 2 * sectors), [((2 * sectors, rows, LON), BF)]
    )(parts)
    sums = lax.all_to_all(sums, ("high", "tile"), 0, 0, tiled=True)
    other_sums = lax.ppermute(sums, "core", [(0, 1), (1, 0)])
    totals = call(
        functools.partial(final_kernel, sectors, rows),
        [
            ((10, CH), F32),
            ((2, K, CH, CH), F32),
            ((12, CH), F32),
            ((12, CH), F32),
            ((2, K, CH, CH), F32),
            ((8, CH), F32),
        ],
        in_specs=[smem(), vmem(), vmem()],
    )(ids, sums, other_sums)
    g_lift, g_conv, g_head, o_lift, o_conv, o_head = totals
    return (next_state[None, None], g_lift.T, g_conv, g_head, o_lift.T, o_conv, o_head)


def solution(mesh):
    high, sectors = mesh.devices.shape[0] // 2, mesh.devices.shape[1]
    split = Mesh(mesh.devices.reshape(high, 2, sectors), BOTH)
    block = P(GROUP, "tile", None, None)
    return jax.shard_map(
        shards,
        mesh=split,
        in_specs=(block, block, block, P(None, "tile", None), P(), P(), P(), P(), P(), P()),
        out_specs=(block, P(), P(), P(), P(), P(), P()),
        check_vma=False,
    )
```

```python
import functools
import math

import jax
import jax.numpy as jnp
from jax import lax
from jax.experimental import pallas as pl
from jax.experimental.pallas import tpu as pltpu
from jax.sharding import Mesh
from jax.sharding import PartitionSpec as P

STEPS = 8
LON = 128
ROWS = 9
CELLS = 384
WIN = ROWS * LON
K = 9
CH = 64
HALO = 32
WIRE = 512
GROUP = ("high", "core")
BOTH = ("high", "core", "tile")
BF = jnp.bfloat16
F32 = jnp.float32
INTERPRET = False
VMEM_LIMIT = 24 * 1024 * 1024
WHOLE_VMEM = 62 * 1024 * 1024
BACK = (
    ((0, 1), (1, 1), (2, 1), (5, 1), (6, 1), (7, 1), (8, 1)),
    ((3, 1), (5, 1), (7, 1), (5, -1), None, (7, -1), None),
    ((4, 1), (6, 1), (8, 1), None, (6, -1), None, (8, -1)),
)

NN = (((1,), (0,)), ((), ()))
NT = (((1,), (1,)), ((), ()))


def dot(a, b, dims=NN):
    return lax.dot_general(a, b, dims, preferred_element_type=F32)


def call(body, outs, scratch=(), in_specs=None, limit=VMEM_LIMIT):
    extra = {}
    if in_specs is not None:
        extra = {"in_specs": in_specs, "out_specs": [vmem()] * len(outs)}
    return pl.pallas_call(
        body,
        out_shape=[jax.ShapeDtypeStruct(shape, dtype) for shape, dtype in outs],
        scratch_shapes=list(scratch),
        interpret=INTERPRET,
        compiler_params=pltpu.CompilerParams(vmem_limit_bytes=limit),
        **extra,
    )


def smem():
    return pl.BlockSpec(memory_space=pltpu.SMEM)


def hbm():
    return pl.BlockSpec(memory_space=pltpu.HBM)


def vmem():
    return pl.BlockSpec(memory_space=pltpu.VMEM)


def lane_ids(shape):
    return lax.broadcasted_iota(jnp.int32, shape, len(shape) - 1)


def sigmoid(value):
    return 0.5 * jnp.tanh(0.5 * value) + 0.5


def seg(row):
    return slice(row * LON, (row + 1) * LON)


def pack_strip(read, half, shape):
    start = jnp.where(half == 0, 0, LON - HALO)
    quarter = lane_ids(shape) // HALO
    packed = []
    for block in range(3):
        total = jnp.zeros(shape, F32)
        for place in range(4):
            row = 4 * block + place
            if row < ROWS:
                moved = pltpu.roll(read(row), lax.rem(HALO * place - start + 2 * LON, LON), 1)
                total = jnp.where(quarter == place, moved, total)
        packed.append(total)
    return packed


def to_window(own, strip, row, half):
    place = row % 4
    lanes = lane_ids(own.shape)
    target = jnp.where(half == 0, LON - HALO, 0)
    moved = pltpu.roll(strip, lax.rem(target - HALO * place + 2 * LON, LON), 1)
    outside = (lanes >= target) & (lanes < target + HALO)
    merged = jnp.where(outside, moved, own)
    return pltpu.roll(merged, jnp.where(half == 0, HALO, LON - HALO), 1)


def pack_kernel(
    ids, state, cotangent, table, sea, atm_lift, atm_head, ocn_lift, ocn_head,
    out, held, held_sea, near_one, near_two, near_three, near_four, done,
):
    near = (near_one, near_two, near_three, near_four)
    pairs = [(state, out.at[0:8]), (cotangent, out.at[8:16]), (table, held), (sea, held_sea)]
    pairs += list(zip((atm_lift, atm_head, ocn_lift, ocn_head), near))
    copies = [pltpu.make_async_copy(a, b, done.at[i]) for i, (a, b) in enumerate(pairs)]
    for copy in copies:
        copy.start()
    for copy in copies:
        copy.wait()
    small = [to_sixteen(ref[...]) for ref in near]
    small = jnp.concatenate(small + [jnp.zeros((16, LON), F32)], axis=1)
    share = small[0:4]
    for place in range(1, 4):
        share = jnp.where(ids[0] == place, small[4 * place : 4 * place + 4], share)
    rows = [held[k].astype(F32) for k in range(K)]
    rows.append(jnp.concatenate([held_sea[cycle] for cycle in range(3)], axis=1).astype(F32))
    rows += [share, jnp.zeros((2, CELLS), F32)]
    out[16:32, :] = jnp.concatenate(rows, axis=0)


def turned(value):
    return jnp.transpose(value.astype(F32)).astype(BF)


def to_sixteen(value):
    zeros = jnp.zeros((16 - value.shape[0], value.shape[1]), F32)
    return jnp.concatenate([value.astype(F32), zeros], axis=0)


def weights_kernel(
    gathered, atm_conv, ocn_conv,
    lift, lift_back, head, head_back, flat, back,
    ocean_lift, ocean_lift_back, ocean_head, ocean_head_back, ocean_flat, ocean_back,
):
    small = jnp.concatenate([gathered[group, 26:30, :] for group in range(4)], axis=0)
    lift[...] = turned(small[:, 0:64])
    head_back[...] = turned(small[:, 64:128])
    row_ids = lax.broadcasted_iota(jnp.int32, (16, CH), 0)
    fields = jnp.where(row_ids < 8, small[:, 64:128], 0.0).astype(BF)
    mixed = dot(turned(small[:, 0:64]), fields)
    head[...] = jnp.concatenate([small[:, 64:128], mixed], axis=0).astype(BF)
    lift_back[...] = jnp.concatenate([small[:, 0:64], jnp.transpose(mixed)], axis=0).astype(BF)
    ocean_lift_back[...] = small[:, 128:192].astype(BF)
    ocean_lift[...] = turned(small[:, 128:192])
    ocean_head[...] = small[:, 192:256].astype(BF)
    ocean_head_back[...] = turned(small[:, 192:256])
    for index in range(2):
        blocks = [atm_conv[index, k] for k in range(K)]
        flat[index] = jnp.concatenate(blocks, axis=1)
        if index == 0:
            folded = [dot(block, mixed.astype(BF)) for block in blocks]
            flat[2] = jnp.concatenate(folded, axis=1).astype(BF)
        blocks = [turned(block) for block in blocks]
        for side, terms in enumerate(BACK):
            parts = [
                jnp.zeros((CH, CH), BF) if term is None else blocks[term[0]] * term[1]
                for term in terms
            ]
            back[index, side * CH : (side + 1) * CH, :] = jnp.concatenate(parts, axis=1)
        blocks = [ocn_conv[index, k] for k in range(K)]
        ocean_flat[index] = jnp.concatenate(blocks, axis=1)
        for k in range(K):
            ocean_back[index, k * CH : (k + 1) * CH, :] = turned(blocks[k])


def hot_kernel(gathered, hot, hot_back, hot_sea):
    for cycle in range(3):
        hot_sea[cycle] = one_hot_sea(sea_row(gathered, cycle))
    table = gathered[3, 16:32, :]
    columns = jnp.transpose(table).astype(jnp.int32)
    table = table.astype(jnp.int32)
    cell_rows = lax.broadcasted_iota(jnp.int32, (CELLS, CELLS), 0)
    cell_lanes = lane_ids((CELLS, CELLS))
    for k in range(K):
        place = slice(k * CELLS, (k + 1) * CELLS)
        hot[k] = jnp.where(cell_rows == table[k : k + 1], 1.0, 0.0).astype(BF)
        target = columns[:, k : k + 1]
        hot_back[place, :] = jnp.where(cell_lanes == target, 1.0, 0.0).astype(BF)


def one_hot_sea(row):
    cells = lax.broadcasted_iota(jnp.int32, (CELLS, LON), 0)
    return jnp.where(cells == row, 1.0, 0.0).astype(BF)


def sea_row(gathered, cycle):
    return gathered[3, 25:26, cycle * LON : (cycle + 1) * LON].astype(jnp.int32)


def sector_kernel(ids, gathered, features, strip):
    half = ids[0] % 2
    for cycle in range(3):
        cols = slice(cycle * CELLS, (cycle + 1) * CELLS)
        features[0:16, cols] = gathered[cycle, 0:16, :]
        warm = gathered[3, 0:8, cycle * LON : (cycle + 1) * LON]
        row_ids = lax.broadcasted_iota(jnp.int32, (8, LON), 0)
        sources = jnp.where(row_ids == 0, warm[0:1], jnp.where(row_ids == 1, 1.0, 0.0))
        sources = jnp.concatenate([sources, jnp.zeros((8, LON), F32)], axis=0).astype(BF)
        placed = dot(sources, one_hot_sea(sea_row(gathered, cycle)), NT)[0:8]
        features[16:24, cols] = placed
        table = gathered[cycle, 16:32, :]
        features[18:20, cols] = jnp.where(table[5:7] == table[1:2], 1.0, 0.0)
        features[20:22, cols] = jnp.where(table[7:9] == table[2:3], 1.0, 0.0)
    packed = pack_strip(lambda row: features[:, seg(row)], half, (24, LON))
    for block in range(3):
        strip[:, seg(block)] = packed[block]


def pick(mask, chosen, other):
    shape = (CH // 16, 16, LON)
    result = jnp.where(mask[None], chosen.reshape(shape), other.reshape(shape))
    return result.reshape(CH, LON)


def shifted(piece):
    mid = piece.astype(BF)
    return mid, pltpu.roll(mid, 1, 1), pltpu.roll(mid, LON - 1, 1)


def build_columns(out, rows, flags):
    for row in range(ROWS):
        mid, west, east = shifted(rows[row])
        places = [(0, row, mid), (3, row, west), (4, row, east)]
        for cell, straight, first in ((row + 1, 1, 5), (row - 1, 2, 7)):
            if 0 <= cell < ROWS:
                places.append((straight, cell, mid))
                for side, k in ((west, first), (east, first + 1)):
                    flag = flags[k - 5, :, seg(cell)] > 0.5
                    places.append((k, cell, pick(flag, mid, side)))
        for k, cell, value in places:
            out[k * CH : (k + 1) * CH, seg(cell)] = value


def build_back(out, at, rows, flags):
    mid = [piece.astype(BF) for piece in rows]
    zero = jnp.zeros((CH, LON), BF)
    for row in range(ROWS):
        blocks = {0: mid[row]}
        for source, straight, first in ((row + 1, 1, 0), (row - 1, 2, 2)):
            if 0 <= source < ROWS:
                blocks[straight] = mid[source]
                for j in (first, first + 1):
                    flag = flags[j : j + 1, seg(source)] > 0.5
                    blocks[3 + j] = jnp.where(flag, mid[source], zero)
        for j, value in blocks.items():
            out[at, j * CH : (j + 1) * CH, seg(row)] = value


def join_sides(value):
    rows = []
    for row in range(ROWS):
        here = value[0:CH, seg(row)]
        west = pltpu.roll(value[CH : 2 * CH, seg(row)], LON - 1, 1)
        east = pltpu.roll(value[2 * CH : 3 * CH, seg(row)], 1, 1)
        rows.append(here + west + east)
    return rows


def split_rows(value):
    return [value[:, seg(row)] for row in range(ROWS)]


def keep_owned(value):
    lanes = lane_ids(value.shape) % LON
    return jnp.where((lanes >= HALO) & (lanes < LON - HALO), value, jnp.zeros_like(value))


def forward_kernel(
    ids, features, strip, lift, flat, head,
    inputs_out, source_out, gate_one, gate_two, last_out, window_out, final_out,
    window, total, columns, columns_two, flags, surface, lifted_total, pre_total,
):
    half = ids[0] % 2
    first = ids[0] // 2 == 0

    for row in range(ROWS):
        block = row // 4
        window[:, seg(row)] = to_window(features[:, seg(row)], strip[:, seg(block)], row, half)
    total[0:8, :] = window[0:8, :]
    total[8:16, :] = jnp.zeros((8, WIN), F32)
    window_out[...] = window[8:24, :]
    for j in range(4):
        flags[j] = jnp.broadcast_to(window[18 + j : 19 + j, :], (16, WIN)).astype(BF)
    for held in (columns, columns_two):
        for row, blocks in ((0, (1, 5, 6)), (ROWS - 1, (2, 7, 8))):
            for k in blocks:
                held[k * CH : (k + 1) * CH, seg(row)] = jnp.zeros((CH, LON), BF)

    row_ids = lax.broadcasted_iota(jnp.int32, (8, WIN), 0)
    surface[...] = jnp.where(row_ids < 2, window[16:24, :], 0.0)
    inputs = jnp.concatenate([total[0:8, :], surface[...]], axis=0)
    lifted_total[...] = dot(lift[...], inputs.astype(BF))

    for at in range(STEPS):
        inputs = jnp.concatenate([total[0:8, :], surface[...]], axis=0)
        inputs_out[at] = keep_owned(inputs).astype(BF)
        lifted = lifted_total[...]
        if at == 0:
            build_columns(columns, split_rows(lifted), flags)
            pre = dot(flat[0], columns[...])
        else:
            build_columns(columns, split_rows(hidden), flags)
            pre = pre_total[...] + dot(flat[2], columns[...])
        pre_total[...] = pre
        gate = sigmoid(pre)
        hidden = pre * gate
        gate_one[at] = (gate + hidden - hidden * gate).astype(BF)
        source_out[at] = jnp.where(first, lifted.astype(BF), hidden.astype(BF))
        build_columns(columns_two, [hidden[:, seg(row)] for row in range(ROWS)], flags)
        pre = dot(flat[1], columns_two[...])
        gate = sigmoid(pre)
        hidden = pre * gate
        gate_two[at] = (gate + hidden - hidden * gate).astype(BF)
        hidden = hidden.astype(BF)
        last_out[at] = hidden
        change = dot(head[...], hidden)
        total[...] += change[0:16]
        lifted_total[...] += change[16:]

    for row in range(ROWS):
        shift = jnp.where(half == 0, LON - HALO, HALO)
        final_out[:, seg(row)] = pltpu.roll(total[:, seg(row)], shift, 1)


def join_halves(half, own, other):
    lanes = lane_ids(own.shape)
    return jnp.where(((lanes % LON) // (LON // 2)) == half, own, other)


def ocean_kernel(
    scale, ids, gathered, own, other, hot, hot_back, hot_sea,
    lift, flat, lift_back, flat_back, head_back,
    flux_grad, strip, columns, slopes, sixteen, wide,
    scatter,
):
    half = ids[0] % 2
    flux = join_halves(half, own[8:16, :], other[8:16, :])
    flux = (flux * (1.0 / STEPS)).astype(BF)
    flux = jnp.concatenate([flux, flux], axis=0)
    forcing = [
        dot(flux[:, cycle * CELLS : (cycle + 1) * CELLS], hot_sea[cycle])[0:8] for cycle in range(3)
    ]
    forcing = jnp.concatenate(forcing, axis=1)
    fields = gathered[3, 0:8, :]
    inputs = jnp.concatenate([fields, forcing], axis=0).astype(BF)

    def gather(at, value):
        for k in range(K):
            columns[at, k * CH : (k + 1) * CH, :] = dot(value, hot[k]).astype(BF)

    def spread(index, slope):
        parts = dot(flat_back[index], slope).astype(BF)
        for k in range(K):
            scatter[:, k * CELLS : (k + 1) * CELLS] = parts[k * CH : (k + 1) * CH]
        return dot(scatter[...], hot_back[...])

    lifted = dot(lift[...], inputs).astype(BF)
    gather(0, lifted)
    pre = dot(flat[0], columns[0])
    gate = sigmoid(pre)
    hidden = pre * gate
    slope_of_one = gate + hidden - hidden * gate
    gather(1, hidden.astype(BF))
    pre = dot(flat[1], columns[1])
    gate = sigmoid(pre)
    hidden = pre * gate
    slope_of_two = gate + hidden - hidden * gate
    hidden = hidden.astype(BF)

    head_grad = gathered[3, 8:16, :] * scale
    head_grad = jnp.concatenate([head_grad, jnp.zeros((8, CELLS), F32)], axis=0).astype(BF)
    slope_two = (dot(head_back[...], head_grad) * slope_of_two).astype(BF)
    slope_one = (spread(1, slope_two) * slope_of_one).astype(BF)
    grad_lifted = spread(0, slope_one).astype(BF)
    forcing_grad = dot(lift_back[...], grad_lifted)[8:16]
    forcing_grad = (forcing_grad * (1.0 / STEPS)).astype(BF)
    forcing_grad = jnp.concatenate([forcing_grad, forcing_grad], axis=0)
    for cycle in range(3):
        part = forcing_grad[:, cycle * LON : (cycle + 1) * LON]
        flux_grad[:, cycle * CELLS : (cycle + 1) * CELLS] = dot(part, hot_sea[cycle], NT)[0:8]
    packed = pack_strip(lambda row: flux_grad[:, seg(row)], half, (8, LON))
    for place in range(3):
        strip[:, seg(place)] = packed[place]
    slopes[0] = slope_one
    slopes[1] = slope_two
    sixteen[0] = inputs
    sixteen[1] = head_grad
    wide[0] = grad_lifted
    wide[1] = hidden


def ocean_weight_kernel(
    ids, gathered, own, other, head, columns, slopes, sixteen, wide, next_state, wire
):
    group = ids[0]
    half = group % 2
    chosen = group // 2
    block = gathered[3, 0:8, :] + dot(head[...], wide[1])[0:8]
    for cycle in range(3):
        cols = slice(cycle * CELLS, (cycle + 1) * CELLS)
        merged = join_halves(half, own[0:8, cols], other[0:8, cols])
        block = jnp.where(group == cycle, merged, block)
    next_state[...] = block
    weight = jnp.transpose(dot(columns[chosen], slopes[chosen], NT))
    weight = jnp.where(half == 0, weight[0:32], weight[32:64])
    for j in range(4):
        wire[32 * j : 32 * j + 32, :] = weight[:, seg(j)].astype(BF)
    rest = weight[:, 512:576]
    wire[128:144, :] = jnp.concatenate([rest[0:16], rest[16:32]], axis=1).astype(BF)
    small = [dot(sixteen[index], wide[index], NT) for index in range(2)]
    wire[144:160, :] = jnp.concatenate(small, axis=1).astype(BF)


def backward_kernel(
    scale, ids, window, flux_own, flux_strip, ocean_wire, back, head_back, lift_back,
    inputs, source, gate_one, gate_two, last,
    wire,
    head_grad, flags, weight_total, small_total, taps_even, taps_odd, sources_even, sources_odd, grad_total,
):
    half = ids[0] % 2
    all_taps = (taps_even, taps_odd)
    all_sources = (sources_even, sources_odd)
    chosen = 1 - jnp.where(ids[0] // 2 == 0, 1, 0)

    head_grad[0:8, :] = window[0:8, :] * scale
    for row in range(ROWS):
        place = row // 4
        head_grad[8:16, seg(row)] = to_window(
            flux_own[:, seg(row)], flux_strip[:, seg(place)], row, half
        )
    flags[0:4, :] = window[10:14, :]
    for taps in all_taps:
        for row, blocks in ((ROWS - 1, (1, 3, 4)), (0, (2, 5, 6))):
            for j in blocks:
                for at in range(2):
                    taps[at, j * CH : (j + 1) * CH, seg(row)] = jnp.zeros((CH, LON), BF)
    grad_total[...] = dot(head_back[...], head_grad[...].astype(BF))
    weight_total[...] = jnp.zeros_like(weight_total)
    small_total[...] = jnp.zeros_like(small_total)

    for at in reversed(range(STEPS)):
        taps = all_taps[at % 2]
        sources = all_sources[at % 2]
        for row in range(ROWS):
            mid = source[at, :, seg(row)]
            for place, value in enumerate((pltpu.roll(mid, 1, 1), mid, pltpu.roll(mid, LON - 1, 1))):
                sources[place * CH : (place + 1) * CH, seg(row)] = keep_owned(value)
        grad = head_grad[...].astype(BF)
        slope_two = grad_total[...] * gate_two[at].astype(F32)
        build_back(taps, 1, split_rows(slope_two), flags)
        grad_one = join_sides(dot(back[1], taps[1]))
        slope_one = [
            grad_one[row] * gate_one[at, :, seg(row)].astype(F32) for row in range(ROWS)
        ]
        build_back(taps, 0, slope_one, flags)
        grad_lifted = jnp.concatenate(join_sides(dot(back[0], taps[0])), axis=1).astype(BF)
        if at > 0:
            change = dot(lift_back[...], grad_lifted)
            grad_total[...] += change[16:]
            head_grad[0:8, :] += change[0:8]
        lift_weight = dot(inputs[at], grad_lifted, NT)
        head_weight = dot(keep_owned(grad), last[at], NT)
        small_total[...] += jnp.concatenate([lift_weight, head_weight], axis=1)
        weight_total[...] += dot(taps[chosen], sources[...], NT)

    def product(slope, side):
        rows = weight_total[slope * CH : (slope + 1) * CH, :]
        return rows[:, side * CH : (side + 1) * CH]

    blocks = [product(0, 1), product(1, 1), product(2, 1), product(0, 0), product(0, 2)]
    for j in range(4):
        straight, side = 1 + j // 2, 2 * (j % 2)
        turned_part = product(straight, side) - product(3 + j, side)
        blocks.append(product(3 + j, 1) + turned_part)
    for j in range(4):
        pair = jnp.concatenate(blocks[2 * j : 2 * j + 2], axis=1)
        wire[64 * j : 64 * j + 64, :] = pair.astype(BF)
    pair = jnp.concatenate([blocks[8][0:32], blocks[8][32:64]], axis=1)
    wire[256:288, :] = pair.astype(BF)
    wire[288:304, :] = small_total[...].astype(BF)
    wire[304:464, :] = ocean_wire[...]
    wire[464:512, :] = jnp.zeros((48, LON), BF)


def sum_kernel(sectors, devices, parts, out):
    total = parts[0].astype(F32)
    for sector in range(1, sectors):
        total = total + parts[sector].astype(F32)
    total = total.astype(BF)
    for place in range(devices):
        out[place] = total


def final_kernel(sectors, rows, ids, own, other, g_lift, g_conv, g_head, o_lift, o_conv, o_head):
    def piece(group, start):
        place = (group // 2) * sectors + start // rows
        at = slice(start % rows, start % rows + 16)
        value = jnp.where(ids[0] % 2 == group % 2, own[place, at, :], other[place, at, :])
        return value.astype(F32)

    def spread(out, index, j, at, value):
        out[index, 2 * j, at : at + 16, :] = value[:, 0:64]
        out[index, 2 * j + 1, at : at + 16, :] = value[:, 64:128]

    for index in range(2):
        low, high = 2 * index, 2 * index + 1
        for j in range(4):
            for at in range(0, 64, 16):
                start = 64 * j + at
                spread(g_conv, index, j, at, piece(low, start) + piece(high, start))
            for at in range(0, 32, 16):
                start = 304 + 32 * j + at
                spread(o_conv, index, j, at, piece(low, start))
                spread(o_conv, index, j, at + 32, piece(high, start))
        for at in range(0, 32, 16):
            pair = piece(low, 256 + at) + piece(high, 256 + at)
            g_conv[index, 8, at : at + 16, :] = pair[:, 0:64]
            g_conv[index, 8, at + 32 : at + 48, :] = pair[:, 64:128]
        for side, at in ((low, 0), (high, 32)):
            value = piece(side, 432)
            o_conv[index, 8, at : at + 16, :] = value[:, 0:64]
            o_conv[index, 8, at + 16 : at + 32, :] = value[:, 64:128]
    small = piece(0, 288) + piece(1, 288)
    g_lift[...] = small[0:10, 0:64]
    g_head[...] = small[0:12, 64:128]
    small = piece(0, 448)
    o_lift[...] = small[0:12, 0:64]
    o_head[...] = small[0:8, 64:128]


def shards(
    state,
    cotangent,
    neighbours,
    sea_cells,
    atm_lift,
    atm_conv,
    atm_head,
    ocn_lift,
    ocn_conv,
    ocn_head,
):
    sectors = lax.axis_size("tile")
    devices = 4 * sectors
    rows = WIRE // sectors
    scale = 1.0 / math.sqrt(devices * CELLS)
    group = 2 * lax.axis_index("high") + lax.axis_index("core")
    ids = group.astype(jnp.int32).reshape(1)

    partner = []
    beside = []
    for g in range(4):
        for t in range(sectors):
            partner.append((g * sectors + t, (g ^ 1) * sectors + t))
            other = (t + 1) % sectors if g % 2 else (t - 1) % sectors
            beside.append((g * sectors + t, (g ^ 1) * sectors + other))

    lifts = (atm_lift.T, atm_head, ocn_lift.T, ocn_head)
    (packed,) = call(
        pack_kernel,
        [((32, CELLS), F32)],
        scratch=[
            pltpu.VMEM((K, 1, CELLS), jnp.int32),
            pltpu.VMEM((3, 1, LON), jnp.int32),
        ]
        + [pltpu.VMEM(array.shape, BF) for array in lifts]
        + [pltpu.SemaphoreType.DMA((8,))],
        in_specs=[smem()] + [hbm()] * 8,
        limit=WHOLE_VMEM,
    )(ids, state[0, 0], cotangent[0, 0], neighbours.reshape(K, 1, CELLS), sea_cells, *lifts)
    gathered = lax.all_gather(packed, GROUP)
    features, strip = call(
        sector_kernel,
        [((24, WIN), F32), ((24, CELLS), F32)],
        in_specs=[smem(), vmem()],
    )(ids, gathered)
    strip = lax.ppermute(strip, BOTH, beside)

    weights = call(
        weights_kernel,
        [
            ((CH, 16), BF),
            ((16 + CH, CH), BF),
            ((16 + CH, CH), BF),
            ((CH, 16), BF),
            ((3, CH, K * CH), BF),
            ((2, 3 * CH, 7 * CH), BF),
            ((CH, 16), BF),
            ((16, CH), BF),
            ((16, CH), BF),
            ((CH, 16), BF),
            ((2, CH, K * CH), BF),
            ((2, K * CH, CH), BF),
        ],
    )(gathered, atm_conv, ocn_conv)
    lift, lift_back, head, head_back, flat, back = weights[:6]
    ocean_lift, ocean_lift_back, ocean_head, ocean_head_back, ocean_flat, ocean_back = weights[6:]

    hot, hot_back, hot_sea = call(hot_kernel, [((K, CELLS, CELLS), BF), ((K * CELLS, CELLS), BF), ((3, CELLS, LON), BF)])(gathered)
    strip, hot, hot_back, hot_sea = lax.optimization_barrier((strip, hot, hot_back, hot_sea))

    wide = (CH, WIN)
    history = [(16, WIN), wide, wide, wide, wide]
    inputs, source, gate_one, gate_two, last, window, final = call(
        forward_kernel,
        [((STEPS,) + shape, BF) for shape in history] + [((16, WIN), F32), ((16, WIN), F32)],
        scratch=[
            pltpu.VMEM((24, WIN), F32),
            pltpu.VMEM((16, WIN), F32),
            pltpu.VMEM((K * CH, WIN), BF),
            pltpu.VMEM((K * CH, WIN), BF),
            pltpu.VMEM((4, 16, WIN), BF),
            pltpu.VMEM((8, WIN), F32),
            pltpu.VMEM((CH, WIN), F32),
            pltpu.VMEM((CH, WIN), F32),
        ],
        in_specs=[smem()] + [vmem()] * 5,
    )(ids, features, strip, lift, flat, head)

    other_final = lax.ppermute(final, BOTH, partner)
    flux_grad, flux_strip, *ocean_parts = call(
        functools.partial(ocean_kernel, scale),
        [
            ((8, WIN), F32),
            ((8, CELLS), F32),
            ((2, K * CH, CELLS), BF),
            ((2, CH, CELLS), BF),
            ((2, 16, CELLS), BF),
            ((2, CH, CELLS), BF),
        ],
        scratch=[pltpu.VMEM((CH, K * CELLS), BF)],
        in_specs=[smem()] + [vmem()] * 11,
    )(
        ids, gathered, final, other_final, hot, hot_back, hot_sea, ocean_lift, ocean_flat,
        ocean_lift_back, ocean_back, ocean_head_back,
    )
    flux_strip = lax.ppermute(flux_strip, BOTH, beside)
    next_state, ocean_wire = call(
        ocean_weight_kernel,
        [((8, CELLS), F32), ((160, LON), BF)],
        in_specs=[smem()] + [vmem()] * 8,
    )(ids, gathered, final, other_final, ocean_head, *ocean_parts)

    (wire,) = call(
        functools.partial(backward_kernel, scale),
        [((WIRE, LON), BF)],
        scratch=[
            pltpu.VMEM((16, WIN), F32),
            pltpu.VMEM((8, WIN), F32),
            pltpu.VMEM((7 * CH, 3 * CH), F32),
            pltpu.VMEM((16, LON), F32),
            pltpu.VMEM((2, 7 * CH, WIN), BF),
            pltpu.VMEM((2, 7 * CH, WIN), BF),
            pltpu.VMEM((3 * CH, WIN), BF),
            pltpu.VMEM((3 * CH, WIN), BF),
            pltpu.VMEM((CH, WIN), F32),
        ],
        in_specs=[smem()] + [vmem()] * 12,
    )(
        ids, window, flux_grad, flux_strip, ocean_wire, back, head_back, lift_back,
        inputs, source, gate_one, gate_two, last,
    )

    parts = lax.all_to_all(wire.reshape(sectors, rows, LON), "tile", 0, 0, tiled=True)
    (sums,) = call(
        functools.partial(sum_kernel, sectors, 2 * sectors), [((2 * sectors, rows, LON), BF)]
    )(parts)
    sums = lax.all_to_all(sums, ("high", "tile"), 0, 0, tiled=True)
    other_sums = lax.ppermute(sums, "core", [(0, 1), (1, 0)])
    totals = call(
        functools.partial(final_kernel, sectors, rows),
        [
            ((10, CH), F32),
            ((2, K, CH, CH), F32),
            ((12, CH), F32),
            ((12, CH), F32),
            ((2, K, CH, CH), F32),
            ((8, CH), F32),
        ],
        in_specs=[smem(), vmem(), vmem()],
    )(ids, sums, other_sums)
    g_lift, g_conv, g_head, o_lift, o_conv, o_head = totals
    return (next_state[None, None], g_lift.T, g_conv, g_head, o_lift.T, o_conv, o_head)


def solution(mesh):
    high, sectors = mesh.devices.shape[0] // 2, mesh.devices.shape[1]
    split = Mesh(mesh.devices.reshape(high, 2, sectors), BOTH)
    block = P(GROUP, "tile", None, None)
    return jax.shard_map(
        shards,
        mesh=split,
        in_specs=(block, block, block, P(None, "tile", None), P(), P(), P(), P(), P(), P()),
        out_specs=(block, P(), P(), P(), P(), P(), P()),
        check_vma=False,
    )
```

```python
import functools
import math

import jax
import jax.numpy as jnp
from jax import lax
from jax.experimental import pallas as pl
from jax.experimental.pallas import tpu as pltpu
from jax.sharding import Mesh
from jax.sharding import PartitionSpec as P

STEPS = 8
LON = 128
ROWS = 9
CELLS = 384
WIN = ROWS * LON
K = 9
CH = 64
HALO = 32
WIRE = 512
GROUP = ("high", "core")
BOTH = ("high", "core", "tile")
BF = jnp.bfloat16
F32 = jnp.float32
INTERPRET = False
VMEM_LIMIT = 24 * 1024 * 1024
WHOLE_VMEM = 62 * 1024 * 1024
BACK = (
    ((0, 1), (1, 1), (2, 1), (5, 1), (6, 1), (7, 1), (8, 1)),
    ((3, 1), (5, 1), (7, 1), (5, -1), None, (7, -1), None),
    ((4, 1), (6, 1), (8, 1), None, (6, -1), None, (8, -1)),
)

NN = (((1,), (0,)), ((), ()))
NT = (((1,), (1,)), ((), ()))


def dot(a, b, dims=NN):
    return lax.dot_general(a, b, dims, preferred_element_type=F32)


def call(body, outs, scratch=(), in_specs=None, limit=VMEM_LIMIT):
    extra = {}
    if in_specs is not None:
        extra = {"in_specs": in_specs, "out_specs": [vmem()] * len(outs)}
    return pl.pallas_call(
        body,
        out_shape=[jax.ShapeDtypeStruct(shape, dtype) for shape, dtype in outs],
        scratch_shapes=list(scratch),
        interpret=INTERPRET,
        compiler_params=pltpu.CompilerParams(vmem_limit_bytes=limit),
        **extra,
    )


def smem():
    return pl.BlockSpec(memory_space=pltpu.SMEM)


def hbm():
    return pl.BlockSpec(memory_space=pltpu.HBM)


def vmem():
    return pl.BlockSpec(memory_space=pltpu.VMEM)


def lane_ids(shape):
    return lax.broadcasted_iota(jnp.int32, shape, len(shape) - 1)


def sigmoid(value):
    return 0.5 * jnp.tanh(0.5 * value) + 0.5


def seg(row):
    return slice(row * LON, (row + 1) * LON)


def pack_strip(read, half, shape):
    start = jnp.where(half == 0, 0, LON - HALO)
    quarter = lane_ids(shape) // HALO
    packed = []
    for block in range(3):
        total = jnp.zeros(shape, F32)
        for place in range(4):
            row = 4 * block + place
            if row < ROWS:
                moved = pltpu.roll(read(row), lax.rem(HALO * place - start + 2 * LON, LON), 1)
                total = jnp.where(quarter == place, moved, total)
        packed.append(total)
    return packed


def to_window(own, strip, row, half):
    place = row % 4
    lanes = lane_ids(own.shape)
    target = jnp.where(half == 0, LON - HALO, 0)
    moved = pltpu.roll(strip, lax.rem(target - HALO * place + 2 * LON, LON), 1)
    outside = (lanes >= target) & (lanes < target + HALO)
    merged = jnp.where(outside, moved, own)
    return pltpu.roll(merged, jnp.where(half == 0, HALO, LON - HALO), 1)


def pack_kernel(
    ids, state, cotangent, table, sea, atm_lift, atm_head, ocn_lift, ocn_head,
    out, held, held_sea, near_one, near_two, near_three, near_four, done,
):
    near = (near_one, near_two, near_three, near_four)
    pairs = [(state, out.at[0:8]), (cotangent, out.at[8:16]), (table, held), (sea, held_sea)]
    pairs += list(zip((atm_lift, atm_head, ocn_lift, ocn_head), near))
    copies = [pltpu.make_async_copy(a, b, done.at[i]) for i, (a, b) in enumerate(pairs)]
    for copy in copies:
        copy.start()
    for copy in copies:
        copy.wait()
    small = [to_sixteen(ref[...]) for ref in near]
    small = jnp.concatenate(small + [jnp.zeros((16, LON), F32)], axis=1)
    share = small[0:4]
    for place in range(1, 4):
        share = jnp.where(ids[0] == place, small[4 * place : 4 * place + 4], share)
    rows = [held[k].astype(F32) for k in range(K)]
    rows.append(jnp.concatenate([held_sea[cycle] for cycle in range(3)], axis=1).astype(F32))
    rows += [share, jnp.zeros((2, CELLS), F32)]
    out[16:32, :] = jnp.concatenate(rows, axis=0)


def turned(value):
    return jnp.transpose(value.astype(F32)).astype(BF)


def to_sixteen(value):
    zeros = jnp.zeros((16 - value.shape[0], value.shape[1]), F32)
    return jnp.concatenate([value.astype(F32), zeros], axis=0)


def weights_kernel(
    gathered, atm_conv, ocn_conv,
    lift, lift_back, head, head_back, flat, back,
    ocean_lift, ocean_lift_back, ocean_head, ocean_head_back, ocean_flat, ocean_back,
):
    small = jnp.concatenate([gathered[group, 26:30, :] for group in range(4)], axis=0)
    lift[...] = turned(small[:, 0:64])
    head_back[...] = turned(small[:, 64:128])
    row_ids = lax.broadcasted_iota(jnp.int32, (16, CH), 0)
    fields = jnp.where(row_ids < 8, small[:, 64:128], 0.0).astype(BF)
    mixed = dot(turned(small[:, 0:64]), fields)
    head[...] = jnp.concatenate([small[:, 64:128], mixed], axis=0).astype(BF)
    lift_back[...] = jnp.concatenate([small[:, 0:64], jnp.transpose(mixed)], axis=0).astype(BF)
    ocean_lift_back[...] = small[:, 128:192].astype(BF)
    ocean_lift[...] = turned(small[:, 128:192])
    ocean_head[...] = small[:, 192:256].astype(BF)
    ocean_head_back[...] = turned(small[:, 192:256])
    for index in range(2):
        blocks = [atm_conv[index, k] for k in range(K)]
        flat[index] = jnp.concatenate(blocks, axis=1)
        if index == 0:
            folded = [dot(block, mixed.astype(BF)) for block in blocks]
            flat[2] = jnp.concatenate(folded, axis=1).astype(BF)
        blocks = [turned(block) for block in blocks]
        for side, terms in enumerate(BACK):
            parts = [
                jnp.zeros((CH, CH), BF) if term is None else blocks[term[0]] * term[1]
                for term in terms
            ]
            back[index, side * CH : (side + 1) * CH, :] = jnp.concatenate(parts, axis=1)
        blocks = [ocn_conv[index, k] for k in range(K)]
        ocean_flat[index] = jnp.concatenate(blocks, axis=1)
        for k in range(K):
            ocean_back[index, k * CH : (k + 1) * CH, :] = turned(blocks[k])


def hot_kernel(gathered, hot, hot_back, hot_sea):
    for cycle in range(3):
        hot_sea[cycle] = one_hot_sea(sea_row(gathered, cycle))
    table = gathered[3, 16:32, :]
    columns = jnp.transpose(table).astype(jnp.int32)
    table = table.astype(jnp.int32)
    cell_rows = lax.broadcasted_iota(jnp.int32, (CELLS, CELLS), 0)
    cell_lanes = lane_ids((CELLS, CELLS))
    for k in range(K):
        place = slice(k * CELLS, (k + 1) * CELLS)
        hot[k] = jnp.where(cell_rows == table[k : k + 1], 1.0, 0.0).astype(BF)
        target = columns[:, k : k + 1]
        hot_back[place, :] = jnp.where(cell_lanes == target, 1.0, 0.0).astype(BF)


def one_hot_sea(row):
    cells = lax.broadcasted_iota(jnp.int32, (CELLS, LON), 0)
    return jnp.where(cells == row, 1.0, 0.0).astype(BF)


def sea_row(gathered, cycle):
    return gathered[3, 25:26, cycle * LON : (cycle + 1) * LON].astype(jnp.int32)


def sector_kernel(ids, gathered, features, strip):
    half = ids[0] % 2
    for cycle in range(3):
        cols = slice(cycle * CELLS, (cycle + 1) * CELLS)
        features[0:16, cols] = gathered[cycle, 0:16, :]
        warm = gathered[3, 0:8, cycle * LON : (cycle + 1) * LON]
        row_ids = lax.broadcasted_iota(jnp.int32, (8, LON), 0)
        sources = jnp.where(row_ids == 0, warm[0:1], jnp.where(row_ids == 1, 1.0, 0.0))
        sources = jnp.concatenate([sources, jnp.zeros((8, LON), F32)], axis=0).astype(BF)
        placed = dot(sources, one_hot_sea(sea_row(gathered, cycle)), NT)[0:8]
        features[16:24, cols] = placed
        table = gathered[cycle, 16:32, :]
        features[18:20, cols] = jnp.where(table[5:7] == table[1:2], 1.0, 0.0)
        features[20:22, cols] = jnp.where(table[7:9] == table[2:3], 1.0, 0.0)
    packed = pack_strip(lambda row: features[:, seg(row)], half, (24, LON))
    for block in range(3):
        strip[:, seg(block)] = packed[block]


def pick(mask, chosen, other):
    shape = (CH // 16, 16, LON)
    result = jnp.where(mask[None], chosen.reshape(shape), other.reshape(shape))
    return result.reshape(CH, LON)


def shifted(piece):
    mid = piece.astype(BF)
    return mid, pltpu.roll(mid, 1, 1), pltpu.roll(mid, LON - 1, 1)


def build_columns(out, rows, flags):
    for row in range(ROWS):
        mid, west, east = shifted(rows[row])
        places = [(0, row, mid), (3, row, west), (4, row, east)]
        for cell, straight, first in ((row + 1, 1, 5), (row - 1, 2, 7)):
            if 0 <= cell < ROWS:
                places.append((straight, cell, mid))
                for side, k in ((west, first), (east, first + 1)):
                    flag = flags[k - 5, :, seg(cell)] > 0.5
                    places.append((k, cell, pick(flag, mid, side)))
        for k, cell, value in places:
            out[k * CH : (k + 1) * CH, seg(cell)] = value


def build_back(out, at, rows, flags):
    mid = [piece.astype(BF) for piece in rows]
    zero = jnp.zeros((CH, LON), BF)
    for row in range(ROWS):
        blocks = {0: mid[row]}
        for source, straight, first in ((row + 1, 1, 0), (row - 1, 2, 2)):
            if 0 <= source < ROWS:
                blocks[straight] = mid[source]
                for j in (first, first + 1):
                    flag = flags[j : j + 1, seg(source)] > 0.5
                    blocks[3 + j] = jnp.where(flag, mid[source], zero)
        for j, value in blocks.items():
            out[at, j * CH : (j + 1) * CH, seg(row)] = value


def join_sides(value):
    rows = []
    for row in range(ROWS):
        here = value[0:CH, seg(row)]
        west = pltpu.roll(value[CH : 2 * CH, seg(row)], LON - 1, 1)
        east = pltpu.roll(value[2 * CH : 3 * CH, seg(row)], 1, 1)
        rows.append(here + west + east)
    return rows


def split_rows(value):
    return [value[:, seg(row)] for row in range(ROWS)]


def keep_owned(value):
    lanes = lane_ids(value.shape) % LON
    return jnp.where((lanes >= HALO) & (lanes < LON - HALO), value, jnp.zeros_like(value))


def forward_kernel(
    ids, features, strip, lift, flat, head,
    inputs_out, source_out, gate_one, gate_two, last_out, window_out, final_out,
    window, total, columns, columns_two, flags, surface, lifted_total, pre_total,
):
    half = ids[0] % 2
    first = ids[0] // 2 == 0

    for row in range(ROWS):
        block = row // 4
        window[:, seg(row)] = to_window(features[:, seg(row)], strip[:, seg(block)], row, half)
    total[0:8, :] = window[0:8, :]
    total[8:16, :] = jnp.zeros((8, WIN), F32)
    window_out[...] = window[8:24, :]
    for j in range(4):
        flags[j] = jnp.broadcast_to(window[18 + j : 19 + j, :], (16, WIN)).astype(BF)
    for held in (columns, columns_two):
        for row, blocks in ((0, (1, 5, 6)), (ROWS - 1, (2, 7, 8))):
            for k in blocks:
                held[k * CH : (k + 1) * CH, seg(row)] = jnp.zeros((CH, LON), BF)

    row_ids = lax.broadcasted_iota(jnp.int32, (8, WIN), 0)
    surface[...] = jnp.where(row_ids < 2, window[16:24, :], 0.0)
    inputs = jnp.concatenate([total[0:8, :], surface[...]], axis=0)
    lifted_total[...] = dot(lift[...], inputs.astype(BF))

    for at in range(STEPS):
        inputs = jnp.concatenate([total[0:8, :], surface[...]], axis=0)
        inputs_out[at] = keep_owned(inputs).astype(BF)
        lifted = lifted_total[...]
        if at == 0:
            build_columns(columns, split_rows(lifted), flags)
            pre = dot(flat[0], columns[...])
        else:
            build_columns(columns, split_rows(hidden), flags)
            pre = pre_total[...] + dot(flat[2], columns[...])
        pre_total[...] = pre
        gate = sigmoid(pre)
        hidden = pre * gate
        gate_one[at] = (gate + hidden - hidden * gate).astype(BF)
        source_out[at] = jnp.where(first, lifted.astype(BF), hidden.astype(BF))
        build_columns(columns_two, [hidden[:, seg(row)] for row in range(ROWS)], flags)
        pre = dot(flat[1], columns_two[...])
        gate = sigmoid(pre)
        hidden = pre * gate
        gate_two[at] = (gate + hidden - hidden * gate).astype(BF)
        hidden = hidden.astype(BF)
        last_out[at] = hidden
        change = dot(head[...], hidden)
        total[...] += change[0:16]
        lifted_total[...] += change[16:]

    for row in range(ROWS):
        shift = jnp.where(half == 0, LON - HALO, HALO)
        final_out[:, seg(row)] = pltpu.roll(total[:, seg(row)], shift, 1)


def join_halves(half, own, other):
    lanes = lane_ids(own.shape)
    return jnp.where(((lanes % LON) // (LON // 2)) == half, own, other)


def ocean_kernel(
    scale, ids, gathered, own, other, hot, hot_back, hot_sea,
    lift, flat, lift_back, flat_back, head_back,
    flux_grad, strip, columns, slopes, sixteen, wide,
    scatter,
):
    half = ids[0] % 2
    flux = join_halves(half, own[8:16, :], other[8:16, :])
    flux = (flux * (1.0 / STEPS)).astype(BF)
    flux = jnp.concatenate([flux, flux], axis=0)
    forcing = [
        dot(flux[:, cycle * CELLS : (cycle + 1) * CELLS], hot_sea[cycle])[0:8] for cycle in range(3)
    ]
    forcing = jnp.concatenate(forcing, axis=1)
    fields = gathered[3, 0:8, :]
    inputs = jnp.concatenate([fields, forcing], axis=0).astype(BF)

    def gather(at, value):
        for k in range(K):
            columns[at, k * CH : (k + 1) * CH, :] = dot(value, hot[k]).astype(BF)

    def spread(index, slope):
        parts = dot(flat_back[index], slope).astype(BF)
        for k in range(K):
            scatter[:, k * CELLS : (k + 1) * CELLS] = parts[k * CH : (k + 1) * CH]
        return dot(scatter[...], hot_back[...])

    lifted = dot(lift[...], inputs).astype(BF)
    gather(0, lifted)
    pre = dot(flat[0], columns[0])
    gate = sigmoid(pre)
    hidden = pre * gate
    slope_of_one = gate + hidden - hidden * gate
    gather(1, hidden.astype(BF))
    pre = dot(flat[1], columns[1])
    gate = sigmoid(pre)
    hidden = pre * gate
    slope_of_two = gate + hidden - hidden * gate
    hidden = hidden.astype(BF)

    head_grad = gathered[3, 8:16, :] * scale
    head_grad = jnp.concatenate([head_grad, jnp.zeros((8, CELLS), F32)], axis=0).astype(BF)
    slope_two = (dot(head_back[...], head_grad) * slope_of_two).astype(BF)
    slope_one = (spread(1, slope_two) * slope_of_one).astype(BF)
    grad_lifted = spread(0, slope_one).astype(BF)
    forcing_grad = dot(lift_back[...], grad_lifted)[8:16]
    forcing_grad = (forcing_grad * (1.0 / STEPS)).astype(BF)
    forcing_grad = jnp.concatenate([forcing_grad, forcing_grad], axis=0)
    for cycle in range(3):
        part = forcing_grad[:, cycle * LON : (cycle + 1) * LON]
        flux_grad[:, cycle * CELLS : (cycle + 1) * CELLS] = dot(part, hot_sea[cycle], NT)[0:8]
    packed = pack_strip(lambda row: flux_grad[:, seg(row)], half, (8, LON))
    for place in range(3):
        strip[:, seg(place)] = packed[place]
    slopes[0] = slope_one
    slopes[1] = slope_two
    sixteen[0] = inputs
    sixteen[1] = head_grad
    wide[0] = grad_lifted
    wide[1] = hidden


def source_kernel(source, sources):
    for at in range(STEPS):
        for row in range(ROWS):
            mid = source[at, :, seg(row)]
            sides = (pltpu.roll(mid, 1, 1), mid, pltpu.roll(mid, LON - 1, 1))
            for place, value in enumerate(sides):
                sources[at, place * CH : (place + 1) * CH, seg(row)] = keep_owned(value)


def ocean_weight_kernel(
    ids, gathered, own, other, head, columns, slopes, sixteen, wide, next_state, wire
):
    group = ids[0]
    half = group % 2
    chosen = group // 2
    block = gathered[3, 0:8, :] + dot(head[...], wide[1])[0:8]
    for cycle in range(3):
        cols = slice(cycle * CELLS, (cycle + 1) * CELLS)
        merged = join_halves(half, own[0:8, cols], other[0:8, cols])
        block = jnp.where(group == cycle, merged, block)
    next_state[...] = block
    weight = jnp.transpose(dot(columns[chosen], slopes[chosen], NT))
    weight = jnp.where(half == 0, weight[0:32], weight[32:64])
    for j in range(4):
        wire[32 * j : 32 * j + 32, :] = weight[:, seg(j)].astype(BF)
    rest = weight[:, 512:576]
    wire[128:144, :] = jnp.concatenate([rest[0:16], rest[16:32]], axis=1).astype(BF)
    small = [dot(sixteen[index], wide[index], NT) for index in range(2)]
    wire[144:160, :] = jnp.concatenate(small, axis=1).astype(BF)


def backward_kernel(
    scale, ids, window, flux_own, flux_strip, ocean_wire, back, head_back, lift_back,
    inputs, source, gate_one, gate_two, last,
    wire,
    head_grad, flags, weight_total, small_total, taps_even, taps_odd, grad_total,
):
    half = ids[0] % 2
    all_taps = (taps_even, taps_odd)
    chosen = 1 - jnp.where(ids[0] // 2 == 0, 1, 0)

    head_grad[0:8, :] = window[0:8, :] * scale
    for row in range(ROWS):
        place = row // 4
        head_grad[8:16, seg(row)] = to_window(
            flux_own[:, seg(row)], flux_strip[:, seg(place)], row, half
        )
    flags[0:4, :] = window[10:14, :]
    for taps in all_taps:
        for row, blocks in ((ROWS - 1, (1, 3, 4)), (0, (2, 5, 6))):
            for j in blocks:
                for at in range(2):
                    taps[at, j * CH : (j + 1) * CH, seg(row)] = jnp.zeros((CH, LON), BF)
    grad_total[...] = dot(head_back[...], head_grad[...].astype(BF))
    weight_total[...] = jnp.zeros_like(weight_total)
    small_total[...] = jnp.zeros_like(small_total)

    for at in reversed(range(STEPS)):
        taps = all_taps[at % 2]
        grad = head_grad[...].astype(BF)
        slope_two = grad_total[...] * gate_two[at].astype(F32)
        build_back(taps, 1, split_rows(slope_two), flags)
        grad_one = join_sides(dot(back[1], taps[1]))
        slope_one = [
            grad_one[row] * gate_one[at, :, seg(row)].astype(F32) for row in range(ROWS)
        ]
        build_back(taps, 0, slope_one, flags)
        grad_lifted = jnp.concatenate(join_sides(dot(back[0], taps[0])), axis=1).astype(BF)
        if at > 0:
            change = dot(lift_back[...], grad_lifted)
            grad_total[...] += change[16:]
            head_grad[0:8, :] += change[0:8]
        lift_weight = dot(inputs[at], grad_lifted, NT)
        head_weight = dot(keep_owned(grad), last[at], NT)
        small_total[...] += jnp.concatenate([lift_weight, head_weight], axis=1)
        weight_total[...] += dot(taps[chosen], source[at], NT)

    def product(slope, side):
        rows = weight_total[slope * CH : (slope + 1) * CH, :]
        return rows[:, side * CH : (side + 1) * CH]

    blocks = [product(0, 1), product(1, 1), product(2, 1), product(0, 0), product(0, 2)]
    for j in range(4):
        straight, side = 1 + j // 2, 2 * (j % 2)
        turned_part = product(straight, side) - product(3 + j, side)
        blocks.append(product(3 + j, 1) + turned_part)
    for j in range(4):
        pair = jnp.concatenate(blocks[2 * j : 2 * j + 2], axis=1)
        wire[64 * j : 64 * j + 64, :] = pair.astype(BF)
    pair = jnp.concatenate([blocks[8][0:32], blocks[8][32:64]], axis=1)
    wire[256:288, :] = pair.astype(BF)
    wire[288:304, :] = small_total[...].astype(BF)
    wire[304:464, :] = ocean_wire[...]
    wire[464:512, :] = jnp.zeros((48, LON), BF)


def sum_kernel(sectors, devices, parts, out):
    total = parts[0].astype(F32)
    for sector in range(1, sectors):
        total = total + parts[sector].astype(F32)
    total = total.astype(BF)
    for place in range(devices):
        out[place] = total


def final_kernel(sectors, rows, ids, own, other, g_lift, g_conv, g_head, o_lift, o_conv, o_head):
    def piece(group, start):
        place = (group // 2) * sectors + start // rows
        at = slice(start % rows, start % rows + 16)
        value = jnp.where(ids[0] % 2 == group % 2, own[place, at, :], other[place, at, :])
        return value.astype(F32)

    def spread(out, index, j, at, value):
        out[index, 2 * j, at : at + 16, :] = value[:, 0:64]
        out[index, 2 * j + 1, at : at + 16, :] = value[:, 64:128]

    for index in range(2):
        low, high = 2 * index, 2 * index + 1
        for j in range(4):
            for at in range(0, 64, 16):
                start = 64 * j + at
                spread(g_conv, index, j, at, piece(low, start) + piece(high, start))
            for at in range(0, 32, 16):
                start = 304 + 32 * j + at
                spread(o_conv, index, j, at, piece(low, start))
                spread(o_conv, index, j, at + 32, piece(high, start))
        for at in range(0, 32, 16):
            pair = piece(low, 256 + at) + piece(high, 256 + at)
            g_conv[index, 8, at : at + 16, :] = pair[:, 0:64]
            g_conv[index, 8, at + 32 : at + 48, :] = pair[:, 64:128]
        for side, at in ((low, 0), (high, 32)):
            value = piece(side, 432)
            o_conv[index, 8, at : at + 16, :] = value[:, 0:64]
            o_conv[index, 8, at + 16 : at + 32, :] = value[:, 64:128]
    small = piece(0, 288) + piece(1, 288)
    g_lift[...] = small[0:10, 0:64]
    g_head[...] = small[0:12, 64:128]
    small = piece(0, 448)
    o_lift[...] = small[0:12, 0:64]
    o_head[...] = small[0:8, 64:128]


def shards(
    state,
    cotangent,
    neighbours,
    sea_cells,
    atm_lift,
    atm_conv,
    atm_head,
    ocn_lift,
    ocn_conv,
    ocn_head,
):
    sectors = lax.axis_size("tile")
    devices = 4 * sectors
    rows = WIRE // sectors
    scale = 1.0 / math.sqrt(devices * CELLS)
    group = 2 * lax.axis_index("high") + lax.axis_index("core")
    ids = group.astype(jnp.int32).reshape(1)

    partner = []
    beside = []
    for g in range(4):
        for t in range(sectors):
            partner.append((g * sectors + t, (g ^ 1) * sectors + t))
            other = (t + 1) % sectors if g % 2 else (t - 1) % sectors
            beside.append((g * sectors + t, (g ^ 1) * sectors + other))

    lifts = (atm_lift.T, atm_head, ocn_lift.T, ocn_head)
    (packed,) = call(
        pack_kernel,
        [((32, CELLS), F32)],
        scratch=[
            pltpu.VMEM((K, 1, CELLS), jnp.int32),
            pltpu.VMEM((3, 1, LON), jnp.int32),
        ]
        + [pltpu.VMEM(array.shape, BF) for array in lifts]
        + [pltpu.SemaphoreType.DMA((8,))],
        in_specs=[smem()] + [hbm()] * 8,
        limit=WHOLE_VMEM,
    )(ids, state[0, 0], cotangent[0, 0], neighbours.reshape(K, 1, CELLS), sea_cells, *lifts)
    gathered = lax.all_gather(packed, GROUP)
    features, strip = call(
        sector_kernel,
        [((24, WIN), F32), ((24, CELLS), F32)],
        in_specs=[smem(), vmem()],
    )(ids, gathered)
    strip = lax.ppermute(strip, BOTH, beside)

    weights = call(
        weights_kernel,
        [
            ((CH, 16), BF),
            ((16 + CH, CH), BF),
            ((16 + CH, CH), BF),
            ((CH, 16), BF),
            ((3, CH, K * CH), BF),
            ((2, 3 * CH, 7 * CH), BF),
            ((CH, 16), BF),
            ((16, CH), BF),
            ((16, CH), BF),
            ((CH, 16), BF),
            ((2, CH, K * CH), BF),
            ((2, K * CH, CH), BF),
        ],
    )(gathered, atm_conv, ocn_conv)
    lift, lift_back, head, head_back, flat, back = weights[:6]
    ocean_lift, ocean_lift_back, ocean_head, ocean_head_back, ocean_flat, ocean_back = weights[6:]

    hot, hot_back, hot_sea = call(hot_kernel, [((K, CELLS, CELLS), BF), ((K * CELLS, CELLS), BF), ((3, CELLS, LON), BF)])(gathered)
    strip, hot, hot_back, hot_sea = lax.optimization_barrier((strip, hot, hot_back, hot_sea))

    wide = (CH, WIN)
    history = [(16, WIN), wide, wide, wide, wide]
    inputs, source, gate_one, gate_two, last, window, final = call(
        forward_kernel,
        [((STEPS,) + shape, BF) for shape in history] + [((16, WIN), F32), ((16, WIN), F32)],
        scratch=[
            pltpu.VMEM((24, WIN), F32),
            pltpu.VMEM((16, WIN), F32),
            pltpu.VMEM((K * CH, WIN), BF),
            pltpu.VMEM((K * CH, WIN), BF),
            pltpu.VMEM((4, 16, WIN), BF),
            pltpu.VMEM((8, WIN), F32),
            pltpu.VMEM((CH, WIN), F32),
            pltpu.VMEM((CH, WIN), F32),
        ],
        in_specs=[smem()] + [vmem()] * 5,
    )(ids, features, strip, lift, flat, head)

    other_final = lax.ppermute(final, BOTH, partner)
    flux_grad, flux_strip, *ocean_parts = call(
        functools.partial(ocean_kernel, scale),
        [
            ((8, WIN), F32),
            ((8, CELLS), F32),
            ((2, K * CH, CELLS), BF),
            ((2, CH, CELLS), BF),
            ((2, 16, CELLS), BF),
            ((2, CH, CELLS), BF),
        ],
        scratch=[pltpu.VMEM((CH, K * CELLS), BF)],
        in_specs=[smem()] + [vmem()] * 11,
    )(
        ids, gathered, final, other_final, hot, hot_back, hot_sea, ocean_lift, ocean_flat,
        ocean_lift_back, ocean_back, ocean_head_back,
    )
    flux_strip = lax.ppermute(flux_strip, BOTH, beside)
    (sources,) = call(source_kernel, [((STEPS, 3 * CH, WIN), BF)])(source)
    next_state, ocean_wire = call(
        ocean_weight_kernel,
        [((8, CELLS), F32), ((160, LON), BF)],
        in_specs=[smem()] + [vmem()] * 8,
    )(ids, gathered, final, other_final, ocean_head, *ocean_parts)

    (wire,) = call(
        functools.partial(backward_kernel, scale),
        [((WIRE, LON), BF)],
        scratch=[
            pltpu.VMEM((16, WIN), F32),
            pltpu.VMEM((8, WIN), F32),
            pltpu.VMEM((7 * CH, 3 * CH), F32),
            pltpu.VMEM((16, LON), F32),
            pltpu.VMEM((2, 7 * CH, WIN), BF),
            pltpu.VMEM((2, 7 * CH, WIN), BF),
            pltpu.VMEM((CH, WIN), F32),
        ],
        in_specs=[smem()] + [vmem()] * 12,
    )(
        ids, window, flux_grad, flux_strip, ocean_wire, back, head_back, lift_back,
        inputs, sources, gate_one, gate_two, last,
    )

    parts = lax.all_to_all(wire.reshape(sectors, rows, LON), "tile", 0, 0, tiled=True)
    (sums,) = call(
        functools.partial(sum_kernel, sectors, 2 * sectors), [((2 * sectors, rows, LON), BF)]
    )(parts)
    sums = lax.all_to_all(sums, ("high", "tile"), 0, 0, tiled=True)
    other_sums = lax.ppermute(sums, "core", [(0, 1), (1, 0)])
    totals = call(
        functools.partial(final_kernel, sectors, rows),
        [
            ((10, CH), F32),
            ((2, K, CH, CH), F32),
            ((12, CH), F32),
            ((12, CH), F32),
            ((2, K, CH, CH), F32),
            ((8, CH), F32),
        ],
        in_specs=[smem(), vmem(), vmem()],
    )(ids, sums, other_sums)
    g_lift, g_conv, g_head, o_lift, o_conv, o_head = totals
    return (next_state[None, None], g_lift.T, g_conv, g_head, o_lift.T, o_conv, o_head)


def solution(mesh):
    high, sectors = mesh.devices.shape[0] // 2, mesh.devices.shape[1]
    split = Mesh(mesh.devices.reshape(high, 2, sectors), BOTH)
    block = P(GROUP, "tile", None, None)
    return jax.shard_map(
        shards,
        mesh=split,
        in_specs=(block, block, block, P(None, "tile", None), P(), P(), P(), P(), P(), P()),
        out_specs=(block, P(), P(), P(), P(), P(), P()),
        check_vma=False,
    )
```

```python
import functools
import math

import jax
import jax.numpy as jnp
from jax import lax
from jax.experimental import pallas as pl
from jax.experimental.pallas import tpu as pltpu
from jax.sharding import Mesh
from jax.sharding import PartitionSpec as P

STEPS = 8
LON = 128
ROWS = 9
CELLS = 384
WIN = ROWS * LON
K = 9
CH = 64
HALO = 32
WIRE = 512
GROUP = ("high", "core")
BOTH = ("high", "core", "tile")
BF = jnp.bfloat16
F32 = jnp.float32
INTERPRET = False
VMEM_LIMIT = 24 * 1024 * 1024
WHOLE_VMEM = 62 * 1024 * 1024
BACK = (
    ((0, 1), (1, 1), (2, 1), (5, 1), (6, 1), (7, 1), (8, 1)),
    ((3, 1), (5, 1), (7, 1), (5, -1), None, (7, -1), None),
    ((4, 1), (6, 1), (8, 1), None, (6, -1), None, (8, -1)),
)

NN = (((1,), (0,)), ((), ()))
NT = (((1,), (1,)), ((), ()))


def dot(a, b, dims=NN):
    return lax.dot_general(a, b, dims, preferred_element_type=F32)


def call(body, outs, scratch=(), in_specs=None, limit=VMEM_LIMIT):
    extra = {}
    if in_specs is not None:
        extra = {"in_specs": in_specs, "out_specs": [vmem()] * len(outs)}
    return pl.pallas_call(
        body,
        out_shape=[jax.ShapeDtypeStruct(shape, dtype) for shape, dtype in outs],
        scratch_shapes=list(scratch),
        interpret=INTERPRET,
        compiler_params=pltpu.CompilerParams(vmem_limit_bytes=limit),
        **extra,
    )


def smem():
    return pl.BlockSpec(memory_space=pltpu.SMEM)


def hbm():
    return pl.BlockSpec(memory_space=pltpu.HBM)


def vmem():
    return pl.BlockSpec(memory_space=pltpu.VMEM)


def lane_ids(shape):
    return lax.broadcasted_iota(jnp.int32, shape, len(shape) - 1)


def sigmoid(value):
    return 0.5 * jnp.tanh(0.5 * value) + 0.5


def seg(row):
    return slice(row * LON, (row + 1) * LON)


def pack_strip(read, half, shape):
    start = jnp.where(half == 0, 0, LON - HALO)
    quarter = lane_ids(shape) // HALO
    packed = []
    for block in range(3):
        total = jnp.zeros(shape, F32)
        for place in range(4):
            row = 4 * block + place
            if row < ROWS:
                moved = pltpu.roll(read(row), lax.rem(HALO * place - start + 2 * LON, LON), 1)
                total = jnp.where(quarter == place, moved, total)
        packed.append(total)
    return packed


def to_window(own, strip, row, half):
    place = row % 4
    lanes = lane_ids(own.shape)
    target = jnp.where(half == 0, LON - HALO, 0)
    moved = pltpu.roll(strip, lax.rem(target - HALO * place + 2 * LON, LON), 1)
    outside = (lanes >= target) & (lanes < target + HALO)
    merged = jnp.where(outside, moved, own)
    return pltpu.roll(merged, jnp.where(half == 0, HALO, LON - HALO), 1)


def pack_kernel(
    ids, state, cotangent, table, sea, atm_lift, atm_head, ocn_lift, ocn_head,
    out, held, held_sea, near_one, near_two, near_three, near_four, done,
):
    near = (near_one, near_two, near_three, near_four)
    pairs = [(state, out.at[0:8]), (cotangent, out.at[8:16]), (table, held), (sea, held_sea)]
    pairs += list(zip((atm_lift, atm_head, ocn_lift, ocn_head), near))
    copies = [pltpu.make_async_copy(a, b, done.at[i]) for i, (a, b) in enumerate(pairs)]
    for copy in copies:
        copy.start()
    for copy in copies:
        copy.wait()
    small = [to_sixteen(ref[...]) for ref in near]
    small = jnp.concatenate(small + [jnp.zeros((16, LON), F32)], axis=1)
    share = small[0:4]
    for place in range(1, 4):
        share = jnp.where(ids[0] == place, small[4 * place : 4 * place + 4], share)
    rows = [held[k].astype(F32) for k in range(K)]
    rows.append(jnp.concatenate([held_sea[cycle] for cycle in range(3)], axis=1).astype(F32))
    rows += [share, jnp.zeros((2, CELLS), F32)]
    out[16:32, :] = jnp.concatenate(rows, axis=0)


def turned(value):
    return jnp.transpose(value.astype(F32)).astype(BF)


def to_sixteen(value):
    zeros = jnp.zeros((16 - value.shape[0], value.shape[1]), F32)
    return jnp.concatenate([value.astype(F32), zeros], axis=0)


def weights_kernel(
    gathered, atm_conv, ocn_conv,
    lift, lift_back, head, head_back, flat, back,
    ocean_lift, ocean_lift_back, ocean_head, ocean_head_back, ocean_flat, ocean_back,
):
    small = jnp.concatenate([gathered[group, 26:30, :] for group in range(4)], axis=0)
    lift[...] = turned(small[:, 0:64])
    head_back[...] = turned(small[:, 64:128])
    row_ids = lax.broadcasted_iota(jnp.int32, (16, CH), 0)
    fields = jnp.where(row_ids < 8, small[:, 64:128], 0.0).astype(BF)
    mixed = dot(turned(small[:, 0:64]), fields)
    head[...] = jnp.concatenate([small[:, 64:128], mixed], axis=0).astype(BF)
    lift_back[...] = jnp.concatenate([small[:, 0:64], jnp.transpose(mixed)], axis=0).astype(BF)
    ocean_lift_back[...] = small[:, 128:192].astype(BF)
    ocean_lift[...] = turned(small[:, 128:192])
    ocean_head[...] = small[:, 192:256].astype(BF)
    ocean_head_back[...] = turned(small[:, 192:256])
    for index in range(2):
        blocks = [atm_conv[index, k] for k in range(K)]
        flat[index] = jnp.concatenate(blocks, axis=1)
        if index == 0:
            folded = [dot(block, mixed.astype(BF)) for block in blocks]
            flat[2] = jnp.concatenate(folded, axis=1).astype(BF)
        blocks = [turned(block) for block in blocks]
        for side, terms in enumerate(BACK):
            parts = [
                jnp.zeros((CH, CH), BF) if term is None else blocks[term[0]] * term[1]
                for term in terms
            ]
            back[index, side * CH : (side + 1) * CH, :] = jnp.concatenate(parts, axis=1)
        blocks = [ocn_conv[index, k] for k in range(K)]
        ocean_flat[index] = jnp.concatenate(blocks, axis=1)
        for k in range(K):
            ocean_back[index, k * CH : (k + 1) * CH, :] = turned(blocks[k])


def hot_kernel(gathered, hot, hot_back, hot_sea):
    for cycle in range(3):
        hot_sea[cycle] = one_hot_sea(sea_row(gathered, cycle))
    table = gathered[3, 16:32, :]
    columns = jnp.transpose(table).astype(jnp.int32)
    table = table.astype(jnp.int32)
    cell_rows = lax.broadcasted_iota(jnp.int32, (CELLS, CELLS), 0)
    cell_lanes = lane_ids((CELLS, CELLS))
    for k in range(K):
        place = slice(k * CELLS, (k + 1) * CELLS)
        hot[k] = jnp.where(cell_rows == table[k : k + 1], 1.0, 0.0).astype(BF)
        target = columns[:, k : k + 1]
        hot_back[place, :] = jnp.where(cell_lanes == target, 1.0, 0.0).astype(BF)


def one_hot_sea(row):
    cells = lax.broadcasted_iota(jnp.int32, (CELLS, LON), 0)
    return jnp.where(cells == row, 1.0, 0.0).astype(BF)


def sea_row(gathered, cycle):
    return gathered[3, 25:26, cycle * LON : (cycle + 1) * LON].astype(jnp.int32)


def sector_kernel(ids, gathered, features, strip):
    half = ids[0] % 2
    for cycle in range(3):
        cols = slice(cycle * CELLS, (cycle + 1) * CELLS)
        features[0:16, cols] = gathered[cycle, 0:16, :]
        warm = gathered[3, 0:8, cycle * LON : (cycle + 1) * LON]
        row_ids = lax.broadcasted_iota(jnp.int32, (8, LON), 0)
        sources = jnp.where(row_ids == 0, warm[0:1], jnp.where(row_ids == 1, 1.0, 0.0))
        sources = jnp.concatenate([sources, jnp.zeros((8, LON), F32)], axis=0).astype(BF)
        placed = dot(sources, one_hot_sea(sea_row(gathered, cycle)), NT)[0:8]
        features[16:24, cols] = placed
        table = gathered[cycle, 16:32, :]
        features[18:20, cols] = jnp.where(table[5:7] == table[1:2], 1.0, 0.0)
        features[20:22, cols] = jnp.where(table[7:9] == table[2:3], 1.0, 0.0)
    packed = pack_strip(lambda row: features[:, seg(row)], half, (24, LON))
    for block in range(3):
        strip[:, seg(block)] = packed[block]


def pick(mask, chosen, other):
    shape = (CH // 16, 16, LON)
    result = jnp.where(mask[None], chosen.reshape(shape), other.reshape(shape))
    return result.reshape(CH, LON)


def shifted(piece):
    mid = piece.astype(BF)
    return mid, pltpu.roll(mid, 1, 1), pltpu.roll(mid, LON - 1, 1)


def build_columns(out, rows, flags):
    for row in range(ROWS):
        mid, west, east = shifted(rows[row])
        places = [(0, row, mid), (3, row, west), (4, row, east)]
        for cell, straight, first in ((row + 1, 1, 5), (row - 1, 2, 7)):
            if 0 <= cell < ROWS:
                places.append((straight, cell, mid))
                for side, k in ((west, first), (east, first + 1)):
                    flag = flags[k - 5, :, seg(cell)] > 0.5
                    places.append((k, cell, pick(flag, mid, side)))
        for k, cell, value in places:
            out[k * CH : (k + 1) * CH, seg(cell)] = value


def build_back(out, at, rows, flags):
    mid = [piece.astype(BF) for piece in rows]
    zero = jnp.zeros((CH, LON), BF)
    for row in range(ROWS):
        blocks = {0: mid[row]}
        for source, straight, first in ((row + 1, 1, 0), (row - 1, 2, 2)):
            if 0 <= source < ROWS:
                blocks[straight] = mid[source]
                for j in (first, first + 1):
                    flag = flags[j : j + 1, seg(source)] > 0.5
                    blocks[3 + j] = jnp.where(flag, mid[source], zero)
        for j, value in blocks.items():
            out[at, j * CH : (j + 1) * CH, seg(row)] = value


def join_sides(value):
    rows = []
    for row in range(ROWS):
        here = value[0:CH, seg(row)]
        west = pltpu.roll(value[CH : 2 * CH, seg(row)], LON - 1, 1)
        east = pltpu.roll(value[2 * CH : 3 * CH, seg(row)], 1, 1)
        rows.append(here + west + east)
    return rows


def split_rows(value):
    return [value[:, seg(row)] for row in range(ROWS)]


def keep_owned(value):
    lanes = lane_ids(value.shape) % LON
    return jnp.where((lanes >= HALO) & (lanes < LON - HALO), value, jnp.zeros_like(value))


def forward_kernel(
    ids, features, strip, lift, flat, head,
    inputs_out, source_out, gate_one, gate_two, last_out, window_out, final_out,
    window, total, columns, columns_two, flags, surface, lifted_total, pre_total,
):
    half = ids[0] % 2
    first = ids[0] // 2 == 0

    for row in range(ROWS):
        block = row // 4
        window[:, seg(row)] = to_window(features[:, seg(row)], strip[:, seg(block)], row, half)
    total[0:8, :] = window[0:8, :]
    total[8:16, :] = jnp.zeros((8, WIN), F32)
    window_out[...] = window[8:24, :]
    for j in range(4):
        flags[j] = jnp.broadcast_to(window[18 + j : 19 + j, :], (16, WIN)).astype(BF)
    for held in (columns, columns_two):
        for row, blocks in ((0, (1, 5, 6)), (ROWS - 1, (2, 7, 8))):
            for k in blocks:
                held[k * CH : (k + 1) * CH, seg(row)] = jnp.zeros((CH, LON), BF)

    row_ids = lax.broadcasted_iota(jnp.int32, (8, WIN), 0)
    surface[...] = jnp.where(row_ids < 2, window[16:24, :], 0.0)
    inputs = jnp.concatenate([total[0:8, :], surface[...]], axis=0)
    lifted_total[...] = dot(lift[...], inputs.astype(BF))

    for at in range(STEPS):
        inputs = jnp.concatenate([total[0:8, :], surface[...]], axis=0)
        inputs_out[at] = keep_owned(inputs).astype(BF)
        lifted = lifted_total[...]
        if at == 0:
            build_columns(columns, split_rows(lifted), flags)
            pre = dot(flat[0], columns[...])
        else:
            build_columns(columns, split_rows(hidden), flags)
            pre = pre_total[...] + dot(flat[2], columns[...])
        if at < STEPS - 1:
            pre_total[...] = pre
        gate = sigmoid(pre)
        hidden = pre * gate
        gate_one[at] = (gate + hidden - hidden * gate).astype(BF)
        source_out[at] = jnp.where(first, lifted.astype(BF), hidden.astype(BF))
        build_columns(columns_two, [hidden[:, seg(row)] for row in range(ROWS)], flags)
        pre = dot(flat[1], columns_two[...])
        gate = sigmoid(pre)
        hidden = pre * gate
        gate_two[at] = (gate + hidden - hidden * gate).astype(BF)
        hidden = hidden.astype(BF)
        last_out[at] = hidden
        if at < STEPS - 1:
            change = dot(head[...], hidden)
            total[...] += change[0:16]
            lifted_total[...] += change[16:]
        else:
            total[...] += dot(head[0:16, :], hidden)

    for row in range(ROWS):
        shift = jnp.where(half == 0, LON - HALO, HALO)
        final_out[:, seg(row)] = pltpu.roll(total[:, seg(row)], shift, 1)


def join_halves(half, own, other):
    lanes = lane_ids(own.shape)
    return jnp.where(((lanes % LON) // (LON // 2)) == half, own, other)


def ocean_kernel(
    scale, ids, gathered, own, other, hot, hot_back, hot_sea,
    lift, flat, lift_back, flat_back, head_back,
    flux_grad, strip, columns, slopes, sixteen, wide,
    scatter,
):
    half = ids[0] % 2
    flux = join_halves(half, own[8:16, :], other[8:16, :])
    flux = (flux * (1.0 / STEPS)).astype(BF)
    flux = jnp.concatenate([flux, flux], axis=0)
    forcing = [
        dot(flux[:, cycle * CELLS : (cycle + 1) * CELLS], hot_sea[cycle])[0:8] for cycle in range(3)
    ]
    forcing = jnp.concatenate(forcing, axis=1)
    fields = gathered[3, 0:8, :]
    inputs = jnp.concatenate([fields, forcing], axis=0).astype(BF)

    def gather(at, value):
        for k in range(K):
            columns[at, k * CH : (k + 1) * CH, :] = dot(value, hot[k]).astype(BF)

    def spread(index, slope):
        parts = dot(flat_back[index], slope).astype(BF)
        for k in range(K):
            scatter[:, k * CELLS : (k + 1) * CELLS] = parts[k * CH : (k + 1) * CH]
        return dot(scatter[...], hot_back[...])

    lifted = dot(lift[...], inputs).astype(BF)
    gather(0, lifted)
    pre = dot(flat[0], columns[0])
    gate = sigmoid(pre)
    hidden = pre * gate
    slope_of_one = gate + hidden - hidden * gate
    gather(1, hidden.astype(BF))
    pre = dot(flat[1], columns[1])
    gate = sigmoid(pre)
    hidden = pre * gate
    slope_of_two = gate + hidden - hidden * gate
    hidden = hidden.astype(BF)

    head_grad = gathered[3, 8:16, :] * scale
    head_grad = jnp.concatenate([head_grad, jnp.zeros((8, CELLS), F32)], axis=0).astype(BF)
    slope_two = (dot(head_back[...], head_grad) * slope_of_two).astype(BF)
    slope_one = (spread(1, slope_two) * slope_of_one).astype(BF)
    grad_lifted = spread(0, slope_one).astype(BF)
    forcing_grad = dot(lift_back[...], grad_lifted)[8:16]
    forcing_grad = (forcing_grad * (1.0 / STEPS)).astype(BF)
    forcing_grad = jnp.concatenate([forcing_grad, forcing_grad], axis=0)
    for cycle in range(3):
        part = forcing_grad[:, cycle * LON : (cycle + 1) * LON]
        flux_grad[:, cycle * CELLS : (cycle + 1) * CELLS] = dot(part, hot_sea[cycle], NT)[0:8]
    packed = pack_strip(lambda row: flux_grad[:, seg(row)], half, (8, LON))
    for place in range(3):
        strip[:, seg(place)] = packed[place]
    slopes[0] = slope_one
    slopes[1] = slope_two
    sixteen[0] = inputs
    sixteen[1] = head_grad
    wide[0] = grad_lifted
    wide[1] = hidden


def source_kernel(source, sources):
    for at in range(STEPS):
        for row in range(ROWS):
            mid = source[at, :, seg(row)]
            sides = (pltpu.roll(mid, 1, 1), mid, pltpu.roll(mid, LON - 1, 1))
            for place, value in enumerate(sides):
                sources[at, place * CH : (place + 1) * CH, seg(row)] = keep_owned(value)


def ocean_weight_kernel(
    ids, gathered, own, other, head, columns, slopes, sixteen, wide, next_state, wire
):
    group = ids[0]
    half = group % 2
    chosen = group // 2
    block = gathered[3, 0:8, :] + dot(head[...], wide[1])[0:8]
    for cycle in range(3):
        cols = slice(cycle * CELLS, (cycle + 1) * CELLS)
        merged = join_halves(half, own[0:8, cols], other[0:8, cols])
        block = jnp.where(group == cycle, merged, block)
    next_state[...] = block
    weight = jnp.transpose(dot(columns[chosen], slopes[chosen], NT))
    weight = jnp.where(half == 0, weight[0:32], weight[32:64])
    for j in range(4):
        wire[32 * j : 32 * j + 32, :] = weight[:, seg(j)].astype(BF)
    rest = weight[:, 512:576]
    wire[128:144, :] = jnp.concatenate([rest[0:16], rest[16:32]], axis=1).astype(BF)
    small = [dot(sixteen[index], wide[index], NT) for index in range(2)]
    wire[144:160, :] = jnp.concatenate(small, axis=1).astype(BF)


def backward_kernel(
    scale, ids, window, flux_own, flux_strip, ocean_wire, back, head_back, lift_back,
    inputs, source, gate_one, gate_two, last,
    wire,
    head_grad, flags, weight_total, small_total, taps_even, taps_odd, grad_total,
):
    half = ids[0] % 2
    all_taps = (taps_even, taps_odd)
    chosen = 1 - jnp.where(ids[0] // 2 == 0, 1, 0)

    head_grad[0:8, :] = window[0:8, :] * scale
    for row in range(ROWS):
        place = row // 4
        head_grad[8:16, seg(row)] = to_window(
            flux_own[:, seg(row)], flux_strip[:, seg(place)], row, half
        )
    flags[0:4, :] = window[10:14, :]
    for taps in all_taps:
        for row, blocks in ((ROWS - 1, (1, 3, 4)), (0, (2, 5, 6))):
            for j in blocks:
                for at in range(2):
                    taps[at, j * CH : (j + 1) * CH, seg(row)] = jnp.zeros((CH, LON), BF)
    grad_total[...] = dot(head_back[...], head_grad[...].astype(BF))
    weight_total[...] = jnp.zeros_like(weight_total)
    small_total[...] = jnp.zeros_like(small_total)

    for at in reversed(range(STEPS)):
        taps = all_taps[at % 2]
        grad = head_grad[...].astype(BF)
        slope_two = grad_total[...] * gate_two[at].astype(F32)
        build_back(taps, 1, split_rows(slope_two), flags)
        grad_one = join_sides(dot(back[1], taps[1]))
        slope_one = [
            grad_one[row] * gate_one[at, :, seg(row)].astype(F32) for row in range(ROWS)
        ]
        build_back(taps, 0, slope_one, flags)
        grad_lifted = jnp.concatenate(join_sides(dot(back[0], taps[0])), axis=1).astype(BF)
        if at > 0:
            change = dot(lift_back[...], grad_lifted)
            grad_total[...] += change[16:]
            head_grad[0:8, :] += change[0:8]
        lift_weight = dot(inputs[at], grad_lifted, NT)
        head_weight = dot(keep_owned(grad), last[at], NT)
        small_total[...] += jnp.concatenate([lift_weight, head_weight], axis=1)
        weight_total[...] += dot(taps[chosen], source[at], NT)

    def product(slope, side):
        rows = weight_total[slope * CH : (slope + 1) * CH, :]
        return rows[:, side * CH : (side + 1) * CH]

    blocks = [product(0, 1), product(1, 1), product(2, 1), product(0, 0), product(0, 2)]
    for j in range(4):
        straight, side = 1 + j // 2, 2 * (j % 2)
        turned_part = product(straight, side) - product(3 + j, side)
        blocks.append(product(3 + j, 1) + turned_part)
    for j in range(4):
        pair = jnp.concatenate(blocks[2 * j : 2 * j + 2], axis=1)
        wire[64 * j : 64 * j + 64, :] = pair.astype(BF)
    pair = jnp.concatenate([blocks[8][0:32], blocks[8][32:64]], axis=1)
    wire[256:288, :] = pair.astype(BF)
    wire[288:304, :] = small_total[...].astype(BF)
    wire[304:464, :] = ocean_wire[...]
    wire[464:512, :] = jnp.zeros((48, LON), BF)


def sum_kernel(sectors, devices, parts, out):
    total = parts[0].astype(F32)
    for sector in range(1, sectors):
        total = total + parts[sector].astype(F32)
    total = total.astype(BF)
    for place in range(devices):
        out[place] = total


def final_kernel(sectors, rows, ids, own, other, g_lift, g_conv, g_head, o_lift, o_conv, o_head):
    def piece(group, start):
        place = (group // 2) * sectors + start // rows
        at = slice(start % rows, start % rows + 16)
        value = jnp.where(ids[0] % 2 == group % 2, own[place, at, :], other[place, at, :])
        return value.astype(F32)

    def spread(out, index, j, at, value):
        out[index, 2 * j, at : at + 16, :] = value[:, 0:64]
        out[index, 2 * j + 1, at : at + 16, :] = value[:, 64:128]

    for index in range(2):
        low, high = 2 * index, 2 * index + 1
        for j in range(4):
            for at in range(0, 64, 16):
                start = 64 * j + at
                spread(g_conv, index, j, at, piece(low, start) + piece(high, start))
            for at in range(0, 32, 16):
                start = 304 + 32 * j + at
                spread(o_conv, index, j, at, piece(low, start))
                spread(o_conv, index, j, at + 32, piece(high, start))
        for at in range(0, 32, 16):
            pair = piece(low, 256 + at) + piece(high, 256 + at)
            g_conv[index, 8, at : at + 16, :] = pair[:, 0:64]
            g_conv[index, 8, at + 32 : at + 48, :] = pair[:, 64:128]
        for side, at in ((low, 0), (high, 32)):
            value = piece(side, 432)
            o_conv[index, 8, at : at + 16, :] = value[:, 0:64]
            o_conv[index, 8, at + 16 : at + 32, :] = value[:, 64:128]
    small = piece(0, 288) + piece(1, 288)
    g_lift[...] = small[0:10, 0:64]
    g_head[...] = small[0:12, 64:128]
    small = piece(0, 448)
    o_lift[...] = small[0:12, 0:64]
    o_head[...] = small[0:8, 64:128]


def shards(
    state,
    cotangent,
    neighbours,
    sea_cells,
    atm_lift,
    atm_conv,
    atm_head,
    ocn_lift,
    ocn_conv,
    ocn_head,
):
    sectors = lax.axis_size("tile")
    devices = 4 * sectors
    rows = WIRE // sectors
    scale = 1.0 / math.sqrt(devices * CELLS)
    group = 2 * lax.axis_index("high") + lax.axis_index("core")
    ids = group.astype(jnp.int32).reshape(1)

    partner = []
    beside = []
    for g in range(4):
        for t in range(sectors):
            partner.append((g * sectors + t, (g ^ 1) * sectors + t))
            other = (t + 1) % sectors if g % 2 else (t - 1) % sectors
            beside.append((g * sectors + t, (g ^ 1) * sectors + other))

    lifts = (atm_lift.T, atm_head, ocn_lift.T, ocn_head)
    (packed,) = call(
        pack_kernel,
        [((32, CELLS), F32)],
        scratch=[
            pltpu.VMEM((K, 1, CELLS), jnp.int32),
            pltpu.VMEM((3, 1, LON), jnp.int32),
        ]
        + [pltpu.VMEM(array.shape, BF) for array in lifts]
        + [pltpu.SemaphoreType.DMA((8,))],
        in_specs=[smem()] + [hbm()] * 8,
        limit=WHOLE_VMEM,
    )(ids, state[0, 0], cotangent[0, 0], neighbours.reshape(K, 1, CELLS), sea_cells, *lifts)
    gathered = lax.all_gather(packed, GROUP)
    features, strip = call(
        sector_kernel,
        [((24, WIN), F32), ((24, CELLS), F32)],
        in_specs=[smem(), vmem()],
    )(ids, gathered)
    strip = lax.ppermute(strip, BOTH, beside)

    weights = call(
        weights_kernel,
        [
            ((CH, 16), BF),
            ((16 + CH, CH), BF),
            ((16 + CH, CH), BF),
            ((CH, 16), BF),
            ((3, CH, K * CH), BF),
            ((2, 3 * CH, 7 * CH), BF),
            ((CH, 16), BF),
            ((16, CH), BF),
            ((16, CH), BF),
            ((CH, 16), BF),
            ((2, CH, K * CH), BF),
            ((2, K * CH, CH), BF),
        ],
    )(gathered, atm_conv, ocn_conv)
    lift, lift_back, head, head_back, flat, back = weights[:6]
    ocean_lift, ocean_lift_back, ocean_head, ocean_head_back, ocean_flat, ocean_back = weights[6:]

    hot, hot_back, hot_sea = call(hot_kernel, [((K, CELLS, CELLS), BF), ((K * CELLS, CELLS), BF), ((3, CELLS, LON), BF)])(gathered)
    strip, hot, hot_back, hot_sea = lax.optimization_barrier((strip, hot, hot_back, hot_sea))

    wide = (CH, WIN)
    history = [(16, WIN), wide, wide, wide, wide]
    inputs, source, gate_one, gate_two, last, window, final = call(
        forward_kernel,
        [((STEPS,) + shape, BF) for shape in history] + [((16, WIN), F32), ((16, WIN), F32)],
        scratch=[
            pltpu.VMEM((24, WIN), F32),
            pltpu.VMEM((16, WIN), F32),
            pltpu.VMEM((K * CH, WIN), BF),
            pltpu.VMEM((K * CH, WIN), BF),
            pltpu.VMEM((4, 16, WIN), BF),
            pltpu.VMEM((8, WIN), F32),
            pltpu.VMEM((CH, WIN), F32),
            pltpu.VMEM((CH, WIN), F32),
        ],
        in_specs=[smem()] + [vmem()] * 5,
    )(ids, features, strip, lift, flat, head)

    other_final = lax.ppermute(final, BOTH, partner)
    flux_grad, flux_strip, *ocean_parts = call(
        functools.partial(ocean_kernel, scale),
        [
            ((8, WIN), F32),
            ((8, CELLS), F32),
            ((2, K * CH, CELLS), BF),
            ((2, CH, CELLS), BF),
            ((2, 16, CELLS), BF),
            ((2, CH, CELLS), BF),
        ],
        scratch=[pltpu.VMEM((CH, K * CELLS), BF)],
        in_specs=[smem()] + [vmem()] * 11,
    )(
        ids, gathered, final, other_final, hot, hot_back, hot_sea, ocean_lift, ocean_flat,
        ocean_lift_back, ocean_back, ocean_head_back,
    )
    flux_strip = lax.ppermute(flux_strip, BOTH, beside)
    (sources,) = call(source_kernel, [((STEPS, 3 * CH, WIN), BF)])(source)
    next_state, ocean_wire = call(
        ocean_weight_kernel,
        [((8, CELLS), F32), ((160, LON), BF)],
        in_specs=[smem()] + [vmem()] * 8,
    )(ids, gathered, final, other_final, ocean_head, *ocean_parts)

    (wire,) = call(
        functools.partial(backward_kernel, scale),
        [((WIRE, LON), BF)],
        scratch=[
            pltpu.VMEM((16, WIN), F32),
            pltpu.VMEM((8, WIN), F32),
            pltpu.VMEM((7 * CH, 3 * CH), F32),
            pltpu.VMEM((16, LON), F32),
            pltpu.VMEM((2, 7 * CH, WIN), BF),
            pltpu.VMEM((2, 7 * CH, WIN), BF),
            pltpu.VMEM((CH, WIN), F32),
        ],
        in_specs=[smem()] + [vmem()] * 12,
    )(
        ids, window, flux_grad, flux_strip, ocean_wire, back, head_back, lift_back,
        inputs, sources, gate_one, gate_two, last,
    )

    parts = lax.all_to_all(wire.reshape(sectors, rows, LON), "tile", 0, 0, tiled=True)
    (sums,) = call(
        functools.partial(sum_kernel, sectors, 2 * sectors), [((2 * sectors, rows, LON), BF)]
    )(parts)
    sums = lax.all_to_all(sums, ("high", "tile"), 0, 0, tiled=True)
    other_sums = lax.ppermute(sums, "core", [(0, 1), (1, 0)])
    totals = call(
        functools.partial(final_kernel, sectors, rows),
        [
            ((10, CH), F32),
            ((2, K, CH, CH), F32),
            ((12, CH), F32),
            ((12, CH), F32),
            ((2, K, CH, CH), F32),
            ((8, CH), F32),
        ],
        in_specs=[smem(), vmem(), vmem()],
    )(ids, sums, other_sums)
    g_lift, g_conv, g_head, o_lift, o_conv, o_head = totals
    return (next_state[None, None], g_lift.T, g_conv, g_head, o_lift.T, o_conv, o_head)


def solution(mesh):
    high, sectors = mesh.devices.shape[0] // 2, mesh.devices.shape[1]
    split = Mesh(mesh.devices.reshape(high, 2, sectors), BOTH)
    block = P(GROUP, "tile", None, None)
    return jax.shard_map(
        shards,
        mesh=split,
        in_specs=(block, block, block, P(None, "tile", None), P(), P(), P(), P(), P(), P()),
        out_specs=(block, P(), P(), P(), P(), P(), P()),
        check_vma=False,
    )
```
